32 devices in a mesh: seq: 4 (over y, x), shard: 8 (over z, core).
Axes of the slice: x: 2, y: 2, z: 4, core: 2. Of those that a mesh axis runs over, the one named last changes fastest.
Arguments:
- block_input: bfloat16 [16, 1024, 768], P('shard', 'seq'), may hold values from -6 to 6
- gain_attn: float32 [768], replicated, may hold values from 0.25 to 1.75
- gain_ffn: float32 [768], replicated, may hold values from 0.25 to 1.75
- w_qkv: bfloat16 [768, 2304], P('shard'), may hold values from -0.09375 to 0.09375
- w_out: bfloat16 [768, 768], P('shard'), may hold values from -4 to 4
- w_router: bfloat16 [768, 16], P('shard'), may hold values from -0.109375 to 0.109375
- rel_bias: float32 [32, 12], replicated, may hold values from -4 to 4
- w_in: bfloat16 [16, 768, 3072], P('shard'), may hold values from -0.21875 to 0.21875
- w_exp_out: bfloat16 [16, 3072, 768], P('shard'), may hold values from -6 to 6
- expert_id: int32 [16, 1024], P('shard', 'seq'), may hold values from 0 to 15, as said below
- capacity_slot: int32 [16, 1024], P('shard', 'seq'), may hold values from 0 to 64, as said below
- buckets: int32 [2047], replicated, may hold values from 0 to 31
- output_grad: bfloat16 [16, 1024, 768], P('shard', 'seq'), may hold values from -6 to 6
Outputs:
- block_output: bfloat16 [16, 1024, 768], P('shard', 'seq')
- input_grad: float32 [16, 1024, 768], P('shard', 'seq')
- grad_gain_attn: float32 [768], replicated
- grad_gain_ffn: float32 [768], replicated
- grad_w_qkv: float32 [768, 2304], P('shard')
- grad_w_out: float32 [768, 768], P('shard')
- grad_w_router: float32 [768, 16], P('shard')
- grad_rel_bias: float32 [32, 12], replicated
- grad_w_in: float32 [16, 768, 3072], P('shard', None, 'seq')
- grad_w_exp_out: float32 [16, 3072, 768], P('shard', 'seq')
The draws below stay inside these ranges and needn't reach their ends.
Inputs may be any that keep to these rules, and one draw needn't show every extreme that they name: `expert_id`: among the 512 tokens of one device (one shard index, one seq index), each expert is named by at most 64 kept tokens, with distinct slots. Slot 64 marks a dropped token; an expert with a dropped token has all 64 slots of that device taken. Some experts have all 64 slots taken on every device. `capacity_slot`: the slot of a token in its expert's buffer for its device's tokens; 64 means dropped.
All inputs are finite; a program needn't handle non-finite values.
Results may differ from the reference program's by a relative error of at most 0.019.
Values may be sent and summed in bfloat16 or wider, within the bound.
No kernel may reach another device: no remote copies, remote signals or barrier semaphores. Data moves between devices by JAX's collectives and lax.ppermute only.
A program may use at most 192 MiB of HBM per device.

```python
import jax
import jax.numpy as jnp
from jax import lax

D = 768
H = 12
HD = 64
FF = 3072
NB = 32
LEN = 1024
SEQS = 2
EXPERTS = 16
TOK_DEV = 512
SEQ_ALL = 16
CAP = 64
N_SEQ = 4
N_SHARD = 8


def routing_tables(key):
    seq_ways = LEN * SEQS // TOK_DEV
    shard_ways = SEQ_ALL // SEQS
    capacity = CAP
    positions = EXPERTS * capacity
    hot_count = EXPERTS // 8
    drop_count = TOK_DEV // 32
    kept_count = TOK_DEV - drop_count
    routing_key = jax.random.fold_in(key, 4099)
    expert_order = jax.random.permutation(jax.random.fold_in(routing_key, 1), EXPERTS).astype(jnp.int32)
    hot_ids = expert_order[:hot_count]
    hot_flag = jnp.zeros((EXPERTS,), jnp.int32).at[hot_ids].set(1)

    def one_device(device_key):
        rank_draw = jax.random.randint(jax.random.fold_in(device_key, 2), (positions,), 0, 4096, dtype=jnp.int32)
        position = jnp.arange(positions, dtype=jnp.int32)
        priority = (hot_flag[position // capacity] * 4096 + rank_draw) * positions + position
        top_scores, chosen = lax.top_k(priority, kept_count)
        chosen = chosen.astype(jnp.int32)
        hot_pick = jax.random.randint(jax.random.fold_in(device_key, 3), (drop_count,), 0, hot_count, dtype=jnp.int32)
        expert = jnp.concatenate([chosen // capacity, hot_ids[hot_pick]])
        slot_rows = jnp.concatenate([chosen % capacity, jnp.full((drop_count,), capacity, jnp.int32)])
        mixing = jax.random.permutation(jax.random.fold_in(device_key, 4), TOK_DEV)
        return (expert[mixing], slot_rows[mixing])
    device_keys = jax.random.split(jax.random.fold_in(routing_key, 5), seq_ways * shard_ways)
    expert, slot_rows = jax.vmap(one_device)(device_keys)
    tok_piece = TOK_DEV // SEQS
    expert = expert.reshape(shard_ways, seq_ways, SEQS, tok_piece).transpose(0, 2, 1, 3).reshape(SEQ_ALL, LEN)
    slot_rows = slot_rows.reshape(shard_ways, seq_ways, SEQS, tok_piece).transpose(0, 2, 1, 3).reshape(SEQ_ALL, LEN)
    return (expert.astype(jnp.int32), slot_rows.astype(jnp.int32))


def draw_expert_id(key, part):
    return routing_tables(key)[0]


def draw_capacity_slot(key, part):
    return routing_tables(key)[1]


def with_ends(values, key, smallest, top_value):
    shape = values.shape
    index_at = [jax.random.randint(jax.random.fold_in(key, axis), (), 0, shape[axis]) for axis in range(len(shape))]
    values = values.at[tuple(index_at)].set(smallest)
    longest = shape.index(max(shape))
    index_at[longest] = (index_at[longest] + 1) % shape[longest]
    return values.at[tuple(index_at)].set(top_value)


def level_of(own_key, dims, cuts, low, top_value):
    factor_of = 1.0
    for dim, blocks in cuts:
        steps = jax.random.uniform(jax.random.fold_in(jax.random.fold_in(own_key, 6), dim), (blocks,), jnp.float32, low / len(cuts), top_value / len(cuts))
        factor_of = factor_of * jnp.repeat(jnp.exp(steps), dims[dim] // blocks).reshape((-1,) + (1,) * (len(dims) - 1 - dim))
    return factor_of


def noise(rng, shape, deviation, limit, shards=(), kind=jnp.bfloat16):
    values = deviation * jax.random.normal(rng, shape, jnp.float32)
    if shards:
        values = values * level_of(rng, shape, shards, -0.22, 0.18)
    return jnp.clip(values, -limit, limit).astype(kind)


def setup_inputs(seed: int = 0) -> dict:
    arg_keys = jax.random.split(jax.random.key(seed), 14)
    return {
        "block_input": noise(arg_keys[0], (SEQ_ALL, LEN, D), 1.0, 6.0, ((0, 8), (1, 4))),
        "gain_attn": jnp.clip(1.0 + 0.15 * jax.random.normal(arg_keys[1], (D,), jnp.float32), 0.25, 1.75),
        "gain_ffn": jnp.clip(1.0 + 0.15 * jax.random.normal(arg_keys[2], (D,), jnp.float32), 0.25, 1.75),
        "w_qkv": noise(arg_keys[3], (D, 3 * D), (5 * D) ** -0.5, 0.09375, ((0, 8),)),
        "w_out": noise(arg_keys[4], (D, D), (max(1, D // 384)) ** -0.5, 4.0, ((0, 8),)),
        "w_router": noise(arg_keys[5], (D, EXPERTS), (4 * D) ** -0.5, 0.109375, ((0, 8),)),
        "rel_bias": noise(arg_keys[6], (NB, H), 1.0, 4.0, (), jnp.float32),
        "w_in": noise(arg_keys[7], (EXPERTS, D, FF), D ** -0.5, 0.21875, ((0, 8),)),
        "w_exp_out": noise(arg_keys[8], (EXPERTS, FF, D), (2.5 * EXPERTS * FF ** -0.5), 6.0, ((0, 8),)),
        "expert_id": draw_expert_id(jax.random.fold_in(arg_keys[13], 71), 0),
        "capacity_slot": draw_capacity_slot(jax.random.fold_in(arg_keys[13], 71), 0),
        "buckets": with_ends(jax.random.randint(arg_keys[11], (2 * LEN - 1,), 0, NB), jax.random.fold_in(arg_keys[11], 1), 0, NB - 1).astype(jnp.int32),
        "output_grad": noise(arg_keys[12], (SEQ_ALL, LEN, D), 1.0, 6.0, ((0, 8), (1, 4))),
    }


@jax.custom_vjp
def low(v):
    return lax.optimization_barrier(v.astype(jnp.bfloat16)).astype(jnp.float32)

@jax.custom_vjp
def low_back(v):
    return v

def low_keep(v):
    return (low(v), None)

def low_pass(kept, grad):
    return (grad,)

def back_keep(v):
    return (v, None)

def back_low(kept, grad):
    return (low(grad),)
low.defvjp(low_keep, low_pass)
low_back.defvjp(back_keep, back_low)
norm_eps = 1e-06
exact_matmul_mode = lax.Precision.HIGHEST

def rms_scale(values, gain_vec):
    inverse = lax.rsqrt(lax.optimization_barrier(jnp.mean(values * values, axis=-1, keepdims=True)) + norm_eps)
    return values * inverse * gain_vec

def attend_one(queries, keys_all, values_all, bias_all):
    scores = jnp.einsum('qhd,khd->hqk', queries, keys_all, precision=exact_matmul_mode) + bias_all
    scores = low_back(scores)
    row_peak = lax.optimization_barrier(jnp.max(scores, axis=-1, keepdims=True))
    exp_scores = jnp.exp(scores - row_peak)
    prob_rows = exp_scores / lax.optimization_barrier(jnp.sum(exp_scores, axis=-1, keepdims=True))
    return jnp.einsum('hqk,khd->qhd', low(prob_rows), values_all, precision=exact_matmul_mode)

def expert_ffn(rows_in, weight_in, weight_out):
    pre_act = low_back(jnp.dot(rows_in, weight_in, precision=exact_matmul_mode, preferred_element_type=jnp.float32))
    hidden = low(jax.nn.gelu(pre_act, approximate=False))
    result = jnp.dot(hidden, weight_out, precision=exact_matmul_mode, preferred_element_type=jnp.float32)
    return low_back(low(result))

def reference(block_input, gain_attn, gain_ffn, w_qkv, w_out, w_router, rel_bias, w_in, w_exp_out, expert_id, capacity_slot, buckets, output_grad):
    capacity = 2 * TOK_DEV // EXPERTS
    rows_all = N_SEQ * N_SHARD * capacity
    tok_piece = LEN // N_SEQ
    token_total = SEQ_ALL * LEN
    grid_shape = (N_SHARD, SEQS, N_SEQ, tok_piece)
    shard_index = lax.broadcasted_iota(jnp.int32, grid_shape, 0).reshape(SEQ_ALL, LEN)
    seq_index = lax.broadcasted_iota(jnp.int32, grid_shape, 2).reshape(SEQ_ALL, LEN)
    target = ((expert_id * N_SEQ + seq_index) * N_SHARD + shard_index) * capacity + capacity_slot
    target = jnp.where(capacity_slot < capacity, target, EXPERTS * rows_all).reshape(token_total).astype(jnp.int32)
    source = jnp.full((EXPERTS * rows_all,), token_total, jnp.int32)
    source = source.at[target].set(jnp.arange(token_total, dtype=jnp.int32), mode='drop')
    offsets = jnp.arange(LEN, dtype=jnp.int32)[None, :] - jnp.arange(LEN, dtype=jnp.int32)[:, None] + (LEN - 1)
    bucket_grid = buckets[offsets]
    chosen = (expert_id[..., None] == jnp.arange(EXPERTS, dtype=jnp.int32)).astype(jnp.float32)
    attend_saved = jax.checkpoint(attend_one)
    ffn_saved = jax.checkpoint(expert_ffn)

    def forward(inputs, gain_one, gain_two, query_key_value_weight, output_projection, routing_weight, bias_table, in_weight, exp_weight):
        normalized_input = low(rms_scale(inputs, gain_one))
        query_key_value_rows = jnp.einsum('imu,uw->imw', normalized_input, query_key_value_weight, precision=exact_matmul_mode)
        query_key_value_rows = low_back(low(query_key_value_rows)).reshape(SEQ_ALL, LEN, 3, H, HD)
        bias_full = jnp.transpose(bias_table[bucket_grid], (2, 0, 1))
        attention_result = lax.map(lambda members: attend_saved(members[0], members[1], members[2], bias_full), (query_key_value_rows[:, :, 0], query_key_value_rows[:, :, 1], query_key_value_rows[:, :, 2]))
        attention_result = low_back(low(attention_result)).reshape(SEQ_ALL, LEN, D)
        residual_branch = low_back(jnp.einsum('imu,uw->imw', attention_result, output_projection, precision=exact_matmul_mode))
        middle = inputs + residual_branch
        second_residual = low(rms_scale(middle, gain_two))
        router_logits = low_back(jnp.einsum('imu,uw->imw', second_residual, routing_weight, precision=exact_matmul_mode))
        row_peak = lax.optimization_barrier(jnp.max(router_logits, axis=-1, keepdims=True))
        exp_logits = jnp.exp(router_logits - row_peak)
        router_probs = exp_logits / lax.optimization_barrier(jnp.sum(exp_logits, axis=-1, keepdims=True))
        gate_prob = lax.optimization_barrier(jnp.sum(router_probs * chosen, axis=-1))
        expert_input = low_back(second_residual).reshape(token_total, D)
        padded = jnp.concatenate([expert_input, jnp.zeros((1, D), jnp.float32)], axis=0)
        buffer = padded[source].reshape(EXPERTS, rows_all, D)
        outputs = lax.map(lambda members: ffn_saved(members[0], members[1], members[2]), (buffer, in_weight, exp_weight))
        out_padded = jnp.concatenate([outputs.reshape(EXPERTS * rows_all, D), jnp.zeros((1, D), jnp.float32)], axis=0)
        returned = out_padded[target].reshape(SEQ_ALL, LEN, D)
        return middle + gate_prob[..., None] * returned
    primals = (block_input.astype(jnp.float32), gain_attn, gain_ffn, w_qkv.astype(jnp.float32), w_out.astype(jnp.float32), w_router.astype(jnp.float32), rel_bias, w_in.astype(jnp.float32), w_exp_out.astype(jnp.float32))
    result, pullback = jax.vjp(forward, *primals)
    gradients = pullback(output_grad.astype(jnp.float32))
    return (result.astype(jnp.bfloat16), gradients[0], gradients[1], gradients[2], gradients[3], gradients[4], gradients[5], gradients[6], gradients[7], gradients[8])
```

```python
import functools
import math

import jax
import jax.numpy as jnp
from jax import lax
from jax.experimental import pallas as pl
from jax.experimental.pallas import tpu as pltpu
from jax.sharding import PartitionSpec as P

f32 = jnp.float32
bf16 = jnp.bfloat16
LANES = 128
MIB = 1024 * 1024
FORWARD_TILE = 1024
norm_eps = 1e-06


def rms_forward(values, gain_vec):
    inverse = lax.rsqrt(jnp.mean(values * values, axis=-1, keepdims=True) + norm_eps)
    return (values * inverse * gain_vec, inverse)


def rms_backward(values, inverse, gain_vec, upstream):
    scaled = upstream * gain_vec
    gain_grad = jnp.sum(upstream * values * inverse, axis=(0, 1))
    inner_mean = jnp.mean(scaled * values, axis=-1, keepdims=True)
    return (inverse * scaled - values * inverse * inverse * inverse * inner_mean, gain_grad)


def nt(a, b):
    return lax.dot_general(a, b, (((1,), (1,)), ((), ())), preferred_element_type=f32)


def tn(a, b):
    return lax.dot_general(a, b, (((0,), (0,)), ((), ())), preferred_element_type=f32)


def attend_kernel(x_ref, w_ref, rel_ref, bucket_ref, qkv_ref, att_ref, prob_ref, toeplitz, *, block_rows):
    heads, length = prob_ref.shape[1], prob_ref.shape[2]
    width = att_ref.shape[-1]
    head_dim = width // heads
    span = 2 * length

    @pl.when(pl.program_id(0) == 0)
    def _():
        bucket_row = bucket_ref[...]
        for head in range(heads):
            row = jnp.zeros((1, span), f32)
            for bucket in range(rel_ref.shape[0]):
                row = jnp.where(bucket_row == bucket, rel_ref[bucket, head], row)
            toeplitz[head] = pltpu.roll(
                jnp.broadcast_to(row, (LANES, span)), span - LANES + 1, 1, stride=1, stride_axis=0
            )

    rows = x_ref[...].reshape(length, x_ref.shape[-1])
    qkv = jnp.dot(rows, w_ref[...], preferred_element_type=f32).astype(bf16)
    qkv_ref[...] = qkv.reshape(qkv_ref.shape)
    pieces = []
    for head in range(heads):
        at = head * head_dim
        q = qkv[:, at : at + head_dim]
        k = qkv[:, width + at : width + at + head_dim]
        v = qkv[:, 2 * width + at : 2 * width + at + head_dim]
        outs = []
        for block in range(length // block_rows):
            start = block * block_rows
            scores = nt(q[start : start + block_rows], k)
            parts = []
            for sub in range(block_rows // LANES):
                off = length - LANES - start - sub * LANES
                parts.append(scores[sub * LANES : (sub + 1) * LANES] + toeplitz[head, :, off : off + length])
            scores = jnp.concatenate(parts, axis=0) if len(parts) > 1 else parts[0]
            peak = jnp.max(scores, axis=-1, keepdims=True)
            expd = jnp.exp(scores - peak)
            total = jnp.sum(expd, axis=-1, keepdims=True)
            prob = (expd * (1.0 / total)).astype(bf16)
            prob_ref[0, head, start : start + block_rows, :] = prob
            outs.append(jnp.dot(prob, v, preferred_element_type=f32).astype(bf16))
        pieces.append(jnp.concatenate(outs, axis=0))
    att_ref[...] = jnp.concatenate(pieces, axis=1).reshape(att_ref.shape)


def attend(x, w, rel, buckets, heads, block_rows=256):
    pieces, seqs, piece, model = x.shape
    length = pieces * piece
    cols = w.shape[1]
    width = cols // 3
    bucket_row = jnp.pad(buckets, (0, 2 * length - buckets.shape[0])).reshape(1, 2 * length)
    return pl.pallas_call(
        functools.partial(attend_kernel, block_rows=block_rows),
        grid=(seqs,),
        in_specs=[
            pl.BlockSpec((pieces, 1, piece, model), lambda s: (0, s, 0, 0)),
            pl.BlockSpec(w.shape, lambda s: (0, 0)),
            pl.BlockSpec(memory_space=pltpu.SMEM),
            pl.BlockSpec(bucket_row.shape, lambda s: (0, 0)),
        ],
        out_specs=[
            pl.BlockSpec((pieces, 1, piece, cols), lambda s: (0, s, 0, 0)),
            pl.BlockSpec((pieces, 1, piece, width), lambda s: (0, s, 0, 0)),
            pl.BlockSpec((1, heads, length, length), lambda s: (s, 0, 0, 0)),
        ],
        out_shape=[
            jax.ShapeDtypeStruct((pieces, seqs, piece, cols), bf16),
            jax.ShapeDtypeStruct((pieces, seqs, piece, width), bf16),
            jax.ShapeDtypeStruct((seqs, heads, length, length), bf16),
        ],
        scratch_shapes=[pltpu.VMEM((heads, LANES, 2 * length), f32)],
        compiler_params=pltpu.CompilerParams(vmem_limit_bytes=52 * MIB),
        name="attend",
    )(x, w, rel, bucket_row)


def attend_back_kernel(qkv_ref, prob_ref, grad_ref, bucket_ref, out_ref, bias_ref, acc, ds_ref, *, block_rows):
    heads, length = prob_ref.shape[1], prob_ref.shape[2]
    width = grad_ref.shape[-1]
    head_dim = width // heads
    span = 2 * length
    step = pl.program_id(0)

    @pl.when(step == 0)
    def _():
        acc[...] = jnp.zeros_like(acc)

    qkv = qkv_ref[...].reshape(length, 3 * width)
    grad = grad_ref[...].reshape(length, width)
    dq, dk, dv = [], [], []
    for head in range(heads):
        at = head * head_dim
        q = qkv[:, at : at + head_dim]
        k = qkv[:, width + at : width + at + head_dim]
        v = qkv[:, 2 * width + at : 2 * width + at + head_dim]
        g = grad[:, at : at + head_dim]
        for block in range(length // block_rows):
            start = block * block_rows
            prob_grad = nt(g[start : start + block_rows], v)
            prob = prob_ref[0, head, start : start + block_rows, :].astype(f32)
            weighted = prob * prob_grad
            inner = jnp.sum(weighted, axis=-1, keepdims=True)
            score_grad = weighted - prob * inner
            ds_ref[start : start + block_rows, :] = score_grad.astype(bf16)
            for sub in range(block_rows // LANES):
                off = length - LANES - start - sub * LANES
                acc[head, :, off : off + length] += score_grad[sub * LANES : (sub + 1) * LANES]
        dq.append(jnp.dot(ds_ref[...], k, preferred_element_type=f32).astype(bf16))
        dk.append(tn(ds_ref[...], q).astype(bf16))
        dv.append(tn(prob_ref[0, head], g).astype(bf16))
    out_ref[...] = jnp.concatenate(dq + dk + dv, axis=1).reshape(out_ref.shape)

    @pl.when(step == pl.num_programs(0) - 1)
    def _():
        buckets = bias_ref.shape[0]
        hot = lax.broadcasted_iota(jnp.int32, (buckets, span), 0) == bucket_ref[...]
        sums = []
        for head in range(heads):
            part = acc[head]
            rows = LANES
            while rows > 8:
                rows //= 2
                part = part[:rows] + pltpu.roll(part[rows:], span - rows, 1)
            offsets = part[0:1]
            for row in range(1, 8):
                offsets = offsets + pltpu.roll(part[row : row + 1], span - row, 1)
            offsets = pltpu.roll(offsets, LANES - 1, 1)
            sums.append(offsets)
        lane = lax.broadcasted_iota(jnp.int32, bias_ref.shape, 1)
        result = jnp.zeros(bias_ref.shape, f32)
        for head in range(heads):
            total = jnp.sum(jnp.where(hot, sums[head], 0.0), axis=1, keepdims=True)
            result = jnp.where(lane == head, total, result)
        bias_ref[...] = result


def attend_back(qkv, prob, grad, buckets, bucket_count, block_rows=256):
    pieces, seqs, piece, cols = qkv.shape
    heads, length = prob.shape[1], prob.shape[2]
    width = cols // 3
    bucket_row = jnp.pad(buckets, (0, 2 * length - buckets.shape[0]), constant_values=-1).reshape(1, 2 * length)
    token_spec = lambda n: pl.BlockSpec((pieces, 1, piece, n), lambda s: (0, s, 0, 0))
    return pl.pallas_call(
        functools.partial(attend_back_kernel, block_rows=block_rows),
        grid=(seqs,),
        in_specs=[
            token_spec(cols),
            pl.BlockSpec((1, heads, length, length), lambda s: (s, 0, 0, 0)),
            token_spec(width),
            pl.BlockSpec(bucket_row.shape, lambda s: (0, 0)),
        ],
        out_specs=[token_spec(cols), pl.BlockSpec((bucket_count, LANES), lambda s: (0, 0))],
        out_shape=[
            jax.ShapeDtypeStruct(qkv.shape, bf16),
            jax.ShapeDtypeStruct((bucket_count, LANES), f32),
        ],
        scratch_shapes=[
            pltpu.VMEM((heads, LANES, 2 * length), f32),
            pltpu.VMEM((length, length), bf16),
        ],
        compiler_params=pltpu.CompilerParams(vmem_limit_bytes=52 * MIB),
        name="attend_back",
    )(qkv, prob, grad, bucket_row)


ROOT_HALF = 1.0 / math.sqrt(2.0)
DENSITY = 1.0 / math.sqrt(2.0 * math.pi)


def gelu_and_slope(v):
    cumulative = 0.5 * (1.0 + lax.erf(v * ROOT_HALF))
    return v * cumulative, cumulative + v * (jnp.exp(-0.5 * v * v) * DENSITY)


def expert_kernel(x_ref, win_ref, wout_ref, y_ref, slope_ref, acc):
    tile = pl.program_id(1)
    rows = acc.shape[0]
    x = x_ref[...].reshape(rows, x_ref.shape[-1])
    pre = jnp.dot(x, win_ref[0], preferred_element_type=f32)
    hidden, slope = gelu_and_slope(pre)
    slope_ref[0] = slope.astype(bf16)
    part = jnp.dot(hidden.astype(bf16), wout_ref[0], preferred_element_type=f32)

    @pl.when(tile == 0)
    def _():
        acc[...] = part

    @pl.when(tile > 0)
    def _():
        acc[...] += part

    @pl.when(tile == pl.num_programs(1) - 1)
    def _():
        y_ref[...] = acc[...].astype(bf16).reshape(y_ref.shape)


def expert_forward(x, w_in, w_out, tile):
    sources, experts, slots, model = x.shape
    hidden = w_in.shape[2]
    rows = sources * slots
    row_spec = pl.BlockSpec((sources, 1, slots, model), lambda e, f: (0, e, 0, 0))
    return pl.pallas_call(
        expert_kernel,
        grid=(experts, hidden // tile),
        in_specs=[
            row_spec,
            pl.BlockSpec((1, model, tile), lambda e, f: (e, 0, f)),
            pl.BlockSpec((1, tile, model), lambda e, f: (e, f, 0)),
        ],
        out_specs=[row_spec, pl.BlockSpec((1, rows, tile), lambda e, f: (e, 0, f))],
        out_shape=[
            jax.ShapeDtypeStruct(x.shape, bf16),
            jax.ShapeDtypeStruct((experts, rows, hidden), bf16),
        ],
        scratch_shapes=[pltpu.VMEM((rows, model), f32)],
        compiler_params=pltpu.CompilerParams(vmem_limit_bytes=52 * MIB),
        name="expert_forward",
    )(x, w_in, w_out)


def expert_back_kernel(g_ref, win_ref, wout_ref, slope_ref, y_ref, acc):
    tile = pl.program_id(1)
    rows = acc.shape[0]
    g = g_ref[...].reshape(rows, g_ref.shape[-1])
    pre_grad = (nt(g, wout_ref[0]) * slope_ref[0].astype(f32)).astype(bf16)
    part = nt(pre_grad, win_ref[0])

    @pl.when(tile == 0)
    def _():
        acc[...] = part

    @pl.when(tile > 0)
    def _():
        acc[...] += part

    @pl.when(tile == pl.num_programs(1) - 1)
    def _():
        y_ref[...] = acc[...].astype(bf16).reshape(y_ref.shape)


def expert_backward(g, w_in, w_out, slope, tile):
    sources, experts, slots, model = g.shape
    hidden = w_in.shape[2]
    rows = sources * slots
    row_spec = pl.BlockSpec((sources, 1, slots, model), lambda e, f: (0, e, 0, 0))
    return pl.pallas_call(
        expert_back_kernel,
        grid=(experts, hidden // tile),
        in_specs=[
            row_spec,
            pl.BlockSpec((1, model, tile), lambda e, f: (e, 0, f)),
            pl.BlockSpec((1, tile, model), lambda e, f: (e, f, 0)),
            pl.BlockSpec((1, rows, tile), lambda e, f: (e, 0, f)),
        ],
        out_specs=row_spec,
        out_shape=jax.ShapeDtypeStruct(g.shape, bf16),
        scratch_shapes=[pltpu.VMEM((rows, model), f32)],
        compiler_params=pltpu.CompilerParams(vmem_limit_bytes=52 * MIB),
        name="expert_backward",
    )(g, w_in, w_out, slope)


def weight_grad_kernel(x_ref, g_ref, win_ref, wout_ref, gin_ref, gout_ref):
    step = pl.program_id(1)
    rows = x_ref.shape[1] * x_ref.shape[3]
    x = x_ref[...].reshape(rows, x_ref.shape[-1])
    g = g_ref[...].reshape(rows, g_ref.shape[-1])
    pre = jnp.dot(x, win_ref[0], preferred_element_type=f32)
    hidden, slope = gelu_and_slope(pre)
    pre_grad = (nt(g, wout_ref[0]) * slope).astype(bf16)
    gin = tn(x, pre_grad)
    gout = tn(hidden.astype(bf16), g)

    @pl.when(step == 0)
    def _():
        gin_ref[0] = gin
        gout_ref[0] = gout

    @pl.when(step > 0)
    def _():
        gin_ref[0] += gin
        gout_ref[0] += gout


def weight_grads(x, g, w_in, w_out, quarter):
    pieces, sources, experts, slots, model = x.shape
    cols = w_in.shape[2] // pieces
    row_spec = pl.BlockSpec((1, sources, 1, slots, model), lambda e, p, q: (p, 0, e, 0, 0))
    grid_spec = pltpu.PrefetchScalarGridSpec(
        num_scalar_prefetch=1,
        grid=(experts, pieces),
        in_specs=[
            row_spec,
            row_spec,
            pl.BlockSpec((1, model, cols), lambda e, p, q: (e, 0, q[0])),
            pl.BlockSpec((1, cols, model), lambda e, p, q: (e, q[0], 0)),
        ],
        out_specs=[
            pl.BlockSpec((1, model, cols), lambda e, p, q: (e, 0, 0)),
            pl.BlockSpec((1, cols, model), lambda e, p, q: (e, 0, 0)),
        ],
    )

    def kern(q_ref, *refs):
        weight_grad_kernel(*refs)

    return pl.pallas_call(
        kern,
        grid_spec=grid_spec,
        out_shape=[
            jax.ShapeDtypeStruct((experts, model, cols), f32),
            jax.ShapeDtypeStruct((experts, cols, model), f32),
        ],
        compiler_params=pltpu.CompilerParams(vmem_limit_bytes=52 * MIB),
        name="weight_grads",
    )(quarter, x, g, w_in, w_out)


def body(
    block_input,
    gain_attn,
    gain_ffn,
    w_qkv,
    w_out,
    w_router,
    rel_bias,
    w_in,
    w_exp_out,
    expert_id,
    capacity_slot,
    buckets,
    output_grad,
):
    seqs, piece, model = block_input.shape
    seq_ways = lax.axis_size("seq")
    shard_ways = lax.axis_size("shard")
    bucket_count, heads_all = rel_bias.shape
    heads = heads_all // seq_ways
    width = model // seq_ways
    experts = w_router.shape[1]
    tokens = seqs * piece
    capacity = 2 * tokens // experts
    positions = experts * capacity
    slot_shape = (shard_ways, experts // shard_ways, capacity, model)
    weight_rows = w_qkv.shape[0]
    seq_index = lax.axis_index("seq")

    own_columns = lax.dynamic_slice_in_dim(
        w_qkv.reshape(weight_rows, 3, model), seq_index * width, width, 2
    ).reshape(weight_rows, 3 * width)
    head_weight = lax.all_gather(own_columns, "shard", axis=0, tiled=True)
    inputs = block_input.astype(f32)
    normalized_input, inverse_one = rms_forward(inputs, gain_attn)
    normed_low = normalized_input.astype(bf16)
    normed_all = lax.all_gather(normed_low, "seq")
    bias_dev = lax.dynamic_slice_in_dim(rel_bias, seq_index * heads, heads, 1)
    qkv_heads, attended, probs = attend(normed_all, head_weight, bias_dev, buckets, heads)
    attended_tok = lax.all_to_all(attended, "seq", 0, 0, tiled=True)
    dense = lax.all_gather(
        jnp.concatenate([w_out, w_router], axis=1), "shard", axis=0, tiled=True
    )
    output_projection = dense[:, :model].reshape(seq_ways, width, model)
    routing_weight = dense[:, model:]
    weight_groups = lax.all_gather(head_weight, "seq")

    residual_branch = jnp.einsum(
        "gstd,gde->ste", attended_tok, output_projection, preferred_element_type=f32
    )
    middle = inputs + residual_branch
    second_residual, inverse_two = rms_forward(middle, gain_ffn)
    second_low = second_residual.astype(bf16)
    router_logits = jnp.einsum("std,de->ste", second_low, routing_weight, preferred_element_type=f32)
    logit_peak = jnp.max(router_logits, axis=-1, keepdims=True)
    exp_logits = jnp.exp(router_logits - logit_peak)
    router_probs = exp_logits / jnp.sum(exp_logits, axis=-1, keepdims=True)
    chosen = (expert_id[..., None] == jnp.arange(experts, dtype=jnp.int32)).astype(f32)
    gate_prob = jnp.sum(router_probs * chosen, axis=-1)
    target = jnp.where(capacity_slot < capacity, expert_id * capacity + capacity_slot, -1).reshape(
        tokens
    )
    dispatch_hot = (jnp.arange(positions, dtype=jnp.int32)[:, None] == target[None, :]).astype(bf16)
    upstream = output_grad.astype(f32)
    out_grad = (gate_prob[..., None] * upstream).astype(bf16).reshape(tokens, model)

    def dispatch(rows):
        sent = jnp.dot(dispatch_hot, rows, preferred_element_type=f32).astype(bf16)
        return lax.all_to_all(sent.reshape(slot_shape), "shard", 0, 0, tiled=True)

    def combine(rows):
        back = lax.all_to_all(rows, "shard", 0, 0, tiled=True).reshape(positions, model)
        merged = jnp.einsum("pt,pd->td", dispatch_hot, back, preferred_element_type=f32)
        return merged.reshape(seqs, piece, model)

    arrived = dispatch(second_low.reshape(tokens, model))
    out_arrived = dispatch(out_grad)
    expert_out, slope = expert_forward(arrived, w_in, w_exp_out, FORWARD_TILE)
    token_out = combine(expert_out)
    rows_grad = expert_backward(out_arrived, w_in, w_exp_out, slope, FORWARD_TILE)
    second_grad = combine(rows_grad)
    arrived_all = lax.all_gather(arrived, "seq")
    out_all = lax.all_gather(out_arrived, "seq")
    grad_in_part, grad_exp_part = weight_grads(
        arrived_all, out_all, w_in, w_exp_out, seq_index.astype(jnp.int32).reshape(1)
    )

    block_output = (middle + gate_prob[..., None] * token_out).astype(bf16)
    gate_grad = jnp.sum(upstream * token_out, axis=-1)
    prob_pick = chosen * gate_grad[..., None]
    logit_grad = router_probs * (
        prob_pick - jnp.sum(router_probs * prob_pick, axis=-1, keepdims=True)
    )
    logit_low = logit_grad.astype(bf16)
    grad_router = jnp.einsum("std,ste->de", second_low, logit_low, preferred_element_type=f32)
    second_grad = second_grad + jnp.einsum(
        "ste,de->std", logit_low, routing_weight, preferred_element_type=f32
    )
    middle_norm_grad, grad_gain_two = rms_backward(middle, inverse_two, gain_ffn, second_grad)
    middle_grad = upstream + middle_norm_grad
    branch_low = middle_grad.astype(bf16)
    attended_grad = jnp.einsum(
        "ste,gde->gstd", branch_low, output_projection, preferred_element_type=f32
    ).astype(bf16)
    attended_grad_heads = lax.all_to_all(attended_grad, "seq", 0, 0, tiled=True)
    grad_out = jnp.einsum(
        "gstd,ste->gde", attended_tok, branch_low, preferred_element_type=f32
    ).reshape(model, model)
    grad_dense = jnp.concatenate([grad_out.astype(bf16), grad_router.astype(bf16)], axis=1)
    grad_dense = lax.psum_scatter(grad_dense, "shard", scatter_dimension=0, tiled=True)
    grad_dense = lax.psum(grad_dense, "seq").astype(f32)
    grad_gain_two = lax.psum(grad_gain_two, ("seq", "shard"))

    qkv_grad, bias_grad_dev = attend_back(
        qkv_heads, probs, attended_grad_heads, buckets, bucket_count
    )
    qkv_grad_tok = lax.all_to_all(qkv_grad, "seq", 0, 0, tiled=True)
    grad_columns = jnp.einsum(
        "pstd,pste->de", normed_all, qkv_grad, preferred_element_type=f32
    ).astype(bf16)
    grad_columns = lax.psum_scatter(grad_columns, "shard", scatter_dimension=0, tiled=True)
    grad_qkv = lax.all_gather(grad_columns, "seq")
    grad_qkv = (
        grad_qkv.reshape(seq_ways, weight_rows, 3, width)
        .transpose(1, 2, 0, 3)
        .reshape(weight_rows, 3 * model)
        .astype(f32)
    )
    normed_grad = jnp.einsum(
        "gste,gde->std", qkv_grad_tok, weight_groups, preferred_element_type=f32
    )
    input_norm_grad, grad_gain_one = rms_backward(inputs, inverse_one, gain_attn, normed_grad)
    input_grad = middle_grad + input_norm_grad
    bias_grad = lax.dynamic_update_slice_in_dim(
        jnp.zeros((bucket_count, heads_all), f32), bias_grad_dev[:, :heads], seq_index * heads, 1
    )
    bias_grad, grad_gain_one = lax.psum((bias_grad, grad_gain_one), ("seq", "shard"))
    return (
        block_output,
        input_grad,
        grad_gain_one,
        grad_gain_two,
        grad_qkv,
        grad_dense[:, :model],
        grad_dense[:, model:],
        bias_grad,
        grad_in_part,
        grad_exp_part,
    )


def solution(mesh):
    placed = (
        P("shard", "seq", None),
        P(),
        P(),
        P("shard", None),
        P("shard", None),
        P("shard", None),
        P(),
        P("shard", None, None),
        P("shard", None, None),
        P("shard", "seq"),
        P("shard", "seq"),
        P(),
        P("shard", "seq", None),
    )
    return jax.shard_map(
        body,
        mesh=mesh,
        in_specs=placed,
        out_specs=(
            P("shard", "seq", None),
            P("shard", "seq", None),
            P(),
            P(),
            P("shard", None),
            P("shard", None),
            P("shard", None),
            P(),
            P("shard", None, "seq"),
            P("shard", "seq", None),
        ),
        check_vma=False,
    )
```

```python
import functools
import math

import jax
import jax.numpy as jnp
from jax import lax
from jax.experimental import pallas as pl
from jax.experimental.pallas import tpu as pltpu
from jax.sharding import PartitionSpec as P

f32 = jnp.float32
bf16 = jnp.bfloat16
LANES = 128
MIB = 1024 * 1024
BLOCK_ROWS = 256
FORWARD_TILE = 1024
GRAD_TILE = 384
norm_eps = 1e-06
ROOT_HALF = 1.0 / math.sqrt(2.0)
DENSITY = 1.0 / math.sqrt(2.0 * math.pi)
PARAMS = pltpu.CompilerParams(vmem_limit_bytes=52 * MIB)
SMEM = pl.BlockSpec(memory_space=pltpu.SMEM)


def nn(a, b):
    return jnp.dot(a, b, preferred_element_type=f32)


def nt(a, b):
    return lax.dot_general(a, b, (((1,), (1,)), ((), ())), preferred_element_type=f32)


def tn(a, b):
    return lax.dot_general(a, b, (((0,), (0,)), ((), ())), preferred_element_type=f32)


def whole(array):
    zeros = (0,) * array.ndim
    return pl.BlockSpec(array.shape, lambda *_: zeros)


def cost(flops, *arrays):
    return pl.CostEstimate(
        flops=int(flops),
        bytes_accessed=int(sum(math.prod(a.shape) * a.dtype.itemsize for a in arrays)),
        transcendentals=0,
    )


def shape(dims, kind):
    return jax.ShapeDtypeStruct(dims, kind)


def pack_rows(values):
    half = values.shape[0] // 2
    return jnp.concatenate([values[:half], values[half:]], axis=1)


def unpack_rows(packed):
    width = packed.shape[1] // 2
    return jnp.concatenate([packed[:, :width], packed[:, width:]], axis=0)


def inverse_norm(values):
    return lax.rsqrt(jnp.mean(values * values, axis=-1, keepdims=True) + norm_eps)


def norm_backward(values, gain, upstream):
    inverse = inverse_norm(values)
    scaled = upstream * gain
    inner = jnp.mean(scaled * values, axis=-1, keepdims=True)
    result = inverse * scaled - values * (inverse * inverse * inverse * inner)
    return result, jnp.sum(upstream * values * inverse, axis=0, keepdims=True)


def gelu_and_slope(v):
    cumulative = 0.5 * (1.0 + lax.erf(v * ROOT_HALF))
    return v * cumulative, cumulative + v * (jnp.exp(-0.5 * v * v) * DENSITY)


def attend_kernel(
    place_ref, rel_ref, own_ref, near_ref, far_ref, low_ref, high_ref, w_ref, bucket_ref,
    rows_ref, qkv_ref, att_ref, prob_ref, split, outs, toeplitz,
):
    head = pl.program_id(0)
    heads, length, head_dim = outs.shape
    width = heads * head_dim
    span = 2 * length
    piece = own_ref.shape[0]

    @pl.when(head == 0)
    def _():
        for number, ref in enumerate((own_ref, near_ref, far_ref)):
            at = pl.multiple_of(place_ref[number] * piece, piece)
            rows_ref[pl.ds(at, piece), :] = ref[...]
        at = pl.multiple_of(place_ref[3] * piece, piece)
        half = piece // 2
        rows_ref[pl.ds(at, half), :] = low_ref[...]
        rows_ref[pl.ds(pl.multiple_of(at + half, half), half), :] = high_ref[...]
        qkv = nn(rows_ref[...], w_ref[...]).astype(bf16)
        qkv_ref[...] = qkv
        for part in range(3):
            for each in range(heads):
                at = part * width + each * head_dim
                split[part, each] = qkv[:, at : at + head_dim]

    bucket_row = bucket_ref[...]
    row = jnp.zeros((1, span), f32)
    for bucket in range(rel_ref.shape[0]):
        row = jnp.where(bucket_row == bucket, rel_ref[bucket, head], row)
    toeplitz[...] = pltpu.roll(
        jnp.broadcast_to(row, (LANES, span)), span - LANES + 1, 1, stride=1, stride_axis=0
    )
    keys = split[1, head]
    values = split[2, head]
    for start in range(0, length, BLOCK_ROWS):
        scores = nt(split[0, head, start : start + BLOCK_ROWS], keys)
        parts = []
        for sub in range(0, BLOCK_ROWS, LANES):
            off = length - LANES - start - sub
            parts.append(scores[sub : sub + LANES] + toeplitz[:, off : off + length])
        scores = jnp.concatenate(parts, axis=0)
        peak = jnp.max(scores, axis=-1, keepdims=True)
        grown = jnp.exp(scores - peak)
        total = jnp.sum(grown, axis=-1, keepdims=True)
        prob = (grown * (1.0 / total)).astype(bf16)
        prob_ref[0, start : start + BLOCK_ROWS, :] = prob
        outs[head, start : start + BLOCK_ROWS, :] = nn(prob, values)

    @pl.when(head == heads - 1)
    def _():
        joined = jnp.concatenate([outs[each].astype(bf16) for each in range(heads)], axis=1)
        for number in range(length // piece):
            att_ref[number] = pack_rows(joined[number * piece : (number + 1) * piece])


def attend(place, pieces, weight, rel, bucket_row, heads):
    own, near, far, low, high = pieces
    piece, model = own.shape
    length = bucket_row.shape[1] // 2
    cols = weight.shape[1]
    width = cols // 3
    head_dim = width // heads
    out_shape = [
        shape((length, model), bf16),
        shape((length, cols), bf16),
        shape((length // piece, piece // 2, 2 * width), bf16),
        shape((heads, length, length), bf16),
    ]
    return pl.pallas_call(
        attend_kernel,
        grid=(heads,),
        in_specs=[SMEM, SMEM]
        + [whole(a) for a in (own, near, far, low, high, weight, bucket_row)],
        out_specs=[whole(a) for a in out_shape[:3]]
        + [pl.BlockSpec((1, length, length), lambda h: (h, 0, 0))],
        out_shape=out_shape,
        scratch_shapes=[
            pltpu.VMEM((3, heads, length, head_dim), bf16),
            pltpu.VMEM((heads, length, head_dim), f32),
            pltpu.VMEM((LANES, 2 * length), f32),
        ],
        compiler_params=PARAMS,
        cost_estimate=cost(2 * length * model * cols + 16 * heads * length * length * head_dim, *out_shape),
        name="attend",
    )(place, rel, own, near, far, low, high, weight, bucket_row)


def attend_back_kernel(
    qkv_ref, prob_ref, grad_ref, bucket_ref, out_ref, bias_ref, split, outs, acc, score_grads
):
    head = pl.program_id(0)
    heads, length, head_dim = outs.shape[1:]
    width = heads * head_dim
    span = 2 * length
    pieces, half, _ = grad_ref.shape
    piece = 2 * half

    @pl.when(head == 0)
    def _():
        bias_ref[...] = jnp.zeros_like(bias_ref)
        for part in range(3):
            for each in range(heads):
                at = part * width + each * head_dim
                split[part, each] = qkv_ref[:, at : at + head_dim]
        for number in range(pieces):
            grad = unpack_rows(grad_ref[number])
            for each in range(heads):
                split[3, each, number * piece : (number + 1) * piece, :] = grad[
                    :, each * head_dim : (each + 1) * head_dim
                ]

    acc[...] = jnp.zeros_like(acc)
    values = split[2, head]
    for start in range(0, length, BLOCK_ROWS):
        prob_grad = nt(split[3, head, start : start + BLOCK_ROWS], values)
        prob = prob_ref[0, start : start + BLOCK_ROWS, :].astype(f32)
        weighted = prob * prob_grad
        inner = jnp.sum(weighted, axis=-1, keepdims=True)
        score_grad = weighted - prob * inner
        score_grads[start : start + BLOCK_ROWS, :] = score_grad.astype(bf16)
        for sub in range(0, BLOCK_ROWS, LANES):
            off = length - LANES - start - sub
            acc[:, off : off + length] += score_grad[sub : sub + LANES]
    outs[0, head] = nn(score_grads[...], split[1, head])
    outs[1, head] = tn(score_grads[...], split[0, head])
    outs[2, head] = tn(prob_ref[0], split[3, head])

    part = acc[...]
    rows = LANES
    while rows > 8:
        rows //= 2
        part = part[:rows] + pltpu.roll(part[rows:], span - rows, 1)
    offsets = part[0:1]
    for row in range(1, 8):
        offsets = offsets + pltpu.roll(part[row : row + 1], span - row, 1)
    offsets = pltpu.roll(offsets, LANES - 1, 1)
    hot = lax.broadcasted_iota(jnp.int32, (bias_ref.shape[0], span), 0) == bucket_ref[...]
    total = jnp.sum(jnp.where(hot, offsets, 0.0), axis=1, keepdims=True)
    lane = lax.broadcasted_iota(jnp.int32, bias_ref.shape, 1)
    bias_ref[...] = jnp.where(lane == head, total, bias_ref[...])

    @pl.when(head == heads - 1)
    def _():
        joined = jnp.concatenate(
            [outs[part, each].astype(bf16) for part in range(3) for each in range(heads)], axis=1
        )
        for number in range(pieces):
            out_ref[number] = pack_rows(joined[number * piece : (number + 1) * piece])


def attend_back(qkv, prob, grad, bucket_row, bucket_count):
    length, cols = qkv.shape
    heads = prob.shape[0]
    head_dim = cols // (3 * heads)
    pieces, half, _ = grad.shape
    out_shape = [shape((pieces, half, 2 * cols), bf16), shape((bucket_count, LANES), f32)]
    return pl.pallas_call(
        attend_back_kernel,
        grid=(heads,),
        in_specs=[
            whole(qkv),
            pl.BlockSpec((1, length, length), lambda h: (h, 0, 0)),
            whole(grad),
            whole(bucket_row),
        ],
        out_specs=[whole(a) for a in out_shape],
        out_shape=out_shape,
        scratch_shapes=[
            pltpu.VMEM((4, heads, length, head_dim), bf16),
            pltpu.VMEM((3, heads, length, head_dim), f32),
            pltpu.VMEM((LANES, 2 * length), f32),
            pltpu.VMEM((length, length), bf16),
        ],
        compiler_params=PARAMS,
        cost_estimate=cost(40 * heads * length * length * head_dim, qkv, prob, grad),
        name="attend_back",
    )(qkv, prob, grad, bucket_row)


def project_kernel(
    x_ref, dy_ref, id_ref, target_ref, gain_ref, dense_ref, *refs
):
    att_refs, (middle_ref, second_ref, flat_ref, prob_ref, sent_ref, grad_ref) = refs[:-6], refs[-6:]
    model = x_ref.shape[1]
    flats = []
    for ref in att_refs:
        flats.append(
            jnp.concatenate([unpack_rows(ref[g]) for g in range(ref.shape[0])], axis=1)
        )
    flat = jnp.concatenate(flats, axis=0)
    flat_ref[...] = flat
    middle = x_ref[...].astype(f32) + nn(flat, dense_ref[:, :model])
    middle_ref[...] = middle
    second = (middle * inverse_norm(middle) * gain_ref[...]).astype(bf16)
    second_ref[...] = second
    positions = sent_ref.shape[0]
    hot = (
        lax.broadcasted_iota(jnp.int32, (positions, x_ref.shape[0]), 0) == target_ref[...]
    ).astype(bf16)
    sent_ref[...] = nn(hot, second).astype(bf16)
    logits = nn(second, dense_ref[:, model:])
    peak = jnp.max(logits, axis=-1, keepdims=True)
    grown = jnp.exp(logits - peak)
    probs = grown / jnp.sum(grown, axis=-1, keepdims=True)
    prob_ref[...] = probs
    chosen = lax.broadcasted_iota(jnp.int32, probs.shape, 1) == id_ref[...]
    gate = jnp.sum(jnp.where(chosen, probs, 0.0), axis=-1, keepdims=True)
    out_grad = (gate * dy_ref[...].astype(f32)).astype(bf16)
    grad_ref[...] = nn(hot, out_grad).astype(bf16)


def project(x, dy, id_column, target_row, gain, dense, attended, positions):
    tokens, model = x.shape
    experts = dense.shape[1] - model
    out_shape = [
        shape((tokens, model), f32),
        shape((tokens, model), bf16),
        shape((tokens, model), bf16),
        shape((tokens, experts), f32),
        shape((positions, model), bf16),
        shape((positions, model), bf16),
    ]
    operands = (x, dy, id_column, target_row, gain, dense, *attended)
    return pl.pallas_call(
        project_kernel,
        in_specs=[whole(a) for a in operands],
        out_specs=[whole(a) for a in out_shape],
        out_shape=out_shape,
        compiler_params=PARAMS,
        cost_estimate=cost(2 * tokens * model * (model + 2 * positions), *out_shape),
        name="project",
    )(*operands)


def returned_kernel(
    back_ref, target_ref, id_ref, middle_ref, dy_ref, prob_ref, second_ref,
    out_ref, logit_ref, router_ref,
):
    tokens = middle_ref.shape[0]
    hot = (
        lax.broadcasted_iota(jnp.int32, (tokens, back_ref.shape[0]), 1) == target_ref[...]
    ).astype(bf16)
    token_out = nn(hot, back_ref[...])
    probs = prob_ref[...]
    chosen = lax.broadcasted_iota(jnp.int32, probs.shape, 1) == id_ref[...]
    gate = jnp.sum(jnp.where(chosen, probs, 0.0), axis=-1, keepdims=True)
    out_ref[...] = (middle_ref[...] + gate * token_out).astype(bf16)
    gate_grad = jnp.sum(dy_ref[...].astype(f32) * token_out, axis=-1, keepdims=True)
    picked = jnp.where(chosen, gate_grad, 0.0)
    logit_grad = probs * (picked - jnp.sum(probs * picked, axis=-1, keepdims=True))
    logit_low = logit_grad.astype(bf16)
    logit_ref[...] = logit_low
    router_ref[...] = tn(second_ref[...], logit_low).astype(bf16)


def returned(back, target_column, id_column, middle, dy, probs, second):
    tokens, model = middle.shape
    experts = probs.shape[1]
    out_shape = [
        shape((tokens, model), bf16),
        shape((tokens, experts), bf16),
        shape((model, experts), bf16),
    ]
    operands = (back, target_column, id_column, middle, dy, probs, second)
    return pl.pallas_call(
        returned_kernel,
        in_specs=[whole(a) for a in operands],
        out_specs=[whole(a) for a in out_shape],
        out_shape=out_shape,
        compiler_params=PARAMS,
        cost_estimate=cost(2 * tokens * model * back.shape[0], *out_shape, middle, back),
        name="returned",
    )(*operands)


def branch_kernel(
    back_ref, target_ref, logit_ref, dense_ref, middle_ref, gain_ref, dy_ref,
    middle_grad_ref, branch_ref, grad_ref, gain_grad_ref,
):
    tokens, model = middle_ref.shape
    hot = (
        lax.broadcasted_iota(jnp.int32, (tokens, back_ref.shape[0]), 1) == target_ref[...]
    ).astype(bf16)
    second_grad = nn(hot, back_ref[...]) + nt(logit_ref[...], dense_ref[:, model:])
    norm_grad, gain_grad = norm_backward(middle_ref[...], gain_ref[...], second_grad)
    gain_grad_ref[...] = gain_grad
    middle_grad = dy_ref[...].astype(f32) + norm_grad
    middle_grad_ref[...] = middle_grad
    branch = middle_grad.astype(bf16)
    branch_ref[...] = branch
    grad = nt(branch, dense_ref[:, :model]).astype(bf16)
    groups = grad_ref.shape[0]
    width = model // groups
    for group in range(groups):
        grad_ref[group] = pack_rows(grad[:, group * width : (group + 1) * width])


def branch_back(back, target_column, logit, dense, middle, gain, dy, number, seqs, groups):
    tokens, model = middle.shape
    piece = tokens // seqs

    def rows_of(array):
        return pl.BlockSpec((piece, array.shape[1]), lambda _: (number, 0))

    out_shape = [
        shape((piece, model), f32),
        shape((piece, model), bf16),
        shape((groups, piece // 2, 2 * model // groups), bf16),
        shape((1, model), f32),
    ]
    return pl.pallas_call(
        branch_kernel,
        grid=(1,),
        in_specs=[
            whole(back), rows_of(target_column), rows_of(logit), whole(dense), rows_of(middle),
            whole(gain), rows_of(dy),
        ],
        out_specs=[whole(a) for a in out_shape],
        out_shape=out_shape,
        compiler_params=PARAMS,
        cost_estimate=cost(2 * piece * model * (back.shape[0] + model), *out_shape, back, dense),
        name="branch_back",
    )(back, target_column, logit, dense, middle, gain, dy)


def input_kernel(grad_ref, weight_ref, x_ref, gain_ref, middle_grad_ref, *refs):
    out_ref, gain_grad_ref = refs[-2:]
    total = None
    for group in range(weight_ref.shape[0]):
        part = nt(unpack_rows(grad_ref[group]), weight_ref[group])
        total = part if total is None else total + part
    norm_grad, gain_grad = norm_backward(x_ref[0].astype(f32), gain_ref[...], total)
    out_ref[0] = middle_grad_ref[...] + norm_grad
    gain_grad_ref[...] = gain_grad


def input_back(grad, weights, x, gain, middle_grad, number, earlier):
    seqs, piece, model = x.shape
    row_spec = pl.BlockSpec((1, piece, model), lambda _: (number, 0, 0))
    out_shape = [shape(x.shape, f32), shape((1, model), f32)]
    operands = [grad, weights, x, gain, middle_grad]
    specs = [whole(grad), whole(weights), row_spec, whole(gain), whole(middle_grad)]
    aliases = {}
    if earlier is not None:
        aliases = {len(operands): 0}
        operands.append(earlier)
        specs.append(pl.BlockSpec(memory_space=pl.ANY))
    return pl.pallas_call(
        input_kernel,
        grid=(1,),
        in_specs=specs,
        out_specs=[row_spec, whole(out_shape[1])],
        out_shape=out_shape,
        input_output_aliases=aliases,
        compiler_params=PARAMS,
        cost_estimate=cost(2 * piece * math.prod(weights.shape), grad, weights, middle_grad),
        name="input_back",
    )(*operands)


def expert_kernel(x_ref, win_ref, wout_ref, y_ref, slope_ref, acc):
    tile = pl.program_id(1)
    rows = acc.shape[0]
    x = x_ref[...].reshape(rows, x_ref.shape[-1])
    pre = jnp.dot(x, win_ref[0], preferred_element_type=f32)
    hidden, slope = gelu_and_slope(pre)
    slope_ref[0] = slope.astype(bf16)
    part = jnp.dot(hidden.astype(bf16), wout_ref[0], preferred_element_type=f32)

    @pl.when(tile == 0)
    def _():
        acc[...] = part

    @pl.when(tile > 0)
    def _():
        acc[...] += part

    @pl.when(tile == pl.num_programs(1) - 1)
    def _():
        y_ref[...] = acc[...].astype(bf16).reshape(y_ref.shape)


def expert_forward(x, w_in, w_out, tile):
    sources, experts, slots, model = x.shape
    hidden = w_in.shape[2]
    rows = sources * slots
    row_spec = pl.BlockSpec((sources, 1, slots, model), lambda e, f: (0, e, 0, 0))
    return pl.pallas_call(
        expert_kernel,
        grid=(experts, hidden // tile),
        in_specs=[
            row_spec,
            pl.BlockSpec((1, model, tile), lambda e, f: (e, 0, f)),
            pl.BlockSpec((1, tile, model), lambda e, f: (e, f, 0)),
        ],
        out_specs=[row_spec, pl.BlockSpec((1, rows, tile), lambda e, f: (e, 0, f))],
        out_shape=[
            jax.ShapeDtypeStruct(x.shape, bf16),
            jax.ShapeDtypeStruct((experts, rows, hidden), bf16),
        ],
        scratch_shapes=[pltpu.VMEM((rows, model), f32)],
        compiler_params=pltpu.CompilerParams(vmem_limit_bytes=52 * MIB),
        name="expert_forward",
    )(x, w_in, w_out)


def expert_back_kernel(g_ref, win_ref, wout_ref, slope_ref, y_ref, acc):
    tile = pl.program_id(1)
    rows = acc.shape[0]
    g = g_ref[...].reshape(rows, g_ref.shape[-1])
    pre_grad = (nt(g, wout_ref[0]) * slope_ref[0].astype(f32)).astype(bf16)
    part = nt(pre_grad, win_ref[0])

    @pl.when(tile == 0)
    def _():
        acc[...] = part

    @pl.when(tile > 0)
    def _():
        acc[...] += part

    @pl.when(tile == pl.num_programs(1) - 1)
    def _():
        y_ref[...] = acc[...].astype(bf16).reshape(y_ref.shape)


def expert_backward(g, w_in, w_out, slope, tile):
    sources, experts, slots, model = g.shape
    hidden = w_in.shape[2]
    rows = sources * slots
    row_spec = pl.BlockSpec((sources, 1, slots, model), lambda e, f: (0, e, 0, 0))
    return pl.pallas_call(
        expert_back_kernel,
        grid=(experts, hidden // tile),
        in_specs=[
            row_spec,
            pl.BlockSpec((1, model, tile), lambda e, f: (e, 0, f)),
            pl.BlockSpec((1, tile, model), lambda e, f: (e, f, 0)),
            pl.BlockSpec((1, rows, tile), lambda e, f: (e, 0, f)),
        ],
        out_specs=row_spec,
        out_shape=jax.ShapeDtypeStruct(g.shape, bf16),
        scratch_shapes=[pltpu.VMEM((rows, model), f32)],
        compiler_params=pltpu.CompilerParams(vmem_limit_bytes=52 * MIB),
        name="expert_backward",
    )(g, w_in, w_out, slope)


def weight_grad_kernel(place_ref, *refs):
    pieces = (len(refs) - 4) // 2
    x_refs, g_refs = refs[:pieces], refs[pieces : 2 * pieces]
    win_ref, wout_ref = refs[2 * pieces : 2 * pieces + 2]
    gin_ref, gout_ref = refs[-2:]
    gin = gout = None
    for x_ref, g_ref in zip(x_refs, g_refs):
        rows = x_ref.shape[0] * x_ref.shape[2]
        x = x_ref[...].reshape(rows, x_ref.shape[-1])
        g = g_ref[...].reshape(rows, g_ref.shape[-1])
        hidden, slope = gelu_and_slope(nn(x, win_ref[0]))
        pre_grad = (nt(g, wout_ref[0]) * slope).astype(bf16)
        gin_part = tn(x, pre_grad)
        gout_part = tn(hidden.astype(bf16), g)
        gin = gin_part if gin is None else gin + gin_part
        gout = gout_part if gout is None else gout + gout_part
    gin_ref[0] = gin
    gout_ref[0] = gout


def weight_grads(place, xs, gs, w_in, w_out, ways):
    experts, model, hidden = w_in.shape
    cols = hidden // ways
    tile = GRAD_TILE if cols % GRAD_TILE == 0 else cols
    tiles = cols // tile

    def rows_of(array):
        sources, _, slots, _ = array.shape
        return pl.BlockSpec((sources, 1, slots, model), lambda e, t, q: (0, e, 0, 0))

    out_shape = [shape((experts, model, cols), f32), shape((experts, cols, model), f32)]
    flops = 8 * sum(math.prod(a.shape) for a in xs) * cols
    return pl.pallas_call(
        weight_grad_kernel,
        grid_spec=pltpu.PrefetchScalarGridSpec(
            num_scalar_prefetch=1,
            grid=(experts, tiles),
            in_specs=[rows_of(a) for a in (*xs, *gs)]
            + [
                pl.BlockSpec((1, model, tile), lambda e, t, q: (e, 0, q[0] * tiles + t)),
                pl.BlockSpec((1, tile, model), lambda e, t, q: (e, q[0] * tiles + t, 0)),
            ],
            out_specs=[
                pl.BlockSpec((1, model, tile), lambda e, t, q: (e, 0, t)),
                pl.BlockSpec((1, tile, model), lambda e, t, q: (e, t, 0)),
            ],
        ),
        out_shape=out_shape,
        compiler_params=PARAMS,
        cost_estimate=cost(2 * flops, *out_shape, *xs, *gs),
        name="weight_grads",
    )(place, *xs, *gs, w_in, w_out)


def partners(ways, step):
    return [(index, index ^ step) for index in range(ways)]


def swap(value, axis, step):
    return lax.ppermute(value, axis, partners(lax.axis_size(axis), step))


def gather_near(value):
    return swap(value, "seq", 1), swap(value, "seq", 2)


def gather_far(near, far):
    half = near.shape[0] // 2
    return swap(near[:half], "seq", 2), swap(far[half:], "seq", 1)


def sum_all(value):
    for axis in ("seq", "shard"):
        ways = lax.axis_size(axis)
        if ways <= 8:
            got = [swap(value, axis, step) for step in range(1, ways)]
            value = functools.reduce(jnp.add, [value] + got)
        else:
            value = lax.psum(value, axis)
    return value


def scatter_rows(value):
    ways = lax.axis_size("shard")
    rows, cols = value.shape
    parts = lax.all_to_all(value.reshape(ways, rows // ways, cols), "shard", 0, 0, tiled=True)
    return jnp.sum(parts.astype(f32), axis=0)


def body(
    block_input,
    gain_attn,
    gain_ffn,
    w_qkv,
    w_out,
    w_router,
    rel_bias,
    w_in,
    w_exp_out,
    expert_id,
    capacity_slot,
    buckets,
    output_grad,
):
    seqs, piece, model = block_input.shape
    seq_ways = lax.axis_size("seq")
    shard_ways = lax.axis_size("shard")
    bucket_count, heads_all = rel_bias.shape
    heads = heads_all // seq_ways
    width = model // seq_ways
    length = piece * seq_ways
    experts = w_router.shape[1]
    tokens = seqs * piece
    capacity = 2 * tokens // experts
    positions = experts * capacity
    slot_shape = (shard_ways, experts // shard_ways, capacity, model)
    weight_rows = w_qkv.shape[0]
    seq_index = lax.axis_index("seq").astype(jnp.int32)
    places = jnp.stack([seq_index ^ step for step in range(seq_ways)])
    gain_one_row = gain_attn.reshape(1, model)
    gain_two_row = gain_ffn.reshape(1, model)
    bucket_row = jnp.pad(
        buckets, (0, 2 * length - buckets.shape[0]), constant_values=-1
    ).reshape(1, 2 * length)
    target = jnp.where(capacity_slot < capacity, expert_id * capacity + capacity_slot, -1)
    target_row = target.reshape(1, tokens)
    target_column = target.reshape(tokens, 1)
    id_column = expert_id.reshape(tokens, 1)
    upstream = output_grad.reshape(tokens, model)

    own_columns = lax.dynamic_slice_in_dim(
        w_qkv.reshape(weight_rows, 3, model), seq_index * width, width, 2
    ).reshape(weight_rows, 3 * width)
    head_weight = lax.all_gather(own_columns, "shard", axis=0, tiled=True)
    dense = lax.all_gather(
        jnp.concatenate([w_out, w_router], axis=1), "shard", axis=0, tiled=True
    )
    inputs = block_input.astype(f32)
    normed = (inputs * inverse_norm(inputs) * gain_attn).astype(bf16)
    bias_dev = lax.dynamic_slice_in_dim(rel_bias, seq_index * heads, heads, 1)

    first_near = gather_near(normed[0])
    held = lax.optimization_barrier((normed[1], first_near))
    first_near = held[1]
    second_near = gather_near(held[0])
    first_far = gather_far(*first_near)
    second_far = gather_far(*second_near)
    sequence_pieces = (
        (normed[0], *first_near, *first_far),
        (normed[1], *second_near, *second_far),
    )
    kept, attended_tok = [], []
    for pieces in sequence_pieces:
        rows, qkv, attended, probs = attend(
            places, pieces, head_weight, bias_dev, bucket_row, heads
        )
        kept.append((rows, qkv, probs))
        attended_tok.append(lax.all_to_all(attended, "seq", 0, 0, tiled=True))

    middle, second, attended_flat, router_probs, sent, sent_grad = project(
        block_input.reshape(tokens, model),
        upstream,
        id_column,
        target_row,
        gain_two_row,
        dense,
        attended_tok,
        positions,
    )

    def exchange(rows):
        return lax.all_to_all(rows, "shard", 0, 0, tiled=True)

    held_weight, sent = lax.optimization_barrier((head_weight, sent))
    weight_groups = lax.all_gather(held_weight, "seq")
    arrived = exchange(sent.reshape(slot_shape))
    out_arrived = exchange(sent_grad.reshape(slot_shape))
    expert_out, slope = expert_forward(arrived, w_in, w_exp_out, FORWARD_TILE)
    back_out = exchange(expert_out).reshape(positions, model)
    rows_grad = expert_backward(out_arrived, w_in, w_exp_out, slope, FORWARD_TILE)
    back_grad = exchange(rows_grad).reshape(positions, model)
    arrived_near = gather_near(arrived)
    arrived_far = gather_far(*arrived_near)
    out_near = gather_near(out_arrived)
    out_far = gather_far(*out_near)

    block_output, logit_low, grad_router = returned(
        back_out, target_column, id_column, middle, upstream, router_probs, second
    )
    back_grad, arrived_near, arrived_far, weight_groups = lax.optimization_barrier(
        (back_grad, arrived_near, arrived_far, weight_groups)
    )
    middle_grads, branches, grad_heads, gain_two = [], [], [], []
    for number in range(seqs):
        middle_grad, branch, attended_grad, gain_part = branch_back(
            back_grad, target_column, logit_low, dense, middle, gain_two_row, upstream,
            number, seqs, seq_ways,
        )
        middle_grads.append(middle_grad)
        branches.append(branch)
        gain_two.append(gain_part)
        grad_heads.append(lax.all_to_all(attended_grad, "seq", 0, 0, tiled=True))
    grad_out = sum(
        tn(attended_flat[number * piece : (number + 1) * piece], branches[number])
        for number in range(seqs)
    )
    grad_dense = jnp.concatenate([grad_out.astype(bf16), grad_router], axis=1)
    grad_dense = scatter_rows(grad_dense)
    for step in (1, 2):
        grad_dense = grad_dense + swap(grad_dense, "seq", step)

    qkv_grads, bias_parts, grad_tok = [], [], []
    for number in range(seqs):
        _, qkv, probs = kept[number]
        grad = grad_heads[number]
        if number == seqs - 1:
            grad, out_near, out_far = lax.optimization_barrier((grad, out_near, out_far))
        qkv_grad, bias_part = attend_back(qkv, probs, grad, bucket_row, bucket_count)
        qkv_grads.append(qkv_grad)
        bias_parts.append(bias_part)
        grad_tok.append(lax.all_to_all(qkv_grad, "seq", 0, 0, tiled=True))
    out_arrived, _ = lax.optimization_barrier((out_arrived, qkv_grads[-1]))
    grad_in_part, grad_exp_part = weight_grads(
        places,
        (arrived, *arrived_near, *arrived_far),
        (out_arrived, *out_near, *out_far),
        w_in,
        w_exp_out,
        seq_ways,
    )
    columns = None
    for number in range(seqs):
        packed = qkv_grads[number]
        cols = packed.shape[2] // 2
        rows = kept[number][0].reshape(seq_ways, 2, piece // 2, model)
        flat = packed.reshape(seq_ways, piece // 2, 2, cols)
        part = jnp.einsum("phrd,prhe->de", rows, flat, preferred_element_type=f32)
        columns = part if columns is None else columns + part
    columns = scatter_rows(columns.astype(bf16)).astype(bf16)
    grad_qkv = lax.all_gather(columns, "seq")
    grad_qkv = (
        grad_qkv.reshape(seq_ways, weight_rows, 3, width)
        .transpose(1, 2, 0, 3)
        .reshape(weight_rows, 3 * model)
        .astype(f32)
    )
    input_grad, gain_one = None, []
    for number in range(seqs):
        input_grad, gain_part = input_back(
            grad_tok[number], weight_groups, block_input, gain_one_row, middle_grads[number],
            number, input_grad,
        )
        gain_one.append(gain_part)
    bias_grad = lax.dynamic_update_slice_in_dim(
        jnp.zeros((bucket_count, heads_all), f32),
        functools.reduce(jnp.add, bias_parts)[:, :heads],
        seq_index * heads,
        1,
    )
    early = jnp.concatenate([bias_grad.reshape(-1), sum(gain_two).reshape(-1)])
    early = sum_all(early.reshape(-1, LANES)).reshape(-1)
    gain_one = sum_all(sum(gain_one).reshape(-1, LANES)).reshape(-1)
    return (
        block_output.reshape(block_input.shape),
        input_grad,
        gain_one,
        early[bucket_count * heads_all :],
        grad_qkv,
        grad_dense[:, :model],
        grad_dense[:, model:],
        early[: bucket_count * heads_all].reshape(bucket_count, heads_all),
        grad_in_part,
        grad_exp_part,
    )


def solution(mesh):
    placed = (
        P("shard", "seq", None),
        P(),
        P(),
        P("shard", None),
        P("shard", None),
        P("shard", None),
        P(),
        P("shard", None, None),
        P("shard", None, None),
        P("shard", "seq"),
        P("shard", "seq"),
        P(),
        P("shard", "seq", None),
    )
    return jax.shard_map(
        body,
        mesh=mesh,
        in_specs=placed,
        out_specs=(
            P("shard", "seq", None),
            P("shard", "seq", None),
            P(),
            P(),
            P("shard", None),
            P("shard", None),
            P("shard", None),
            P(),
            P("shard", None, "seq"),
            P("shard", "seq", None),
        ),
        check_vma=False,
    )
```

```python
import functools
import math

import jax
import jax.numpy as jnp
from jax import lax
from jax.experimental import pallas as pl
from jax.experimental.pallas import tpu as pltpu
from jax.sharding import PartitionSpec as P

f32 = jnp.float32
bf16 = jnp.bfloat16
LANES = 128
MIB = 1024 * 1024
BLOCK_ROWS = 256
FORWARD_TILE = 1024
GRAD_TILE = 384
norm_eps = 1e-06
ROOT_HALF = 1.0 / math.sqrt(2.0)
DENSITY = 1.0 / math.sqrt(2.0 * math.pi)
PARAMS = pltpu.CompilerParams(vmem_limit_bytes=52 * MIB)
SMEM = pl.BlockSpec(memory_space=pltpu.SMEM)


def nn(a, b):
    return jnp.dot(a, b, preferred_element_type=f32)


def nt(a, b):
    return lax.dot_general(a, b, (((1,), (1,)), ((), ())), preferred_element_type=f32)


def tn(a, b):
    return lax.dot_general(a, b, (((0,), (0,)), ((), ())), preferred_element_type=f32)


def whole(array):
    zeros = (0,) * array.ndim
    return pl.BlockSpec(array.shape, lambda *_: zeros)


def cost(flops, *arrays):
    return pl.CostEstimate(
        flops=int(flops),
        bytes_accessed=int(sum(math.prod(a.shape) * a.dtype.itemsize for a in arrays)),
        transcendentals=0,
    )


def shape(dims, kind):
    return jax.ShapeDtypeStruct(dims, kind)


def pack_rows(values):
    half = values.shape[0] // 2
    return jnp.concatenate([values[:half], values[half:]], axis=1)


def unpack_rows(packed):
    width = packed.shape[1] // 2
    return jnp.concatenate([packed[:, :width], packed[:, width:]], axis=0)


def inverse_norm(values):
    return lax.rsqrt(jnp.mean(values * values, axis=-1, keepdims=True) + norm_eps)


def norm_backward(values, gain, upstream):
    inverse = inverse_norm(values)
    scaled = upstream * gain
    inner = jnp.mean(scaled * values, axis=-1, keepdims=True)
    result = inverse * scaled - values * (inverse * inverse * inverse * inner)
    return result, jnp.sum(upstream * values * inverse, axis=0, keepdims=True)


def gelu_and_slope(v):
    cumulative = 0.5 * (1.0 + lax.erf(v * ROOT_HALF))
    return v * cumulative, cumulative + v * (jnp.exp(-0.5 * v * v) * DENSITY)


def bias_kernel(rel_ref, bucket_ref, out_ref):
    span = bucket_ref.shape[1]
    bucket_row = bucket_ref[...]
    for head in range(out_ref.shape[0]):
        row = jnp.zeros((1, span), f32)
        for bucket in range(rel_ref.shape[0]):
            row = jnp.where(bucket_row == bucket, rel_ref[bucket, head], row)
        out_ref[head] = pltpu.roll(
            jnp.broadcast_to(row, (LANES, span)), span - LANES + 1, 1, stride=1, stride_axis=0
        )


def bias_tiles(rel, bucket_row):
    out_shape = shape((rel.shape[1], LANES, bucket_row.shape[1]), f32)
    return pl.pallas_call(
        bias_kernel,
        in_specs=[SMEM, whole(bucket_row)],
        out_specs=whole(out_shape),
        out_shape=out_shape,
        compiler_params=PARAMS,
        cost_estimate=cost(0, out_shape),
        name="bias_tiles",
    )(rel, bucket_row)


def attend_kernel(
    place_ref, own_ref, near_ref, far_ref, low_ref, high_ref, w_ref, toeplitz_ref,
    rows_ref, qkv_ref, att_ref, prob_ref, split, outs,
):
    head = pl.program_id(0)
    heads, length, head_dim = outs.shape
    width = heads * head_dim
    piece = own_ref.shape[0]

    @pl.when(head == 0)
    def _():
        for number, ref in enumerate((own_ref, near_ref, far_ref)):
            at = pl.multiple_of(place_ref[number] * piece, piece)
            rows_ref[pl.ds(at, piece), :] = ref[...]
        at = pl.multiple_of(place_ref[3] * piece, piece)
        half = piece // 2
        rows_ref[pl.ds(at, half), :] = low_ref[...]
        rows_ref[pl.ds(pl.multiple_of(at + half, half), half), :] = high_ref[...]
        qkv = nn(rows_ref[...], w_ref[:, : 3 * width]).astype(bf16)
        qkv_ref[...] = qkv
        for part in range(3):
            for each in range(heads):
                at = part * width + each * head_dim
                split[part, each] = qkv[:, at : at + head_dim]

    keys = split[1, head]
    values = split[2, head]
    for start in range(0, length, BLOCK_ROWS):
        scores = nt(split[0, head, start : start + BLOCK_ROWS], keys)
        parts = []
        for sub in range(0, BLOCK_ROWS, LANES):
            off = length - LANES - start - sub
            parts.append(scores[sub : sub + LANES] + toeplitz_ref[0, :, off : off + length])
        scores = jnp.concatenate(parts, axis=0)
        peak = jnp.max(scores, axis=-1, keepdims=True)
        grown = jnp.exp(scores - peak)
        total = jnp.sum(grown, axis=-1, keepdims=True)
        prob = (grown * (1.0 / total)).astype(bf16)
        prob_ref[0, start : start + BLOCK_ROWS, :] = prob
        outs[head, start : start + BLOCK_ROWS, :] = nn(prob, values)

    @pl.when(head == heads - 1)
    def _():
        joined = jnp.concatenate([outs[each].astype(bf16) for each in range(heads)], axis=1)
        for number in range(length // piece):
            att_ref[number] = pack_rows(joined[number * piece : (number + 1) * piece])


def attend(place, pieces, weight, tiles):
    own, near, far, low, high = pieces
    piece, model = own.shape
    heads, _, span = tiles.shape
    length = span // 2
    cols = 3 * (model // (length // piece))
    width = cols // 3
    head_dim = width // heads
    out_shape = [
        shape((length, model), bf16),
        shape((length, cols), bf16),
        shape((length // piece, piece // 2, 2 * width), bf16),
        shape((heads, length, length), bf16),
    ]
    return pl.pallas_call(
        attend_kernel,
        grid=(heads,),
        in_specs=[SMEM]
        + [whole(a) for a in (own, near, far, low, high, weight)]
        + [pl.BlockSpec((1, LANES, span), lambda h: (h, 0, 0))],
        out_specs=[whole(a) for a in out_shape[:3]]
        + [pl.BlockSpec((1, length, length), lambda h: (h, 0, 0))],
        out_shape=out_shape,
        scratch_shapes=[
            pltpu.VMEM((3, heads, length, head_dim), bf16),
            pltpu.VMEM((heads, length, head_dim), f32),
        ],
        compiler_params=PARAMS,
        cost_estimate=cost(2 * length * model * cols + 16 * heads * length * length * head_dim, *out_shape),
        name="attend",
    )(place, own, near, far, low, high, weight, tiles)


def attend_back_kernel(
    qkv_ref, prob_ref, grad_ref, bucket_ref, out_ref, bias_ref, split, outs, acc, score_grads
):
    head = pl.program_id(0)
    heads, length, head_dim = outs.shape[1:]
    width = heads * head_dim
    span = 2 * length
    pieces, half, _ = grad_ref.shape
    piece = 2 * half

    @pl.when(head == 0)
    def _():
        bias_ref[...] = jnp.zeros_like(bias_ref)
        for part in range(3):
            for each in range(heads):
                at = part * width + each * head_dim
                split[part, each] = qkv_ref[:, at : at + head_dim]
        for number in range(pieces):
            grad = unpack_rows(grad_ref[number])
            for each in range(heads):
                split[3, each, number * piece : (number + 1) * piece, :] = grad[
                    :, each * head_dim : (each + 1) * head_dim
                ]

    acc[...] = jnp.zeros_like(acc)
    values = split[2, head]
    for start in range(0, length, BLOCK_ROWS):
        prob_grad = nt(split[3, head, start : start + BLOCK_ROWS], values)
        prob = prob_ref[0, start : start + BLOCK_ROWS, :].astype(f32)
        weighted = prob * prob_grad
        inner = jnp.sum(weighted, axis=-1, keepdims=True)
        score_grad = weighted - prob * inner
        score_grads[start : start + BLOCK_ROWS, :] = score_grad.astype(bf16)
        for sub in range(0, BLOCK_ROWS, LANES):
            off = length - LANES - start - sub
            acc[:, off : off + length] += score_grad[sub : sub + LANES]
    outs[0, head] = nn(score_grads[...], split[1, head])
    outs[1, head] = tn(score_grads[...], split[0, head])
    outs[2, head] = tn(prob_ref[0], split[3, head])

    part = acc[...]
    rows = LANES
    while rows > 8:
        rows //= 2
        part = part[:rows] + pltpu.roll(part[rows:], span - rows, 1)
    offsets = part[0:1]
    for row in range(1, 8):
        offsets = offsets + pltpu.roll(part[row : row + 1], span - row, 1)
    offsets = pltpu.roll(offsets, LANES - 1, 1)
    hot = lax.broadcasted_iota(jnp.int32, (bias_ref.shape[0], span), 0) == bucket_ref[...]
    total = jnp.sum(jnp.where(hot, offsets, 0.0), axis=1, keepdims=True)
    lane = lax.broadcasted_iota(jnp.int32, bias_ref.shape, 1)
    bias_ref[...] = jnp.where(lane == head, total, bias_ref[...])

    @pl.when(head == heads - 1)
    def _():
        joined = jnp.concatenate(
            [outs[part, each].astype(bf16) for part in range(3) for each in range(heads)], axis=1
        )
        for number in range(pieces):
            out_ref[number] = pack_rows(joined[number * piece : (number + 1) * piece])


def attend_back(qkv, prob, grad, bucket_row, bucket_count):
    length, cols = qkv.shape
    heads = prob.shape[0]
    head_dim = cols // (3 * heads)
    pieces, half, _ = grad.shape
    out_shape = [shape((pieces, half, 2 * cols), bf16), shape((bucket_count, LANES), f32)]
    return pl.pallas_call(
        attend_back_kernel,
        grid=(heads,),
        in_specs=[
            whole(qkv),
            pl.BlockSpec((1, length, length), lambda h: (h, 0, 0)),
            whole(grad),
            whole(bucket_row),
        ],
        out_specs=[whole(a) for a in out_shape],
        out_shape=out_shape,
        scratch_shapes=[
            pltpu.VMEM((4, heads, length, head_dim), bf16),
            pltpu.VMEM((3, heads, length, head_dim), f32),
            pltpu.VMEM((LANES, 2 * length), f32),
            pltpu.VMEM((length, length), bf16),
        ],
        compiler_params=PARAMS,
        cost_estimate=cost(40 * heads * length * length * head_dim, qkv, prob, grad),
        name="attend_back",
    )(qkv, prob, grad, bucket_row)


def project_kernel(
    x_ref, dy_ref, id_ref, target_ref, gain_ref, dense_ref, *refs
):
    att_refs, (middle_ref, second_ref, flat_ref, prob_ref, sent_ref, grad_ref) = refs[:-6], refs[-6:]
    model = x_ref.shape[1]
    flats = []
    for ref in att_refs:
        flats.append(
            jnp.concatenate([unpack_rows(ref[g]) for g in range(ref.shape[0])], axis=1)
        )
    flat = jnp.concatenate(flats, axis=0)
    flat_ref[...] = flat
    middle = x_ref[...].astype(f32) + nn(flat, dense_ref[:, :model])
    middle_ref[...] = middle
    second = (middle * inverse_norm(middle) * gain_ref[...]).astype(bf16)
    second_ref[...] = second
    positions = sent_ref.shape[0]
    hot = (
        lax.broadcasted_iota(jnp.int32, (positions, x_ref.shape[0]), 0) == target_ref[...]
    ).astype(bf16)
    sent_ref[...] = nn(hot, second).astype(bf16)
    logits = nn(second, dense_ref[:, model:])
    peak = jnp.max(logits, axis=-1, keepdims=True)
    grown = jnp.exp(logits - peak)
    probs = grown / jnp.sum(grown, axis=-1, keepdims=True)
    prob_ref[...] = probs
    chosen = lax.broadcasted_iota(jnp.int32, probs.shape, 1) == id_ref[...]
    gate = jnp.sum(jnp.where(chosen, probs, 0.0), axis=-1, keepdims=True)
    out_grad = (gate * dy_ref[...].astype(f32)).astype(bf16)
    grad_ref[...] = nn(hot, out_grad).astype(bf16)


def project(x, dy, id_column, target_row, gain, dense, attended, positions):
    tokens, model = x.shape
    experts = dense.shape[1] - model
    out_shape = [
        shape((tokens, model), f32),
        shape((tokens, model), bf16),
        shape((tokens, model), bf16),
        shape((tokens, experts), f32),
        shape((positions, model), bf16),
        shape((positions, model), bf16),
    ]
    operands = (x, dy, id_column, target_row, gain, dense, *attended)
    return pl.pallas_call(
        project_kernel,
        in_specs=[whole(a) for a in operands],
        out_specs=[whole(a) for a in out_shape],
        out_shape=out_shape,
        compiler_params=PARAMS,
        cost_estimate=cost(2 * tokens * model * (model + 2 * positions), *out_shape),
        name="project",
    )(*operands)


def returned_kernel(
    back_ref, target_ref, id_ref, middle_ref, dy_ref, prob_ref, second_ref,
    out_ref, logit_ref, router_ref,
):
    tokens = middle_ref.shape[0]
    hot = (
        lax.broadcasted_iota(jnp.int32, (tokens, back_ref.shape[0]), 1) == target_ref[...]
    ).astype(bf16)
    token_out = nn(hot, back_ref[...])
    probs = prob_ref[...]
    chosen = lax.broadcasted_iota(jnp.int32, probs.shape, 1) == id_ref[...]
    gate = jnp.sum(jnp.where(chosen, probs, 0.0), axis=-1, keepdims=True)
    out_ref[...] = (middle_ref[...] + gate * token_out).astype(bf16)
    gate_grad = jnp.sum(dy_ref[...].astype(f32) * token_out, axis=-1, keepdims=True)
    picked = jnp.where(chosen, gate_grad, 0.0)
    logit_grad = probs * (picked - jnp.sum(probs * picked, axis=-1, keepdims=True))
    logit_low = logit_grad.astype(bf16)
    logit_ref[...] = logit_low
    router_ref[...] = tn(second_ref[...], logit_low).astype(bf16)


def returned(back, target_column, id_column, middle, dy, probs, second):
    tokens, model = middle.shape
    experts = probs.shape[1]
    out_shape = [
        shape((tokens, model), bf16),
        shape((tokens, experts), bf16),
        shape((model, experts), bf16),
    ]
    operands = (back, target_column, id_column, middle, dy, probs, second)
    return pl.pallas_call(
        returned_kernel,
        in_specs=[whole(a) for a in operands],
        out_specs=[whole(a) for a in out_shape],
        out_shape=out_shape,
        compiler_params=PARAMS,
        cost_estimate=cost(2 * tokens * model * back.shape[0], *out_shape, middle, back),
        name="returned",
    )(*operands)


def branch_kernel(
    back_ref, target_ref, logit_ref, dense_ref, middle_ref, gain_ref, dy_ref,
    middle_grad_ref, branch_ref, grad_ref, gain_grad_ref,
):
    tokens, model = middle_ref.shape
    hot = (
        lax.broadcasted_iota(jnp.int32, (tokens, back_ref.shape[0]), 1) == target_ref[...]
    ).astype(bf16)
    second_grad = nn(hot, back_ref[...]) + nt(logit_ref[...], dense_ref[:, model:])
    norm_grad, gain_grad = norm_backward(middle_ref[...], gain_ref[...], second_grad)
    gain_grad_ref[...] = gain_grad
    middle_grad = dy_ref[...].astype(f32) + norm_grad
    middle_grad_ref[...] = middle_grad
    branch = middle_grad.astype(bf16)
    branch_ref[...] = branch
    grad = nt(branch, dense_ref[:, :model]).astype(bf16)
    groups = grad_ref.shape[0]
    width = model // groups
    for group in range(groups):
        grad_ref[group] = pack_rows(grad[:, group * width : (group + 1) * width])


def branch_back(back, target_column, logit, dense, middle, gain, dy, number, seqs, groups):
    tokens, model = middle.shape
    piece = tokens // seqs

    def rows_of(array):
        return pl.BlockSpec((piece, array.shape[1]), lambda _: (number, 0))

    out_shape = [
        shape((piece, model), f32),
        shape((piece, model), bf16),
        shape((groups, piece // 2, 2 * model // groups), bf16),
        shape((1, model), f32),
    ]
    return pl.pallas_call(
        branch_kernel,
        grid=(1,),
        in_specs=[
            whole(back), rows_of(target_column), rows_of(logit), whole(dense), rows_of(middle),
            whole(gain), rows_of(dy),
        ],
        out_specs=[whole(a) for a in out_shape],
        out_shape=out_shape,
        compiler_params=PARAMS,
        cost_estimate=cost(2 * piece * model * (back.shape[0] + model), *out_shape, back, dense),
        name="branch_back",
    )(back, target_column, logit, dense, middle, gain, dy)


def input_kernel(grad_ref, weight_ref, x_ref, gain_ref, middle_grad_ref, *refs):
    out_ref, gain_grad_ref = refs[-2:]
    total = None
    for group in range(weight_ref.shape[0]):
        part = nt(unpack_rows(grad_ref[group]), weight_ref[group])
        total = part if total is None else total + part
    norm_grad, gain_grad = norm_backward(x_ref[0].astype(f32), gain_ref[...], total)
    out_ref[0] = middle_grad_ref[...] + norm_grad
    gain_grad_ref[...] = gain_grad


def input_back(grad, weights, x, gain, middle_grad, number, earlier):
    seqs, piece, model = x.shape
    row_spec = pl.BlockSpec((1, piece, model), lambda _: (number, 0, 0))
    out_shape = [shape(x.shape, f32), shape((1, model), f32)]
    operands = [grad, weights, x, gain, middle_grad]
    specs = [whole(grad), whole(weights), row_spec, whole(gain), whole(middle_grad)]
    aliases = {}
    if earlier is not None:
        aliases = {len(operands): 0}
        operands.append(earlier)
        specs.append(pl.BlockSpec(memory_space=pl.ANY))
    return pl.pallas_call(
        input_kernel,
        grid=(1,),
        in_specs=specs,
        out_specs=[row_spec, whole(out_shape[1])],
        out_shape=out_shape,
        input_output_aliases=aliases,
        compiler_params=PARAMS,
        cost_estimate=cost(2 * piece * math.prod(weights.shape), grad, weights, middle_grad),
        name="input_back",
    )(*operands)


def column_kernel(seqs, place_ref, *refs):
    count = len(refs) - 2 * seqs - 1
    row_refs, grad_refs, out_refs = refs[:seqs], refs[seqs : 2 * seqs], refs[2 * seqs : -1]
    total = refs[-1]
    value = None
    for row_ref, grad_ref in zip(row_refs, grad_refs):
        grad = jnp.concatenate(
            [unpack_rows(grad_ref[piece]) for piece in range(grad_ref.shape[0])], axis=0
        )
        part = tn(row_ref[...], grad)
        value = part if value is None else value + part
    total[...] = value.astype(bf16)
    for number in range(count):
        rows = out_refs[number].shape[0]
        at = pl.multiple_of(place_ref[number] * rows, rows)
        out_refs[number][...] = total[pl.ds(at, rows), :]


def column_grads(places, rows, grads, chunks):
    model = rows[0].shape[1]
    cols = grads[0].shape[2] // 2
    out_shape = [shape((model // chunks, cols), bf16)] * chunks
    return pl.pallas_call(
        functools.partial(column_kernel, len(rows)),
        in_specs=[SMEM] + [whole(a) for a in (*rows, *grads)],
        out_specs=[whole(a) for a in out_shape],
        out_shape=out_shape,
        scratch_shapes=[pltpu.VMEM((model, cols), bf16)],
        compiler_params=PARAMS,
        cost_estimate=cost(2 * sum(math.prod(r.shape) for r in rows) * cols, *rows, *grads),
        name="column_grads",
    )(places, *rows, *grads)


def column_order_kernel(place_ref, *refs):
    out_ref, held = refs[-2:]
    groups = held.shape[0]
    width = held.shape[2] // 3
    for number in range(groups):
        held[number] = refs[number][...].astype(f32)
    for part in range(3):
        joined = [
            held[place_ref[group], :, part * width : (part + 1) * width] for group in range(groups)
        ]
        out_ref[:, part * groups * width : (part + 1) * groups * width] = jnp.concatenate(
            joined, axis=1
        )


def column_order(places, pieces):
    rows, cols = pieces[0].shape
    out_shape = shape((rows, cols * len(pieces)), f32)
    return pl.pallas_call(
        column_order_kernel,
        in_specs=[SMEM] + [whole(a) for a in pieces],
        out_specs=whole(out_shape),
        out_shape=out_shape,
        scratch_shapes=[pltpu.VMEM((len(pieces), rows, cols), f32)],
        compiler_params=PARAMS,
        cost_estimate=cost(0, out_shape, *pieces),
        name="column_order",
    )(places, *pieces)


def expert_kernel(x_ref, win_ref, wout_ref, y_ref, slope_ref, acc):
    tile = pl.program_id(1)
    rows = acc.shape[0]
    x = x_ref[...].reshape(rows, x_ref.shape[-1])
    pre = jnp.dot(x, win_ref[0], preferred_element_type=f32)
    hidden, slope = gelu_and_slope(pre)
    slope_ref[0] = slope.astype(bf16)
    part = jnp.dot(hidden.astype(bf16), wout_ref[0], preferred_element_type=f32)

    @pl.when(tile == 0)
    def _():
        acc[...] = part

    @pl.when(tile > 0)
    def _():
        acc[...] += part

    @pl.when(tile == pl.num_programs(1) - 1)
    def _():
        y_ref[...] = acc[...].astype(bf16).reshape(y_ref.shape)


def expert_forward(x, w_in, w_out, tile):
    sources, experts, slots, model = x.shape
    hidden = w_in.shape[2]
    rows = sources * slots
    row_spec = pl.BlockSpec((sources, 1, slots, model), lambda e, f: (0, e, 0, 0))
    return pl.pallas_call(
        expert_kernel,
        grid=(experts, hidden // tile),
        in_specs=[
            row_spec,
            pl.BlockSpec((1, model, tile), lambda e, f: (e, 0, f)),
            pl.BlockSpec((1, tile, model), lambda e, f: (e, f, 0)),
        ],
        out_specs=[row_spec, pl.BlockSpec((1, rows, tile), lambda e, f: (e, 0, f))],
        out_shape=[
            jax.ShapeDtypeStruct(x.shape, bf16),
            jax.ShapeDtypeStruct((experts, rows, hidden), bf16),
        ],
        scratch_shapes=[pltpu.VMEM((rows, model), f32)],
        compiler_params=pltpu.CompilerParams(vmem_limit_bytes=52 * MIB),
        name="expert_forward",
    )(x, w_in, w_out)


def expert_back_kernel(g_ref, win_ref, wout_ref, slope_ref, y_ref, acc):
    tile = pl.program_id(1)
    rows = acc.shape[0]
    g = g_ref[...].reshape(rows, g_ref.shape[-1])
    pre_grad = (nt(g, wout_ref[0]) * slope_ref[0].astype(f32)).astype(bf16)
    part = nt(pre_grad, win_ref[0])

    @pl.when(tile == 0)
    def _():
        acc[...] = part

    @pl.when(tile > 0)
    def _():
        acc[...] += part

    @pl.when(tile == pl.num_programs(1) - 1)
    def _():
        y_ref[...] = acc[...].astype(bf16).reshape(y_ref.shape)


def expert_backward(g, w_in, w_out, slope, tile):
    sources, experts, slots, model = g.shape
    hidden = w_in.shape[2]
    rows = sources * slots
    row_spec = pl.BlockSpec((sources, 1, slots, model), lambda e, f: (0, e, 0, 0))
    return pl.pallas_call(
        expert_back_kernel,
        grid=(experts, hidden // tile),
        in_specs=[
            row_spec,
            pl.BlockSpec((1, model, tile), lambda e, f: (e, 0, f)),
            pl.BlockSpec((1, tile, model), lambda e, f: (e, f, 0)),
            pl.BlockSpec((1, rows, tile), lambda e, f: (e, 0, f)),
        ],
        out_specs=row_spec,
        out_shape=jax.ShapeDtypeStruct(g.shape, bf16),
        scratch_shapes=[pltpu.VMEM((rows, model), f32)],
        compiler_params=pltpu.CompilerParams(vmem_limit_bytes=52 * MIB),
        name="expert_backward",
    )(g, w_in, w_out, slope)


def weight_grad_kernel(pieces, place_ref, *refs):
    x_refs, g_refs = refs[:pieces], refs[pieces : 2 * pieces]
    win_ref, wout_ref = refs[2 * pieces : 2 * pieces + 2]
    gin_ref, gout_ref = refs[-2:]
    gin = gout = None
    for x_ref, g_ref in zip(x_refs, g_refs):
        rows = x_ref.shape[0] * x_ref.shape[2]
        x = x_ref[...].reshape(rows, x_ref.shape[-1])
        g = g_ref[...].reshape(rows, g_ref.shape[-1])
        hidden, slope = gelu_and_slope(nn(x, win_ref[0]))
        pre_grad = (nt(g, wout_ref[0]) * slope).astype(bf16)
        gin_part = tn(x, pre_grad)
        gout_part = tn(hidden.astype(bf16), g)
        gin = gin_part if gin is None else gin + gin_part
        gout = gout_part if gout is None else gout + gout_part
    gin_ref[0] = gin
    gout_ref[0] = gout


def weight_grads(place, xs, gs, w_in, w_out, ways, expert, earlier):
    experts, model, hidden = w_in.shape
    cols = hidden // ways
    tile = GRAD_TILE if cols % GRAD_TILE == 0 else cols
    tiles = cols // tile

    def rows_of(array):
        sources, _, slots, _ = array.shape
        return pl.BlockSpec((sources, 1, slots, model), lambda t, q: (0, expert, 0, 0))

    out_shape = [shape((experts, model, cols), f32), shape((experts, cols, model), f32)]
    flops = 8 * sum(math.prod(a.shape) for a in xs) * cols // experts
    operands = [place, *xs, *gs, w_in, w_out]
    specs = [rows_of(a) for a in (*xs, *gs)] + [
        pl.BlockSpec((1, model, tile), lambda t, q: (expert, 0, q[0] * tiles + t)),
        pl.BlockSpec((1, tile, model), lambda t, q: (expert, q[0] * tiles + t, 0)),
    ]
    aliases = {}
    if earlier is not None:
        aliases = {len(operands): 0, len(operands) + 1: 1}
        operands += list(earlier)
        specs += [pl.BlockSpec(memory_space=pl.ANY)] * 2
    return pl.pallas_call(
        functools.partial(weight_grad_kernel, len(xs)),
        grid_spec=pltpu.PrefetchScalarGridSpec(
            num_scalar_prefetch=1,
            grid=(tiles,),
            in_specs=specs,
            out_specs=[
                pl.BlockSpec((1, model, tile), lambda t, q: (expert, 0, t)),
                pl.BlockSpec((1, tile, model), lambda t, q: (expert, t, 0)),
            ],
        ),
        out_shape=out_shape,
        input_output_aliases=aliases,
        compiler_params=PARAMS,
        cost_estimate=cost(2 * flops, *out_shape, *xs, *gs),
        name="weight_grads",
    )(*operands)


def partners(ways, step):
    return [(index, index ^ step) for index in range(ways)]


def swap(value, axis, step):
    return lax.ppermute(value, axis, partners(lax.axis_size(axis), step))


def gather_near(value):
    return swap(value, "seq", 1), swap(value, "seq", 2)


def gather_far(near, far):
    half = near.shape[0] // 2
    return swap(near[:half], "seq", 2), swap(far[half:], "seq", 1)


def sum_all(value):
    for axis in ("seq", "shard"):
        step = 1
        while step < lax.axis_size(axis):
            value = value + swap(value, axis, step)
            step *= 2
    return value


def scatter_rows(value):
    ways = lax.axis_size("shard")
    rows, cols = value.shape
    parts = lax.all_to_all(value.reshape(ways, rows // ways, cols), "shard", 0, 0, tiled=True)
    return jnp.sum(parts.astype(f32), axis=0)


def body(
    block_input,
    gain_attn,
    gain_ffn,
    w_qkv,
    w_out,
    w_router,
    rel_bias,
    w_in,
    w_exp_out,
    expert_id,
    capacity_slot,
    buckets,
    output_grad,
):
    seqs, piece, model = block_input.shape
    seq_ways = lax.axis_size("seq")
    shard_ways = lax.axis_size("shard")
    bucket_count, heads_all = rel_bias.shape
    heads = heads_all // seq_ways
    width = model // seq_ways
    length = piece * seq_ways
    experts = w_router.shape[1]
    tokens = seqs * piece
    capacity = 2 * tokens // experts
    positions = experts * capacity
    slot_shape = (shard_ways, experts // shard_ways, capacity, model)
    weight_rows = w_qkv.shape[0]
    seq_index = lax.axis_index("seq").astype(jnp.int32)
    places = jnp.stack([seq_index ^ step for step in range(seq_ways)])
    gain_one_row = gain_attn.reshape(1, model)
    gain_two_row = gain_ffn.reshape(1, model)
    bucket_row = jnp.pad(
        buckets, (0, 2 * length - buckets.shape[0]), constant_values=-1
    ).reshape(1, 2 * length)
    target = jnp.where(capacity_slot < capacity, expert_id * capacity + capacity_slot, -1)
    target_row = target.reshape(1, tokens)
    target_column = target.reshape(tokens, 1)
    id_column = expert_id.reshape(tokens, 1)
    upstream = output_grad.reshape(tokens, model)

    own_columns = lax.dynamic_slice_in_dim(
        w_qkv.reshape(weight_rows, 3, model), seq_index * width, width, 2
    ).reshape(weight_rows, 3 * width)
    own_columns = jnp.pad(own_columns, ((0, 0), (0, max(0, model - 3 * width))))
    head_weight = lax.all_gather(own_columns, "shard", axis=0, tiled=True)
    dense_rows, head_weight = lax.optimization_barrier(
        (jnp.concatenate([w_out, w_router], axis=1), head_weight)
    )
    dense = lax.all_gather(dense_rows, "shard", axis=0, tiled=True)
    inputs = block_input.astype(f32)
    normed = (inputs * inverse_norm(inputs) * gain_attn).astype(bf16)
    tiles = bias_tiles(
        lax.dynamic_slice_in_dim(rel_bias, seq_index * heads, heads, 1), bucket_row
    )

    first_near = gather_near(normed[0])
    held = lax.optimization_barrier((normed[1], first_near))
    first_near = held[1]
    second_near = gather_near(held[0])
    first_far = gather_far(*first_near)
    second_far = gather_far(*second_near)
    sequence_pieces = (
        (normed[0], *first_near, *first_far),
        (normed[1], *second_near, *second_far),
    )
    kept, attended_tok = [], []
    for pieces in sequence_pieces:
        rows, qkv, attended, probs = attend(places, pieces, head_weight, tiles)
        kept.append((rows, qkv, probs))
        attended_tok.append(lax.all_to_all(attended, "seq", 0, 0, tiled=True))

    middle, second, attended_flat, router_probs, sent, sent_grad = project(
        block_input.reshape(tokens, model),
        upstream,
        id_column,
        target_row,
        gain_two_row,
        dense,
        attended_tok,
        positions,
    )

    def exchange(rows):
        return lax.all_to_all(rows, "shard", 0, 0, tiled=True)

    held_weight, sent = lax.optimization_barrier((head_weight, sent))
    weight_groups = lax.all_gather(held_weight[:, : 3 * width], "seq")
    arrived = exchange(sent.reshape(slot_shape))
    out_arrived = exchange(sent_grad.reshape(slot_shape))
    arrived_near = gather_near(arrived)
    expert_out, slope = expert_forward(arrived, w_in, w_exp_out, FORWARD_TILE)
    expert_out, weight_groups = lax.optimization_barrier((expert_out, weight_groups))
    back_out = exchange(expert_out).reshape(positions, model)
    rows_grad = expert_backward(out_arrived, w_in, w_exp_out, slope, FORWARD_TILE)
    arrived_near, rows_grad = lax.optimization_barrier((arrived_near, rows_grad))
    back_grad = exchange(rows_grad).reshape(positions, model)
    arrived_far = gather_far(*arrived_near)
    out_near = gather_near(out_arrived)
    back_out, arrived_far, out_near = lax.optimization_barrier((back_out, arrived_far, out_near))
    out_far = gather_far(*out_near)
    block_output, logit_low, grad_router = returned(
        back_out, target_column, id_column, middle, upstream, router_probs, second
    )
    expert_xs = (arrived, *arrived_near, *arrived_far)
    expert_gs = (out_arrived, *out_near, *out_far)
    expert_count = experts // shard_ways

    def expert_grads(number, earlier):
        return weight_grads(
            places, expert_xs, expert_gs, w_in, w_exp_out, seq_ways, number, earlier
        )

    expert_part = expert_grads(0, None)
    back_grad, expert_part, logit_low = lax.optimization_barrier(
        (back_grad, expert_part, logit_low)
    )
    middle_grads, branches, grad_heads, gain_two = [], [], [], []
    for number in range(seqs):
        middle_grad, branch, attended_grad, gain_part = branch_back(
            back_grad, target_column, logit_low, dense, middle, gain_two_row, upstream,
            number, seqs, seq_ways,
        )
        middle_grads.append(middle_grad)
        branches.append(branch)
        gain_two.append(gain_part)
        grad_heads.append(lax.all_to_all(attended_grad, "seq", 0, 0, tiled=True))
    grad_out = sum(
        tn(attended_flat[number * piece : (number + 1) * piece], branches[number])
        for number in range(seqs)
    )
    grad_dense = jnp.concatenate([grad_out.astype(bf16), grad_router], axis=1)
    grad_dense = lax.psum_scatter(grad_dense, "shard", scatter_dimension=0, tiled=True)
    grad_dense = grad_dense.astype(f32)
    for step in (1, 2):
        grad_dense = grad_dense + swap(grad_dense, "seq", step)

    qkv_grads, bias_parts, grad_tok = [], [], []
    for number in range(seqs):
        _, qkv, probs = kept[number]
        grad = grad_heads[number]
        qkv_grad, bias_part = attend_back(qkv, probs, grad, bucket_row, bucket_count)
        qkv_grads.append(qkv_grad)
        bias_parts.append(bias_part)
        grad_tok.append(lax.all_to_all(qkv_grad, "seq", 0, 0, tiled=True))
    rows_all = [each[0] for each in kept]
    if shard_ways <= 8 and weight_rows % 16 == 0:
        shard_index = lax.axis_index("shard").astype(jnp.int32)
        order = jnp.stack([shard_index ^ step for step in range(shard_ways)])
        chunks = column_grads(order, rows_all, qkv_grads, shard_ways)
        got = [chunks[0]] + [swap(chunks[step], "shard", step) for step in range(1, shard_ways)]
        columns = functools.reduce(jnp.add, [each.astype(f32) for each in got])
        last = chunks[0]
    else:
        (last,) = column_grads(places - places, rows_all, qkv_grads, 1)
        columns = scatter_rows(last)
    columns = columns.astype(bf16)
    expert_gs = lax.optimization_barrier((expert_gs, last))[0]
    for number in range(1, expert_count):
        expert_part = expert_grads(number, expert_part)
    grad_in_part, grad_exp_part = expert_part
    grad_qkv = column_order(
        places, [columns] + [swap(columns, "seq", step) for step in range(1, seq_ways)]
    )
    input_grad, gain_one = None, []
    for number in range(seqs):
        input_grad, gain_part = input_back(
            grad_tok[number], weight_groups, block_input, gain_one_row, middle_grads[number],
            number, input_grad,
        )
        gain_one.append(gain_part)
    bias_grad = lax.dynamic_update_slice_in_dim(
        jnp.zeros((bucket_count, heads_all), f32),
        functools.reduce(jnp.add, bias_parts)[:, :heads],
        seq_index * heads,
        1,
    )
    small = sum_all(
        jnp.concatenate(
            [bias_grad.reshape(-1), sum(gain_two).reshape(-1), sum(gain_one).reshape(-1)]
        ).reshape(-1, LANES)
    ).reshape(-1)
    bias_size = bucket_count * heads_all
    return (
        block_output.reshape(block_input.shape),
        input_grad,
        small[bias_size + model :],
        small[bias_size : bias_size + model],
        grad_qkv,
        grad_dense[:, :model],
        grad_dense[:, model:],
        small[:bias_size].reshape(bucket_count, heads_all),
        grad_in_part,
        grad_exp_part,
    )


def solution(mesh):
    placed = (
        P("shard", "seq", None),
        P(),
        P(),
        P("shard", None),
        P("shard", None),
        P("shard", None),
        P(),
        P("shard", None, None),
        P("shard", None, None),
        P("shard", "seq"),
        P("shard", "seq"),
        P(),
        P("shard", "seq", None),
    )
    return jax.shard_map(
        body,
        mesh=mesh,
        in_specs=placed,
        out_specs=(
            P("shard", "seq", None),
            P("shard", "seq", None),
            P(),
            P(),
            P("shard", None),
            P("shard", None),
            P("shard", None),
            P(),
            P("shard", None, "seq"),
            P("shard", "seq", None),
        ),
        check_vma=False,
    )
```

```python
import functools
import math

import jax
import jax.numpy as jnp
from jax import lax
from jax.experimental import pallas as pl
from jax.experimental.pallas import tpu as pltpu
from jax.sharding import PartitionSpec as P

f32 = jnp.float32
bf16 = jnp.bfloat16
LANES = 128
MIB = 1024 * 1024
BLOCK_ROWS = 256
FORWARD_TILE = 1024
GRAD_TILE = 384
norm_eps = 1e-06
ROOT_HALF = 1.0 / math.sqrt(2.0)
DENSITY = 1.0 / math.sqrt(2.0 * math.pi)
PARAMS = pltpu.CompilerParams(vmem_limit_bytes=52 * MIB)
SMEM = pl.BlockSpec(memory_space=pltpu.SMEM)


def nn(a, b):
    return jnp.dot(a, b, preferred_element_type=f32)


def nt(a, b):
    return lax.dot_general(a, b, (((1,), (1,)), ((), ())), preferred_element_type=f32)


def tn(a, b):
    return lax.dot_general(a, b, (((0,), (0,)), ((), ())), preferred_element_type=f32)


def whole(array):
    zeros = (0,) * array.ndim
    return pl.BlockSpec(array.shape, lambda *_: zeros)


def cost(flops, *arrays):
    return pl.CostEstimate(
        flops=int(flops),
        bytes_accessed=int(sum(math.prod(a.shape) * a.dtype.itemsize for a in arrays)),
        transcendentals=0,
    )


def shape(dims, kind):
    return jax.ShapeDtypeStruct(dims, kind)


def pack_rows(values):
    half = values.shape[0] // 2
    return jnp.concatenate([values[:half], values[half:]], axis=1)


def unpack_rows(packed):
    width = packed.shape[1] // 2
    return jnp.concatenate([packed[:, :width], packed[:, width:]], axis=0)


def inverse_norm(values):
    return lax.rsqrt(jnp.mean(values * values, axis=-1, keepdims=True) + norm_eps)


def norm_backward(values, gain, upstream):
    inverse = inverse_norm(values)
    scaled = upstream * gain
    inner = jnp.mean(scaled * values, axis=-1, keepdims=True)
    result = inverse * scaled - values * (inverse * inverse * inverse * inner)
    return result, jnp.sum(upstream * values * inverse, axis=0, keepdims=True)


def gelu_and_slope(v):
    cumulative = 0.5 * (1.0 + lax.erf(v * ROOT_HALF))
    return v * cumulative, cumulative + v * (jnp.exp(-0.5 * v * v) * DENSITY)


def bias_kernel(rel_ref, bucket_ref, out_ref):
    span = bucket_ref.shape[1]
    bucket_row = bucket_ref[...]
    for head in range(out_ref.shape[0]):
        row = jnp.zeros((1, span), f32)
        for bucket in range(rel_ref.shape[0]):
            row = jnp.where(bucket_row == bucket, rel_ref[bucket, head], row)
        out_ref[head] = pltpu.roll(
            jnp.broadcast_to(row, (LANES, span)), span - LANES + 1, 1, stride=1, stride_axis=0
        )


def bias_tiles(rel, bucket_row):
    out_shape = shape((rel.shape[1], LANES, bucket_row.shape[1]), f32)
    return pl.pallas_call(
        bias_kernel,
        in_specs=[SMEM, whole(bucket_row)],
        out_specs=whole(out_shape),
        out_shape=out_shape,
        compiler_params=PARAMS,
        cost_estimate=cost(0, out_shape),
        name="bias_tiles",
    )(rel, bucket_row)


def attend_kernel(
    place_ref, own_ref, near_ref, far_ref, low_ref, high_ref, w_ref, toeplitz_ref,
    rows_ref, qkv_ref, att_ref, prob_ref, split, outs,
):
    head = pl.program_id(0)
    heads, length, head_dim = outs.shape
    width = heads * head_dim
    piece = own_ref.shape[0]

    @pl.when(head == 0)
    def _():
        for number, ref in enumerate((own_ref, near_ref, far_ref)):
            at = pl.multiple_of(place_ref[number] * piece, piece)
            rows_ref[pl.ds(at, piece), :] = ref[...]
        at = pl.multiple_of(place_ref[3] * piece, piece)
        half = piece // 2
        rows_ref[pl.ds(at, half), :] = low_ref[...]
        rows_ref[pl.ds(pl.multiple_of(at + half, half), half), :] = high_ref[...]
        qkv = nn(rows_ref[...], w_ref[:, : 3 * width]).astype(bf16)
        qkv_ref[...] = qkv
        for part in range(3):
            for each in range(heads):
                at = part * width + each * head_dim
                split[part, each] = qkv[:, at : at + head_dim]

    keys = split[1, head]
    values = split[2, head]
    for start in range(0, length, BLOCK_ROWS):
        scores = nt(split[0, head, start : start + BLOCK_ROWS], keys)
        parts = []
        for sub in range(0, BLOCK_ROWS, LANES):
            off = length - LANES - start - sub
            parts.append(scores[sub : sub + LANES] + toeplitz_ref[0, :, off : off + length])
        scores = jnp.concatenate(parts, axis=0)
        peak = jnp.max(scores, axis=-1, keepdims=True)
        grown = jnp.exp(scores - peak)
        total = jnp.sum(grown, axis=-1, keepdims=True)
        prob = (grown * (1.0 / total)).astype(bf16)
        prob_ref[0, start : start + BLOCK_ROWS, :] = prob
        outs[head, start : start + BLOCK_ROWS, :] = nn(prob, values)

    @pl.when(head == heads - 1)
    def _():
        joined = jnp.concatenate([outs[each].astype(bf16) for each in range(heads)], axis=1)
        for number in range(length // piece):
            att_ref[number] = pack_rows(joined[number * piece : (number + 1) * piece])


def attend(place, pieces, weight, tiles):
    own, near, far, low, high = pieces
    piece, model = own.shape
    heads, _, span = tiles.shape
    length = span // 2
    cols = 3 * (model // (length // piece))
    width = cols // 3
    head_dim = width // heads
    out_shape = [
        shape((length, model), bf16),
        shape((length, cols), bf16),
        shape((length // piece, piece // 2, 2 * width), bf16),
        shape((heads, length, length), bf16),
    ]
    return pl.pallas_call(
        attend_kernel,
        grid=(heads,),
        in_specs=[SMEM]
        + [whole(a) for a in (own, near, far, low, high, weight)]
        + [pl.BlockSpec((1, LANES, span), lambda h: (h, 0, 0))],
        out_specs=[whole(a) for a in out_shape[:3]]
        + [pl.BlockSpec((1, length, length), lambda h: (h, 0, 0))],
        out_shape=out_shape,
        scratch_shapes=[
            pltpu.VMEM((3, heads, length, head_dim), bf16),
            pltpu.VMEM((heads, length, head_dim), f32),
        ],
        compiler_params=PARAMS,
        cost_estimate=cost(2 * length * model * cols + 16 * heads * length * length * head_dim, *out_shape),
        name="attend",
    )(place, own, near, far, low, high, weight, tiles)


def attend_back_kernel(
    qkv_ref, prob_ref, grad_ref, bucket_ref, out_ref, bias_ref, split, outs, acc, score_grads
):
    head = pl.program_id(0)
    heads, length, head_dim = outs.shape[1:]
    width = heads * head_dim
    span = 2 * length
    pieces, half, _ = grad_ref.shape
    piece = 2 * half

    @pl.when(head == 0)
    def _():
        bias_ref[...] = jnp.zeros_like(bias_ref)
        for part in range(3):
            for each in range(heads):
                at = part * width + each * head_dim
                split[part, each] = qkv_ref[:, at : at + head_dim]
        for number in range(pieces):
            grad = unpack_rows(grad_ref[number])
            for each in range(heads):
                split[3, each, number * piece : (number + 1) * piece, :] = grad[
                    :, each * head_dim : (each + 1) * head_dim
                ]

    acc[...] = jnp.zeros_like(acc)
    values = split[2, head]
    for start in range(0, length, BLOCK_ROWS):
        prob_grad = nt(split[3, head, start : start + BLOCK_ROWS], values)
        prob = prob_ref[0, start : start + BLOCK_ROWS, :].astype(f32)
        weighted = prob * prob_grad
        inner = jnp.sum(weighted, axis=-1, keepdims=True)
        score_grad = weighted - prob * inner
        score_grads[start : start + BLOCK_ROWS, :] = score_grad.astype(bf16)
        for sub in range(0, BLOCK_ROWS, LANES):
            off = length - LANES - start - sub
            acc[:, off : off + length] += score_grad[sub : sub + LANES]
    outs[0, head] = nn(score_grads[...], split[1, head])
    outs[1, head] = tn(score_grads[...], split[0, head])
    outs[2, head] = tn(prob_ref[0], split[3, head])

    part = acc[...]
    rows = LANES
    while rows > 8:
        rows //= 2
        part = part[:rows] + pltpu.roll(part[rows:], span - rows, 1)
    offsets = part[0:1]
    for row in range(1, 8):
        offsets = offsets + pltpu.roll(part[row : row + 1], span - row, 1)
    offsets = pltpu.roll(offsets, LANES - 1, 1)
    hot = lax.broadcasted_iota(jnp.int32, (bias_ref.shape[0], span), 0) == bucket_ref[...]
    total = jnp.sum(jnp.where(hot, offsets, 0.0), axis=1, keepdims=True)
    lane = lax.broadcasted_iota(jnp.int32, bias_ref.shape, 1)
    bias_ref[...] = jnp.where(lane == head, total, bias_ref[...])

    @pl.when(head == heads - 1)
    def _():
        joined = jnp.concatenate(
            [outs[part, each].astype(bf16) for part in range(3) for each in range(heads)], axis=1
        )
        for number in range(pieces):
            out_ref[number] = pack_rows(joined[number * piece : (number + 1) * piece])


def attend_back(qkv, prob, grad, bucket_row, bucket_count):
    length, cols = qkv.shape
    heads = prob.shape[0]
    head_dim = cols // (3 * heads)
    pieces, half, _ = grad.shape
    out_shape = [shape((pieces, half, 2 * cols), bf16), shape((bucket_count, LANES), f32)]
    return pl.pallas_call(
        attend_back_kernel,
        grid=(heads,),
        in_specs=[
            whole(qkv),
            pl.BlockSpec((1, length, length), lambda h: (h, 0, 0)),
            whole(grad),
            whole(bucket_row),
        ],
        out_specs=[whole(a) for a in out_shape],
        out_shape=out_shape,
        scratch_shapes=[
            pltpu.VMEM((4, heads, length, head_dim), bf16),
            pltpu.VMEM((3, heads, length, head_dim), f32),
            pltpu.VMEM((LANES, 2 * length), f32),
            pltpu.VMEM((length, length), bf16),
        ],
        compiler_params=PARAMS,
        cost_estimate=cost(40 * heads * length * length * head_dim, qkv, prob, grad),
        name="attend_back",
    )(qkv, prob, grad, bucket_row)


def project_kernel(x_ref, target_ref, gain_ref, dense_ref, *refs):
    att_refs, (middle_ref, second_ref, sent_ref) = refs[:-3], refs[-3:]
    model = x_ref.shape[1]
    flats = []
    for ref in att_refs:
        flats.append(
            jnp.concatenate([unpack_rows(ref[g]) for g in range(ref.shape[0])], axis=1)
        )
    flat = jnp.concatenate(flats, axis=0)
    middle = x_ref[...].astype(f32) + nn(flat, dense_ref[:, :model])
    middle_ref[...] = middle
    second = (middle * inverse_norm(middle) * gain_ref[...]).astype(bf16)
    second_ref[...] = second
    positions = sent_ref.shape[0]
    hot = (
        lax.broadcasted_iota(jnp.int32, (positions, x_ref.shape[0]), 0) == target_ref[...]
    ).astype(bf16)
    sent_ref[...] = nn(hot, second).astype(bf16)


def project(x, target_row, gain, dense, attended, positions):
    tokens, model = x.shape
    out_shape = [
        shape((tokens, model), f32),
        shape((tokens, model), bf16),
        shape((positions, model), bf16),
    ]
    operands = (x, target_row, gain, dense, *attended)
    return pl.pallas_call(
        project_kernel,
        in_specs=[whole(a) for a in operands],
        out_specs=[whole(a) for a in out_shape],
        out_shape=out_shape,
        compiler_params=PARAMS,
        cost_estimate=cost(2 * tokens * model * (model + positions), *out_shape),
        name="project",
    )(*operands)


def route_kernel(
    second_ref, dy_ref, id_ref, target_ref, dense_ref, *refs
):
    att_refs, (flat_ref, prob_ref, grad_ref) = refs[:-3], refs[-3:]
    tokens, model = dy_ref.shape
    flats = []
    for ref in att_refs:
        flats.append(
            jnp.concatenate([unpack_rows(ref[g]) for g in range(ref.shape[0])], axis=1)
        )
    flat_ref[...] = jnp.concatenate(flats, axis=0)
    logits = nn(second_ref[...], dense_ref[:, model:])
    peak = jnp.max(logits, axis=-1, keepdims=True)
    grown = jnp.exp(logits - peak)
    probs = grown / jnp.sum(grown, axis=-1, keepdims=True)
    prob_ref[...] = probs
    chosen = lax.broadcasted_iota(jnp.int32, probs.shape, 1) == id_ref[...]
    gate = jnp.sum(jnp.where(chosen, probs, 0.0), axis=-1, keepdims=True)
    out_grad = (gate * dy_ref[...].astype(f32)).astype(bf16)
    hot = (
        lax.broadcasted_iota(jnp.int32, (grad_ref.shape[0], tokens), 0) == target_ref[...]
    ).astype(bf16)
    grad_ref[...] = nn(hot, out_grad).astype(bf16)


def route(second, dy, id_column, target_row, dense, attended, positions):
    tokens, model = dy.shape
    out_shape = [
        shape((tokens, model), bf16),
        shape((tokens, dense.shape[1] - model), f32),
        shape((positions, model), bf16),
    ]
    operands = (second, dy, id_column, target_row, dense, *attended)
    return pl.pallas_call(
        route_kernel,
        in_specs=[whole(a) for a in operands],
        out_specs=[whole(a) for a in out_shape],
        out_shape=out_shape,
        compiler_params=PARAMS,
        cost_estimate=cost(2 * tokens * model * positions, *out_shape),
        name="route",
    )(*operands)


def returned_kernel(target_ref, id_ref, middle_ref, dy_ref, prob_ref, second_ref, *refs):
    back_refs, (out_ref, logit_ref, router_ref) = refs[:-3], refs[-3:]
    tokens, model = middle_ref.shape
    back = jnp.concatenate([ref[...].reshape(-1, model) for ref in back_refs], axis=0)
    hot = (
        lax.broadcasted_iota(jnp.int32, (tokens, back.shape[0]), 1) == target_ref[...]
    ).astype(bf16)
    token_out = nn(hot, back)
    probs = prob_ref[...]
    chosen = lax.broadcasted_iota(jnp.int32, probs.shape, 1) == id_ref[...]
    gate = jnp.sum(jnp.where(chosen, probs, 0.0), axis=-1, keepdims=True)
    out_ref[...] = (middle_ref[...] + gate * token_out).astype(bf16)
    gate_grad = jnp.sum(dy_ref[...].astype(f32) * token_out, axis=-1, keepdims=True)
    picked = jnp.where(chosen, gate_grad, 0.0)
    logit_grad = probs * (picked - jnp.sum(probs * picked, axis=-1, keepdims=True))
    logit_low = logit_grad.astype(bf16)
    logit_ref[...] = logit_low
    router_ref[...] = tn(second_ref[...], logit_low).astype(bf16)


def returned(back, target_column, id_column, middle, dy, probs, second):
    tokens, model = middle.shape
    experts = probs.shape[1]
    out_shape = [
        shape((tokens, model), bf16),
        shape((tokens, experts), bf16),
        shape((model, experts), bf16),
    ]
    operands = (target_column, id_column, middle, dy, probs, second, *back)
    return pl.pallas_call(
        returned_kernel,
        in_specs=[whole(a) for a in operands],
        out_specs=[whole(a) for a in out_shape],
        out_shape=out_shape,
        compiler_params=PARAMS,
        cost_estimate=cost(4 * tokens * tokens * model, *out_shape, middle, *back),
        name="returned",
    )(*operands)


def branch_kernel(
    back_ref, target_ref, logit_ref, dense_ref, middle_ref, gain_ref, dy_ref,
    middle_grad_ref, branch_ref, grad_ref, gain_grad_ref,
):
    tokens, model = middle_ref.shape
    hot = (
        lax.broadcasted_iota(jnp.int32, (tokens, back_ref.shape[0]), 1) == target_ref[...]
    ).astype(bf16)
    second_grad = nn(hot, back_ref[...]) + nt(logit_ref[...], dense_ref[:, model:])
    norm_grad, gain_grad = norm_backward(middle_ref[...], gain_ref[...], second_grad)
    gain_grad_ref[...] = gain_grad
    middle_grad = dy_ref[...].astype(f32) + norm_grad
    middle_grad_ref[...] = middle_grad
    branch = middle_grad.astype(bf16)
    branch_ref[...] = branch
    grad = nt(branch, dense_ref[:, :model]).astype(bf16)
    groups = grad_ref.shape[0]
    width = model // groups
    for group in range(groups):
        grad_ref[group] = pack_rows(grad[:, group * width : (group + 1) * width])


def branch_back(back, target_column, logit, dense, middle, gain, dy, number, seqs, groups):
    tokens, model = middle.shape
    piece = tokens // seqs

    def rows_of(array):
        return pl.BlockSpec((piece, array.shape[1]), lambda _: (number, 0))

    out_shape = [
        shape((piece, model), f32),
        shape((piece, model), bf16),
        shape((groups, piece // 2, 2 * model // groups), bf16),
        shape((1, model), f32),
    ]
    return pl.pallas_call(
        branch_kernel,
        grid=(1,),
        in_specs=[
            whole(back), rows_of(target_column), rows_of(logit), whole(dense), rows_of(middle),
            whole(gain), rows_of(dy),
        ],
        out_specs=[whole(a) for a in out_shape],
        out_shape=out_shape,
        compiler_params=PARAMS,
        cost_estimate=cost(6 * piece * model * model, *out_shape, back, dense),
        name="branch_back",
    )(back, target_column, logit, dense, middle, gain, dy)


def input_kernel(grad_ref, weight_ref, x_ref, gain_ref, middle_grad_ref, *refs):
    out_ref, gain_grad_ref = refs[-2:]
    total = None
    for group in range(weight_ref.shape[0]):
        part = nt(unpack_rows(grad_ref[group]), weight_ref[group])
        total = part if total is None else total + part
    norm_grad, gain_grad = norm_backward(x_ref[0].astype(f32), gain_ref[...], total)
    out_ref[0] = middle_grad_ref[...] + norm_grad
    gain_grad_ref[...] = gain_grad


def input_back(grad, weights, x, gain, middle_grad, number, earlier):
    seqs, piece, model = x.shape
    row_spec = pl.BlockSpec((1, piece, model), lambda _: (number, 0, 0))
    out_shape = [shape(x.shape, f32), shape((1, model), f32)]
    operands = [grad, weights, x, gain, middle_grad]
    specs = [whole(grad), whole(weights), row_spec, whole(gain), whole(middle_grad)]
    aliases = {}
    if earlier is not None:
        aliases = {len(operands): 0}
        operands.append(earlier)
        specs.append(pl.BlockSpec(memory_space=pl.ANY))
    return pl.pallas_call(
        input_kernel,
        grid=(1,),
        in_specs=specs,
        out_specs=[row_spec, whole(out_shape[1])],
        out_shape=out_shape,
        input_output_aliases=aliases,
        compiler_params=PARAMS,
        cost_estimate=cost(2 * piece * math.prod(weights.shape), grad, weights, middle_grad),
        name="input_back",
    )(*operands)


def column_kernel(seqs, place_ref, *refs):
    row_refs, grad_refs, out_refs = refs[:seqs], refs[seqs : 2 * seqs], refs[2 * seqs : -1]
    total = refs[-1]
    value = None
    for row_ref, grad_ref in zip(row_refs, grad_refs):
        grad = jnp.concatenate(
            [unpack_rows(grad_ref[piece]) for piece in range(grad_ref.shape[0])], axis=0
        )
        part = tn(row_ref[...], grad)
        value = part if value is None else value + part
    if len(out_refs) == 1:
        out_refs[0][...] = value.astype(bf16)
        return
    total[...] = value.astype(bf16)
    for number in range(2 * out_refs[0].shape[0]):
        ref = out_refs[number % 2]
        rows = ref.shape[1]
        at = pl.multiple_of(place_ref[number] * rows, rows)
        ref[number // 2] = total[pl.ds(at, rows), :]


def column_grads(places, rows, grads, chunks):
    model = rows[0].shape[1]
    cols = grads[0].shape[2] // 2
    if chunks > 1:
        out_shape = [shape((chunks // 2, model // chunks, cols), bf16)] * 2
    else:
        out_shape = [shape((model, cols), bf16)]
    return pl.pallas_call(
        functools.partial(column_kernel, len(rows)),
        in_specs=[SMEM] + [whole(a) for a in (*rows, *grads)],
        out_specs=[whole(a) for a in out_shape],
        out_shape=out_shape,
        scratch_shapes=[pltpu.VMEM((model, cols), bf16)],
        compiler_params=PARAMS,
        cost_estimate=cost(2 * sum(math.prod(r.shape) for r in rows) * cols, *rows, *grads),
        name="column_grads",
    )(places, *rows, *grads)


def column_order_kernel(place_ref, *refs):
    out_ref, held = refs[-2:]
    groups = held.shape[0]
    width = held.shape[2] // 3
    for number in range(groups):
        held[number] = refs[number][...].astype(f32)
    for part in range(3):
        joined = [
            held[place_ref[group], :, part * width : (part + 1) * width] for group in range(groups)
        ]
        out_ref[:, part * groups * width : (part + 1) * groups * width] = jnp.concatenate(
            joined, axis=1
        )


def column_order(places, pieces):
    rows, cols = pieces[0].shape
    out_shape = shape((rows, cols * len(pieces)), f32)
    return pl.pallas_call(
        column_order_kernel,
        in_specs=[SMEM] + [whole(a) for a in pieces],
        out_specs=whole(out_shape),
        out_shape=out_shape,
        scratch_shapes=[pltpu.VMEM((len(pieces), rows, cols), f32)],
        compiler_params=PARAMS,
        cost_estimate=cost(0, out_shape, *pieces),
        name="column_order",
    )(places, *pieces)


def expert_kernel(x_ref, win_ref, wout_ref, y_ref, slope_ref, acc):
    tile = pl.program_id(1)
    rows = acc.shape[0]
    x = x_ref[...].reshape(rows, x_ref.shape[-1])
    pre = jnp.dot(x, win_ref[0], preferred_element_type=f32)
    hidden, slope = gelu_and_slope(pre)
    slope_ref[0] = slope.astype(bf16)
    part = jnp.dot(hidden.astype(bf16), wout_ref[0], preferred_element_type=f32)

    @pl.when(tile == 0)
    def _():
        acc[...] = part

    @pl.when(tile > 0)
    def _():
        acc[...] += part

    @pl.when(tile == pl.num_programs(1) - 1)
    def _():
        y_ref[...] = acc[...].astype(bf16).reshape(y_ref.shape)


def expert_forward(x, w_in, w_out, tile):
    sources, experts, slots, model = x.shape
    hidden = w_in.shape[2]
    rows = sources * slots
    row_spec = pl.BlockSpec((sources, 1, slots, model), lambda e, f: (0, e, 0, 0))
    return pl.pallas_call(
        expert_kernel,
        grid=(experts, hidden // tile),
        in_specs=[
            row_spec,
            pl.BlockSpec((1, model, tile), lambda e, f: (e, 0, f)),
            pl.BlockSpec((1, tile, model), lambda e, f: (e, f, 0)),
        ],
        out_specs=[row_spec, pl.BlockSpec((1, rows, tile), lambda e, f: (e, 0, f))],
        out_shape=[
            jax.ShapeDtypeStruct(x.shape, bf16),
            jax.ShapeDtypeStruct((experts, rows, hidden), bf16),
        ],
        scratch_shapes=[pltpu.VMEM((rows, model), f32)],
        compiler_params=pltpu.CompilerParams(vmem_limit_bytes=52 * MIB),
        name="expert_forward",
    )(x, w_in, w_out)


def expert_back_kernel(g_ref, win_ref, wout_ref, slope_ref, y_ref, acc):
    tile = pl.program_id(1)
    rows = acc.shape[0]
    g = g_ref[...].reshape(rows, g_ref.shape[-1])
    pre_grad = (nt(g, wout_ref[0]) * slope_ref[0].astype(f32)).astype(bf16)
    part = nt(pre_grad, win_ref[0])

    @pl.when(tile == 0)
    def _():
        acc[...] = part

    @pl.when(tile > 0)
    def _():
        acc[...] += part

    @pl.when(tile == pl.num_programs(1) - 1)
    def _():
        y_ref[...] = acc[...].astype(bf16).reshape(y_ref.shape)


def expert_backward(g, w_in, w_out, slope, tile):
    sources, experts, slots, model = g.shape
    hidden = w_in.shape[2]
    rows = sources * slots
    row_spec = pl.BlockSpec((sources, 1, slots, model), lambda e, f: (0, e, 0, 0))
    return pl.pallas_call(
        expert_back_kernel,
        grid=(experts, hidden // tile),
        in_specs=[
            row_spec,
            pl.BlockSpec((1, model, tile), lambda e, f: (e, 0, f)),
            pl.BlockSpec((1, tile, model), lambda e, f: (e, f, 0)),
            pl.BlockSpec((1, rows, tile), lambda e, f: (e, 0, f)),
        ],
        out_specs=row_spec,
        out_shape=jax.ShapeDtypeStruct(g.shape, bf16),
        scratch_shapes=[pltpu.VMEM((rows, model), f32)],
        compiler_params=PARAMS,
        cost_estimate=cost(4 * experts * rows * model * hidden, g, w_in, w_out, slope),
        name="expert_backward",
    )(g, w_in, w_out, slope)


def weight_grad_kernel(pieces, place_ref, *refs):
    x_refs, g_refs = refs[:pieces], refs[pieces : 2 * pieces]
    win_ref, wout_ref = refs[2 * pieces : 2 * pieces + 2]
    earlier = refs[2 * pieces + 2 : -2]
    gin_ref, gout_ref = refs[-2:]
    gin, gout = (earlier[0][0], earlier[1][0]) if earlier else (None, None)
    for x_ref, g_ref in zip(x_refs, g_refs):
        rows = x_ref.shape[0] * x_ref.shape[2]
        x = x_ref[...].reshape(rows, x_ref.shape[-1])
        g = g_ref[...].reshape(rows, g_ref.shape[-1])
        hidden, slope = gelu_and_slope(nn(x, win_ref[0]))
        pre_grad = (nt(g, wout_ref[0]) * slope).astype(bf16)
        gin_part = tn(x, pre_grad)
        gout_part = tn(hidden.astype(bf16), g)
        gin = gin_part if gin is None else gin + gin_part
        gout = gout_part if gout is None else gout + gout_part
    gin_ref[0] = gin
    gout_ref[0] = gout


def weight_grads(place, xs, gs, w_in, w_out, ways, earlier):
    experts, model, hidden = w_in.shape
    cols = hidden // ways
    tile = GRAD_TILE if cols % GRAD_TILE == 0 else cols
    tiles = cols // tile

    def rows_of(array):
        sources, _, slots, _ = array.shape
        return pl.BlockSpec((sources, 1, slots, model), lambda e, t, q: (0, e, 0, 0))

    out_shape = [shape((experts, model, cols), f32), shape((experts, cols, model), f32)]
    out_specs = [
        pl.BlockSpec((1, model, tile), lambda e, t, q: (e, 0, t)),
        pl.BlockSpec((1, tile, model), lambda e, t, q: (e, t, 0)),
    ]
    flops = 16 * sum(math.prod(a.shape) for a in xs) * cols
    operands = [place, *xs, *gs, w_in, w_out]
    specs = [rows_of(a) for a in (*xs, *gs)] + [
        pl.BlockSpec((1, model, tile), lambda e, t, q: (e, 0, q[0] * tiles + t)),
        pl.BlockSpec((1, tile, model), lambda e, t, q: (e, q[0] * tiles + t, 0)),
    ]
    aliases = {}
    if earlier is not None:
        aliases = {len(operands): 0, len(operands) + 1: 1}
        operands += list(earlier)
        specs += out_specs
    return pl.pallas_call(
        functools.partial(weight_grad_kernel, len(xs)),
        grid_spec=pltpu.PrefetchScalarGridSpec(
            num_scalar_prefetch=1,
            grid=(experts, tiles),
            in_specs=specs,
            out_specs=out_specs,
        ),
        out_shape=out_shape,
        input_output_aliases=aliases,
        compiler_params=PARAMS,
        cost_estimate=cost(flops, *out_shape, *xs, *gs),
        name="weight_grads",
    )(*operands)


def partners(ways, step):
    return [(index, index ^ step) for index in range(ways)]


def swap(value, axis, step):
    return lax.ppermute(value, axis, partners(lax.axis_size(axis), step))


def gather_near(value):
    return swap(value, "seq", 1), swap(value, "seq", 2)


def gather_far(near, far):
    half = near.shape[0] // 2
    return swap(near[:half], "seq", 2), swap(far[half:], "seq", 1)


def sum_by_doubling(value, axis):
    step = 1
    while step < lax.axis_size(axis):
        value = value + swap(value, axis, step)
        step *= 2
    return value


def add_low(a, b):
    return (a.astype(f32) + b.astype(f32)).astype(bf16)


def scatter_rows(value):
    ways = lax.axis_size("shard")
    rows, cols = value.shape
    parts = lax.all_to_all(value.reshape(ways, rows // ways, cols), "shard", 0, 0, tiled=True)
    return jnp.sum(parts.astype(f32), axis=0)


def body(
    block_input,
    gain_attn,
    gain_ffn,
    w_qkv,
    w_out,
    w_router,
    rel_bias,
    w_in,
    w_exp_out,
    expert_id,
    capacity_slot,
    buckets,
    output_grad,
):
    seqs, piece, model = block_input.shape
    seq_ways = lax.axis_size("seq")
    shard_ways = lax.axis_size("shard")
    bucket_count, heads_all = rel_bias.shape
    heads = heads_all // seq_ways
    width = model // seq_ways
    length = piece * seq_ways
    experts = w_router.shape[1]
    tokens = seqs * piece
    capacity = 2 * tokens // experts
    positions = experts * capacity
    slot_shape = (shard_ways, experts // shard_ways, capacity, model)
    weight_rows = w_qkv.shape[0]
    seq_index = lax.axis_index("seq").astype(jnp.int32)
    places = jnp.stack([seq_index ^ step for step in range(seq_ways)])
    gain_one_row = gain_attn.reshape(1, model)
    gain_two_row = gain_ffn.reshape(1, model)
    bucket_row = jnp.pad(
        buckets, (0, 2 * length - buckets.shape[0]), constant_values=-1
    ).reshape(1, 2 * length)
    target = jnp.where(capacity_slot < capacity, expert_id * capacity + capacity_slot, -1)
    target_row = target.reshape(1, tokens)
    target_column = target.reshape(tokens, 1)
    by_chunks = shard_ways <= 8 and weight_rows % 16 == 0
    shard_index = lax.axis_index("shard").astype(jnp.int32)
    order = jnp.stack([shard_index ^ step for step in range(shard_ways)])
    id_column = expert_id.reshape(tokens, 1)
    upstream = output_grad.reshape(tokens, model)

    own_columns = lax.dynamic_slice_in_dim(
        w_qkv.reshape(weight_rows, 3, model), seq_index * width, width, 2
    ).reshape(weight_rows, 3 * width)
    own_columns = jnp.pad(own_columns, ((0, 0), (0, max(0, model - 3 * width))))
    head_weight = lax.all_gather(own_columns, "shard", axis=0, tiled=True)
    inputs = block_input.astype(f32)
    normed = (inputs * inverse_norm(inputs) * gain_attn).astype(bf16)
    tiles = bias_tiles(
        lax.dynamic_slice_in_dim(rel_bias, seq_index * heads, heads, 1), bucket_row
    )

    first_near = gather_near(normed[0])
    held = lax.optimization_barrier((normed[1], first_near))
    first_near = held[1]
    second_near = gather_near(held[0])
    first_far = gather_far(*first_near)
    dense_rows, head_weight, first_far, second_near, tiles = lax.optimization_barrier(
        (jnp.concatenate([w_out, w_router], axis=1), head_weight, first_far, second_near, tiles)
    )
    second_far = gather_far(*second_near)
    dense = lax.all_gather(dense_rows, "shard", axis=0, tiled=True)
    sequence_pieces = (
        (normed[0], *first_near, *first_far),
        (normed[1], *second_near, *second_far),
    )
    kept, attended_tok = [], []
    for pieces in sequence_pieces:
        rows, qkv, attended, probs = attend(places, pieces, head_weight, tiles)
        kept.append((rows, qkv, probs))
        attended_tok.append(lax.all_to_all(attended, "seq", 0, 0, tiled=True))

    middle, second, sent = project(
        block_input.reshape(tokens, model), target_row, gain_two_row, dense, attended_tok, positions
    )
    attended_flat, router_probs, sent_grad = route(
        second, upstream, id_column, target_row, dense, attended_tok, positions
    )

    def exchange(rows):
        return lax.all_to_all(rows, "shard", 0, 0, tiled=True)

    held_weight, sent = lax.optimization_barrier((head_weight[:, : 3 * width], sent))
    weight_groups = lax.all_gather(held_weight, "seq")
    arrived = exchange(sent.reshape(slot_shape))
    arrived, sent_grad = lax.optimization_barrier((arrived, sent_grad))
    arrived_near = gather_near(arrived)
    out_arrived = exchange(sent_grad.reshape(slot_shape))
    expert_out, slope = expert_forward(arrived, w_in, w_exp_out, FORWARD_TILE)
    expert_out, out_arrived, weight_groups, arrived_near = lax.optimization_barrier(
        (expert_out, out_arrived, weight_groups, arrived_near)
    )
    back_out = exchange(expert_out).reshape(positions, model)
    out_near = gather_near(out_arrived)

    def expert_grads(xs, gs, earlier):
        return weight_grads(places, xs, gs, w_in, w_exp_out, seq_ways, earlier)

    rows_grad = expert_backward(out_arrived, w_in, w_exp_out, slope, FORWARD_TILE)
    expert_part = expert_grads((arrived,), (out_arrived,), None)
    rows_grad, back_out, expert_part = lax.optimization_barrier((rows_grad, back_out, expert_part))
    back_grad = exchange(rows_grad).reshape(positions, model)
    block_output, logit_low, grad_router = returned(
        (back_out,), target_column, id_column, middle, upstream, router_probs, second
    )
    expert_part = expert_grads(arrived_near, out_near, expert_part)
    arrived_near, out_near = lax.optimization_barrier((arrived_near, out_near))
    out_far = gather_far(*out_near)
    arrived_far = gather_far(*arrived_near)
    back_grad, logit_low, expert_part, out_far, arrived_far = lax.optimization_barrier(
        (back_grad, logit_low, expert_part, out_far, arrived_far)
    )
    middle_grads, branches, grad_heads, gain_two = [], [], [], []
    for number in range(seqs):
        middle_grad, branch, attended_grad, gain_part = branch_back(
            back_grad, target_column, logit_low, dense, middle, gain_two_row, upstream,
            number, seqs, seq_ways,
        )
        middle_grads.append(middle_grad)
        branches.append(branch)
        gain_two.append(gain_part)
        grad_heads.append(lax.all_to_all(attended_grad, "seq", 0, 0, tiled=True))
    grad_out = sum(
        tn(attended_flat[number * piece : (number + 1) * piece], branches[number])
        for number in range(seqs)
    )
    grad_dense = jnp.concatenate([grad_out.astype(bf16), grad_router], axis=1)
    grad_dense = lax.psum_scatter(grad_dense, "shard", scatter_dimension=0, tiled=True)
    grad_dense = grad_dense.astype(f32)
    for step in (1, 2):
        grad_dense = grad_dense + swap(grad_dense, "seq", step)

    qkv_grads, bias_parts, grad_tok = [], [], []
    for number in range(seqs):
        _, qkv, probs = kept[number]
        grad = grad_heads[number]
        qkv_grad, bias_part = attend_back(qkv, probs, grad, bucket_row, bucket_count)
        qkv_grads.append(qkv_grad)
        bias_parts.append(bias_part)
        grad_tok.append(lax.all_to_all(qkv_grad, "seq", 0, 0, tiled=True))
    input_grad, first_gain = input_back(
        grad_tok[0], weight_groups, block_input, gain_one_row, middle_grads[0], 0, None
    )
    gain_one = [first_gain]
    rows_all = [each[0] for each in kept]
    if by_chunks:
        columns, other = column_grads(order, rows_all, qkv_grads, shard_ways)
        columns = add_low(columns, swap(other, "shard", 1))
        last = other
        columns, input_grad = lax.optimization_barrier((columns, input_grad))
        step = shard_ways // 2
        if step > 1:
            half = columns.shape[0] // 2
            columns = add_low(columns[:half], swap(columns[half:], "shard", step))
            step //= 2
    else:
        (last,) = column_grads(places - places, rows_all, qkv_grads, 1)
        columns = last
    out_far = lax.optimization_barrier((out_far, last))[0]
    expert_part = expert_grads(arrived_far, out_far, expert_part)
    grad_in_part, grad_exp_part, columns = lax.optimization_barrier((*expert_part, columns))
    grad_tok[-1], input_grad, _ = lax.optimization_barrier((grad_tok[-1], input_grad, last))
    for number in range(1, seqs):
        input_grad, gain_part = input_back(
            grad_tok[number], weight_groups, block_input, gain_one_row,
            middle_grads[number], number, input_grad,
        )
        gain_one.append(gain_part)
    bias_grad = lax.dynamic_update_slice_in_dim(
        jnp.zeros((bucket_count, heads_all), f32),
        functools.reduce(jnp.add, bias_parts)[:, :heads],
        seq_index * heads,
        1,
    )
    small = jnp.concatenate(
        [bias_grad.reshape(-1), sum(gain_two).reshape(-1), sum(gain_one).reshape(-1)]
    ).reshape(-1, LANES)
    if by_chunks:
        while step > 1:
            half = columns.shape[0] // 2
            columns = add_low(columns[:half], swap(columns[half:], "shard", step))
            step //= 2
        columns = columns[0]
    else:
        columns = scatter_rows(columns).astype(bf16)
    grad_qkv = column_order(
        places, [columns] + [swap(columns, "seq", step) for step in range(1, seq_ways)]
    )
    small = sum_by_doubling(sum_by_doubling(small, "seq"), "shard").reshape(-1)
    bias_size = bucket_count * heads_all
    return (
        block_output.reshape(block_input.shape),
        input_grad,
        small[bias_size + model :],
        small[bias_size : bias_size + model],
        grad_qkv,
        grad_dense[:, :model],
        grad_dense[:, model:],
        small[:bias_size].reshape(bucket_count, heads_all),
        grad_in_part,
        grad_exp_part,
    )


def solution(mesh):
    placed = (
        P("shard", "seq", None),
        P(),
        P(),
        P("shard", None),
        P("shard", None),
        P("shard", None),
        P(),
        P("shard", None, None),
        P("shard", None, None),
        P("shard", "seq"),
        P("shard", "seq"),
        P(),
        P("shard", "seq", None),
    )
    return jax.shard_map(
        body,
        mesh=mesh,
        in_specs=placed,
        out_specs=(
            P("shard", "seq", None),
            P("shard", "seq", None),
            P(),
            P(),
            P("shard", None),
            P("shard", None),
            P("shard", None),
            P(),
            P("shard", None, "seq"),
            P("shard", "seq", None),
        ),
        check_vma=False,
    )
```

```python
import functools
import math

import jax
import jax.numpy as jnp
from jax import lax
from jax.experimental import pallas as pl
from jax.experimental.pallas import tpu as pltpu
from jax.sharding import PartitionSpec as P

f32 = jnp.float32
bf16 = jnp.bfloat16
LANES = 128
MIB = 1024 * 1024
BLOCK_ROWS = 256
FORWARD_TILE = 1024
GRAD_TILE = 768
norm_eps = 1e-06
ROOT_HALF = 1.0 / math.sqrt(2.0)
DENSITY = 1.0 / math.sqrt(2.0 * math.pi)
PARAMS = pltpu.CompilerParams(vmem_limit_bytes=52 * MIB)
SMEM = pl.BlockSpec(memory_space=pltpu.SMEM)


def nn(a, b):
    return jnp.dot(a, b, preferred_element_type=f32)


def nt(a, b):
    return lax.dot_general(a, b, (((1,), (1,)), ((), ())), preferred_element_type=f32)


def tn(a, b):
    return lax.dot_general(a, b, (((0,), (0,)), ((), ())), preferred_element_type=f32)


def whole(array):
    zeros = (0,) * array.ndim
    return pl.BlockSpec(array.shape, lambda *_: zeros)


def cost(flops, *arrays):
    return pl.CostEstimate(
        flops=int(flops),
        bytes_accessed=int(sum(math.prod(a.shape) * a.dtype.itemsize for a in arrays)),
        transcendentals=0,
    )


def shape(dims, kind):
    return jax.ShapeDtypeStruct(dims, kind)


def pack_rows(values):
    half = values.shape[0] // 2
    return jnp.concatenate([values[:half], values[half:]], axis=1)


def unpack_rows(packed):
    width = packed.shape[1] // 2
    return jnp.concatenate([packed[:, :width], packed[:, width:]], axis=0)


def inverse_norm(values):
    return lax.rsqrt(jnp.mean(values * values, axis=-1, keepdims=True) + norm_eps)


def norm_backward(values, gain, upstream):
    inverse = inverse_norm(values)
    scaled = upstream * gain
    inner = jnp.mean(scaled * values, axis=-1, keepdims=True)
    result = inverse * scaled - values * (inverse * inverse * inverse * inner)
    return result, jnp.sum(upstream * values * inverse, axis=0, keepdims=True)


def gelu_and_slope(v):
    cumulative = 0.5 * (1.0 + lax.erf(v * ROOT_HALF))
    return v * cumulative, cumulative + v * (jnp.exp(-0.5 * v * v) * DENSITY)


def bias_kernel(rel_ref, bucket_ref, out_ref):
    span = bucket_ref.shape[1]
    bucket_row = bucket_ref[...]
    for head in range(out_ref.shape[0]):
        row = jnp.zeros((1, span), f32)
        for bucket in range(rel_ref.shape[0]):
            row = jnp.where(bucket_row == bucket, rel_ref[bucket, head], row)
        out_ref[head] = pltpu.roll(
            jnp.broadcast_to(row, (LANES, span)), span - LANES + 1, 1, stride=1, stride_axis=0
        )


def bias_tiles(rel, bucket_row):
    out_shape = shape((rel.shape[1], LANES, bucket_row.shape[1]), f32)
    return pl.pallas_call(
        bias_kernel,
        in_specs=[SMEM, whole(bucket_row)],
        out_specs=whole(out_shape),
        out_shape=out_shape,
        compiler_params=PARAMS,
        cost_estimate=cost(0, out_shape),
        name="bias_tiles",
    )(rel, bucket_row)


def attend_kernel(
    place_ref, own_ref, near_ref, far_ref, low_ref, high_ref, w_ref, toeplitz_ref,
    rows_ref, qkv_ref, att_ref, prob_ref, split, outs,
):
    head = pl.program_id(0)
    heads, length, head_dim = outs.shape
    width = heads * head_dim
    piece = own_ref.shape[0]

    @pl.when(head == 0)
    def _():
        for number, ref in enumerate((own_ref, near_ref, far_ref)):
            at = pl.multiple_of(place_ref[number] * piece, piece)
            rows_ref[pl.ds(at, piece), :] = ref[...]
        at = pl.multiple_of(place_ref[3] * piece, piece)
        half = piece // 2
        rows_ref[pl.ds(at, half), :] = low_ref[...]
        rows_ref[pl.ds(pl.multiple_of(at + half, half), half), :] = high_ref[...]
        qkv = nn(rows_ref[...], w_ref[:, : 3 * width]).astype(bf16)
        qkv_ref[...] = qkv
        for part in range(3):
            for each in range(heads):
                at = part * width + each * head_dim
                split[part, each] = qkv[:, at : at + head_dim]

    keys = split[1, head]
    turned = split[2, head].T
    for start in range(0, length, BLOCK_ROWS):
        scores = nt(split[0, head, start : start + BLOCK_ROWS], keys)
        parts = []
        for sub in range(0, BLOCK_ROWS, LANES):
            off = length - LANES - start - sub
            parts.append(scores[sub : sub + LANES] + toeplitz_ref[0, :, off : off + length])
        scores = jnp.concatenate(parts, axis=0)
        peak = jnp.max(scores, axis=-1, keepdims=True)
        grown = jnp.exp(scores - peak)
        total = jnp.sum(grown, axis=-1, keepdims=True)
        prob_ref[0, start : start + BLOCK_ROWS, :] = (grown * (1.0 / total)).astype(bf16)
    outs[head] = nt(turned, prob_ref[0]).T

    @pl.when(head == heads - 1)
    def _():
        joined = jnp.concatenate([outs[each].astype(bf16) for each in range(heads)], axis=1)
        for number in range(length // piece):
            att_ref[number] = pack_rows(joined[number * piece : (number + 1) * piece])


def attend(place, pieces, weight, tiles):
    own, near, far, low, high = pieces
    piece, model = own.shape
    heads, _, span = tiles.shape
    length = span // 2
    cols = 3 * (model // (length // piece))
    width = cols // 3
    head_dim = width // heads
    out_shape = [
        shape((length, model), bf16),
        shape((length, cols), bf16),
        shape((length // piece, piece // 2, 2 * width), bf16),
        shape((heads, length, length), bf16),
    ]
    return pl.pallas_call(
        attend_kernel,
        grid=(heads,),
        in_specs=[SMEM]
        + [whole(a) for a in (own, near, far, low, high, weight)]
        + [pl.BlockSpec((1, LANES, span), lambda h: (h, 0, 0))],
        out_specs=[whole(a) for a in out_shape[:3]]
        + [pl.BlockSpec((1, length, length), lambda h: (h, 0, 0))],
        out_shape=out_shape,
        scratch_shapes=[
            pltpu.VMEM((3, heads, length, head_dim), bf16),
            pltpu.VMEM((heads, length, head_dim), f32),
        ],
        compiler_params=PARAMS,
        cost_estimate=cost(2 * length * model * cols + 16 * heads * length * length * head_dim, *out_shape),
        name="attend",
    )(place, own, near, far, low, high, weight, tiles)


def attend_back_kernel(
    qkv_ref, prob_ref, grad_ref, bucket_ref, out_ref, bias_ref, split, outs, acc, score_grads
):
    head = pl.program_id(0)
    heads, length, head_dim = outs.shape[1:]
    width = heads * head_dim
    span = 2 * length
    pieces, half, _ = grad_ref.shape
    piece = 2 * half

    @pl.when(head == 0)
    def _():
        bias_ref[...] = jnp.zeros_like(bias_ref)
        for part in range(3):
            for each in range(heads):
                at = part * width + each * head_dim
                split[part, each] = qkv_ref[:, at : at + head_dim]
        for number in range(pieces):
            grad = unpack_rows(grad_ref[number])
            for each in range(heads):
                split[3, each, number * piece : (number + 1) * piece, :] = grad[
                    :, each * head_dim : (each + 1) * head_dim
                ]

    acc[...] = jnp.zeros_like(acc)
    values = split[2, head]
    for start in range(0, length, BLOCK_ROWS):
        prob_grad = nt(split[3, head, start : start + BLOCK_ROWS], values)
        prob = prob_ref[0, start : start + BLOCK_ROWS, :].astype(f32)
        weighted = prob * prob_grad
        inner = jnp.sum(weighted, axis=-1, keepdims=True)
        score_grad = weighted - prob * inner
        score_grads[start : start + BLOCK_ROWS, :] = score_grad.astype(bf16)
        for sub in range(0, BLOCK_ROWS, LANES):
            off = length - LANES - start - sub
            acc[:, off : off + length] += score_grad[sub : sub + LANES]
    outs[0, head] = nn(score_grads[...], split[1, head])
    outs[1, head] = tn(split[0, head], score_grads[...]).T
    outs[2, head] = tn(split[3, head], prob_ref[0]).T

    part = acc[...]
    rows = LANES
    while rows > 8:
        rows //= 2
        part = part[:rows] + pltpu.roll(part[rows:], span - rows, 1)
    offsets = part[0:1]
    for row in range(1, 8):
        offsets = offsets + pltpu.roll(part[row : row + 1], span - row, 1)
    offsets = pltpu.roll(offsets, LANES - 1, 1)
    hot = lax.broadcasted_iota(jnp.int32, (bias_ref.shape[0], span), 0) == bucket_ref[...]
    total = jnp.sum(jnp.where(hot, offsets, 0.0), axis=1, keepdims=True)
    lane = lax.broadcasted_iota(jnp.int32, bias_ref.shape, 1)
    bias_ref[...] = jnp.where(lane == head, total, bias_ref[...])

    @pl.when(head == heads - 1)
    def _():
        joined = jnp.concatenate(
            [outs[part, each].astype(bf16) for part in range(3) for each in range(heads)], axis=1
        )
        for number in range(pieces):
            out_ref[number] = pack_rows(joined[number * piece : (number + 1) * piece])


def attend_back(qkv, prob, grad, bucket_row, bucket_count):
    length, cols = qkv.shape
    heads = prob.shape[0]
    head_dim = cols // (3 * heads)
    pieces, half, _ = grad.shape
    out_shape = [shape((pieces, half, 2 * cols), bf16), shape((bucket_count, LANES), f32)]
    return pl.pallas_call(
        attend_back_kernel,
        grid=(heads,),
        in_specs=[
            whole(qkv),
            pl.BlockSpec((1, length, length), lambda h: (h, 0, 0)),
            whole(grad),
            whole(bucket_row),
        ],
        out_specs=[whole(a) for a in out_shape],
        out_shape=out_shape,
        scratch_shapes=[
            pltpu.VMEM((4, heads, length, head_dim), bf16),
            pltpu.VMEM((3, heads, length, head_dim), f32),
            pltpu.VMEM((LANES, 2 * length), f32),
            pltpu.VMEM((length, length), bf16),
        ],
        compiler_params=PARAMS,
        cost_estimate=cost(40 * heads * length * length * head_dim, qkv, prob, grad),
        name="attend_back",
    )(qkv, prob, grad, bucket_row)


def project_kernel(x_ref, target_ref, gain_ref, dense_ref, *refs):
    att_refs, (middle_ref, second_ref, sent_ref) = refs[:-3], refs[-3:]
    model = x_ref.shape[1]
    flats = []
    for ref in att_refs:
        flats.append(
            jnp.concatenate([unpack_rows(ref[g]) for g in range(ref.shape[0])], axis=1)
        )
    flat = jnp.concatenate(flats, axis=0)
    middle = x_ref[...].astype(f32) + nn(flat, dense_ref[:, :model])
    middle_ref[...] = middle
    second = (middle * inverse_norm(middle) * gain_ref[...]).astype(bf16)
    second_ref[...] = second
    positions = sent_ref.shape[0]
    hot = (
        lax.broadcasted_iota(jnp.int32, (positions, x_ref.shape[0]), 0) == target_ref[...]
    ).astype(bf16)
    sent_ref[...] = nn(hot, second).astype(bf16)


def project(x, target_row, gain, dense, attended, positions):
    tokens, model = x.shape
    out_shape = [
        shape((tokens, model), f32),
        shape((tokens, model), bf16),
        shape((positions, model), bf16),
    ]
    operands = (x, target_row, gain, dense, *attended)
    return pl.pallas_call(
        project_kernel,
        in_specs=[whole(a) for a in operands],
        out_specs=[whole(a) for a in out_shape],
        out_shape=out_shape,
        compiler_params=PARAMS,
        cost_estimate=cost(2 * tokens * model * (model + positions), *out_shape),
        name="project",
    )(*operands)


def route_kernel(
    second_ref, dy_ref, id_ref, target_ref, dense_ref, *refs
):
    att_refs, (flat_ref, prob_ref, grad_ref) = refs[:-3], refs[-3:]
    tokens, model = dy_ref.shape
    flats = []
    for ref in att_refs:
        flats.append(
            jnp.concatenate([unpack_rows(ref[g]) for g in range(ref.shape[0])], axis=1)
        )
    flat_ref[...] = jnp.concatenate(flats, axis=0)
    logits = nn(second_ref[...], dense_ref[:, model:])
    peak = jnp.max(logits, axis=-1, keepdims=True)
    grown = jnp.exp(logits - peak)
    probs = grown / jnp.sum(grown, axis=-1, keepdims=True)
    prob_ref[...] = probs
    chosen = lax.broadcasted_iota(jnp.int32, probs.shape, 1) == id_ref[...]
    gate = jnp.sum(jnp.where(chosen, probs, 0.0), axis=-1, keepdims=True)
    out_grad = (gate * dy_ref[...].astype(f32)).astype(bf16)
    hot = (
        lax.broadcasted_iota(jnp.int32, (grad_ref.shape[0], tokens), 0) == target_ref[...]
    ).astype(bf16)
    grad_ref[...] = nn(hot, out_grad).astype(bf16)


def route(second, dy, id_column, target_row, dense, attended, positions):
    tokens, model = dy.shape
    out_shape = [
        shape((tokens, model), bf16),
        shape((tokens, dense.shape[1] - model), f32),
        shape((positions, model), bf16),
    ]
    operands = (second, dy, id_column, target_row, dense, *attended)
    return pl.pallas_call(
        route_kernel,
        in_specs=[whole(a) for a in operands],
        out_specs=[whole(a) for a in out_shape],
        out_shape=out_shape,
        compiler_params=PARAMS,
        cost_estimate=cost(2 * tokens * model * positions, *out_shape),
        name="route",
    )(*operands)


def returned_kernel(target_ref, id_ref, middle_ref, dy_ref, prob_ref, second_ref, *refs):
    back_refs, (out_ref, logit_ref, router_ref) = refs[:-3], refs[-3:]
    tokens, model = middle_ref.shape
    back = jnp.concatenate([ref[...].reshape(-1, model) for ref in back_refs], axis=0)
    hot = (
        lax.broadcasted_iota(jnp.int32, (tokens, back.shape[0]), 1) == target_ref[...]
    ).astype(bf16)
    token_out = nn(hot, back)
    probs = prob_ref[...]
    chosen = lax.broadcasted_iota(jnp.int32, probs.shape, 1) == id_ref[...]
    gate = jnp.sum(jnp.where(chosen, probs, 0.0), axis=-1, keepdims=True)
    out_ref[...] = (middle_ref[...] + gate * token_out).astype(bf16)
    gate_grad = jnp.sum(dy_ref[...].astype(f32) * token_out, axis=-1, keepdims=True)
    picked = jnp.where(chosen, gate_grad, 0.0)
    logit_grad = probs * (picked - jnp.sum(probs * picked, axis=-1, keepdims=True))
    logit_low = logit_grad.astype(bf16)
    logit_ref[...] = logit_low
    router_ref[...] = tn(second_ref[...], logit_low).astype(bf16)


def returned(back, target_column, id_column, middle, dy, probs, second):
    tokens, model = middle.shape
    experts = probs.shape[1]
    out_shape = [
        shape((tokens, model), bf16),
        shape((tokens, experts), bf16),
        shape((model, experts), bf16),
    ]
    operands = (target_column, id_column, middle, dy, probs, second, *back)
    return pl.pallas_call(
        returned_kernel,
        in_specs=[whole(a) for a in operands],
        out_specs=[whole(a) for a in out_shape],
        out_shape=out_shape,
        compiler_params=PARAMS,
        cost_estimate=cost(4 * tokens * tokens * model, *out_shape, middle, *back),
        name="returned",
    )(*operands)


def branch_kernel(
    back_ref, target_ref, logit_ref, dense_ref, middle_ref, gain_ref, dy_ref,
    middle_grad_ref, branch_ref, grad_ref, gain_grad_ref,
):
    tokens, model = middle_ref.shape
    hot = (
        lax.broadcasted_iota(jnp.int32, (tokens, back_ref.shape[0]), 1) == target_ref[...]
    ).astype(bf16)
    second_grad = nn(hot, back_ref[...]) + nt(logit_ref[...], dense_ref[:, model:])
    norm_grad, gain_grad = norm_backward(middle_ref[...], gain_ref[...], second_grad)
    gain_grad_ref[...] = gain_grad
    middle_grad = dy_ref[...].astype(f32) + norm_grad
    middle_grad_ref[...] = middle_grad
    branch = middle_grad.astype(bf16)
    branch_ref[...] = branch
    grad = nt(branch, dense_ref[:, :model]).astype(bf16)
    groups = grad_ref.shape[0]
    width = model // groups
    for group in range(groups):
        grad_ref[group] = pack_rows(grad[:, group * width : (group + 1) * width])


def branch_back(back, target_column, logit, dense, middle, gain, dy, number, seqs, groups):
    tokens, model = middle.shape
    piece = tokens // seqs

    def rows_of(array):
        return pl.BlockSpec((piece, array.shape[1]), lambda _: (number, 0))

    out_shape = [
        shape((piece, model), f32),
        shape((piece, model), bf16),
        shape((groups, piece // 2, 2 * model // groups), bf16),
        shape((1, model), f32),
    ]
    return pl.pallas_call(
        branch_kernel,
        grid=(1,),
        in_specs=[
            whole(back), rows_of(target_column), rows_of(logit), whole(dense), rows_of(middle),
            whole(gain), rows_of(dy),
        ],
        out_specs=[whole(a) for a in out_shape],
        out_shape=out_shape,
        compiler_params=PARAMS,
        cost_estimate=cost(6 * piece * model * model, *out_shape, back, dense),
        name="branch_back",
    )(back, target_column, logit, dense, middle, gain, dy)


def dense_kernel(flat_ref, router_ref, *refs):
    out_ref = refs[-1]
    branch = jnp.concatenate([ref[...] for ref in refs[:-1]], axis=0)
    model = branch.shape[1]
    out_ref[:, :model] = tn(flat_ref[...], branch).astype(bf16)
    out_ref[:, model:] = router_ref[...]


def dense_grads(flat, branches, router):
    model, experts = router.shape
    out_shape = shape((model, model + experts), bf16)
    return pl.pallas_call(
        dense_kernel,
        in_specs=[whole(a) for a in (flat, router, *branches)],
        out_specs=whole(out_shape),
        out_shape=out_shape,
        compiler_params=PARAMS,
        cost_estimate=cost(2 * math.prod(flat.shape) * model, flat, router, *branches),
        name="dense_grads",
    )(flat, router, *branches)


def input_kernel(grad_ref, weight_ref, x_ref, gain_ref, middle_grad_ref, *refs):
    out_ref, gain_grad_ref = refs[-2:]
    total = None
    for group in range(weight_ref.shape[0]):
        part = nt(unpack_rows(grad_ref[group]), weight_ref[group])
        total = part if total is None else total + part
    norm_grad, gain_grad = norm_backward(x_ref[0].astype(f32), gain_ref[...], total)
    out_ref[0] = middle_grad_ref[...] + norm_grad
    gain_grad_ref[...] = gain_grad


def input_back(grad, weights, x, gain, middle_grad, number, earlier):
    seqs, piece, model = x.shape
    row_spec = pl.BlockSpec((1, piece, model), lambda _: (number, 0, 0))
    out_shape = [shape(x.shape, f32), shape((1, model), f32)]
    operands = [grad, weights, x, gain, middle_grad]
    specs = [whole(grad), whole(weights), row_spec, whole(gain), whole(middle_grad)]
    aliases = {}
    if earlier is not None:
        aliases = {len(operands): 0}
        operands.append(earlier)
        specs.append(pl.BlockSpec(memory_space=pl.ANY))
    return pl.pallas_call(
        input_kernel,
        grid=(1,),
        in_specs=specs,
        out_specs=[row_spec, whole(out_shape[1])],
        out_shape=out_shape,
        input_output_aliases=aliases,
        compiler_params=PARAMS,
        cost_estimate=cost(2 * piece * math.prod(weights.shape), grad, weights, middle_grad),
        name="input_back",
    )(*operands)


def column_kernel(seqs, place_ref, *refs):
    row_refs, grad_refs, out_refs = refs[:seqs], refs[seqs : 2 * seqs], refs[2 * seqs : -1]
    total = refs[-1]
    value = None
    for row_ref, grad_ref in zip(row_refs, grad_refs):
        grad = jnp.concatenate(
            [unpack_rows(grad_ref[piece]) for piece in range(grad_ref.shape[0])], axis=0
        )
        part = tn(row_ref[...], grad)
        value = part if value is None else value + part
    if len(out_refs) == 1:
        out_refs[0][...] = value.astype(bf16)
        return
    total[...] = value.astype(bf16)
    for number in range(2 * out_refs[0].shape[0]):
        ref = out_refs[number % 2]
        rows = ref.shape[1]
        at = pl.multiple_of(place_ref[number] * rows, rows)
        ref[number // 2] = total[pl.ds(at, rows), :]


def column_grads(places, rows, grads, chunks):
    model = rows[0].shape[1]
    cols = grads[0].shape[2] // 2
    if chunks > 1:
        out_shape = [shape((chunks // 2, model // chunks, cols), bf16)] * 2
    else:
        out_shape = [shape((model, cols), bf16)]
    return pl.pallas_call(
        functools.partial(column_kernel, len(rows)),
        in_specs=[SMEM] + [whole(a) for a in (*rows, *grads)],
        out_specs=[whole(a) for a in out_shape],
        out_shape=out_shape,
        scratch_shapes=[pltpu.VMEM((model, cols), bf16)],
        compiler_params=PARAMS,
        cost_estimate=cost(2 * sum(math.prod(r.shape) for r in rows) * cols, *rows, *grads),
        name="column_grads",
    )(places, *rows, *grads)


def column_order_kernel(place_ref, *refs):
    out_ref, held = refs[-2:]
    groups = held.shape[0]
    width = held.shape[2] // 3
    for number in range(groups):
        held[number] = refs[number][...].astype(f32)
    for part in range(3):
        joined = [
            held[place_ref[group], :, part * width : (part + 1) * width] for group in range(groups)
        ]
        out_ref[:, part * groups * width : (part + 1) * groups * width] = jnp.concatenate(
            joined, axis=1
        )


def column_order(places, pieces):
    rows, cols = pieces[0].shape
    out_shape = shape((rows, cols * len(pieces)), f32)
    return pl.pallas_call(
        column_order_kernel,
        in_specs=[SMEM] + [whole(a) for a in pieces],
        out_specs=whole(out_shape),
        out_shape=out_shape,
        scratch_shapes=[pltpu.VMEM((len(pieces), rows, cols), f32)],
        compiler_params=PARAMS,
        cost_estimate=cost(0, out_shape, *pieces),
        name="column_order",
    )(places, *pieces)


def expert_kernel(x_ref, win_ref, wout_ref, y_ref, slope_ref, acc):
    tile = pl.program_id(1)
    rows = acc.shape[0]
    x = x_ref[...].reshape(rows, x_ref.shape[-1])
    pre = jnp.dot(x, win_ref[0], preferred_element_type=f32)
    hidden, slope = gelu_and_slope(pre)
    slope_ref[0] = slope.astype(bf16)
    part = jnp.dot(hidden.astype(bf16), wout_ref[0], preferred_element_type=f32)

    @pl.when(tile == 0)
    def _():
        acc[...] = part

    @pl.when(tile > 0)
    def _():
        acc[...] += part

    @pl.when(tile == pl.num_programs(1) - 1)
    def _():
        y_ref[...] = acc[...].astype(bf16).reshape(y_ref.shape)


def expert_forward(x, w_in, w_out, tile):
    sources, experts, slots, model = x.shape
    hidden = w_in.shape[2]
    rows = sources * slots
    row_spec = pl.BlockSpec((sources, 1, slots, model), lambda e, f: (0, e, 0, 0))
    return pl.pallas_call(
        expert_kernel,
        grid=(experts, hidden // tile),
        in_specs=[
            row_spec,
            pl.BlockSpec((1, model, tile), lambda e, f: (e, 0, f)),
            pl.BlockSpec((1, tile, model), lambda e, f: (e, f, 0)),
        ],
        out_specs=[row_spec, pl.BlockSpec((1, rows, tile), lambda e, f: (e, 0, f))],
        out_shape=[
            jax.ShapeDtypeStruct(x.shape, bf16),
            jax.ShapeDtypeStruct((experts, rows, hidden), bf16),
        ],
        scratch_shapes=[pltpu.VMEM((rows, model), f32)],
        compiler_params=pltpu.CompilerParams(vmem_limit_bytes=52 * MIB),
        name="expert_forward",
    )(x, w_in, w_out)


def expert_back_kernel(g_ref, win_ref, wout_ref, slope_ref, y_ref, acc):
    tile = pl.program_id(1)
    rows = acc.shape[0]
    g = g_ref[...].reshape(rows, g_ref.shape[-1])
    pre_grad = (nt(g, wout_ref[0]) * slope_ref[0].astype(f32)).astype(bf16)
    part = nt(pre_grad, win_ref[0])

    @pl.when(tile == 0)
    def _():
        acc[...] = part

    @pl.when(tile > 0)
    def _():
        acc[...] += part

    @pl.when(tile == pl.num_programs(1) - 1)
    def _():
        y_ref[...] = acc[...].astype(bf16).reshape(y_ref.shape)


def expert_backward(g, w_in, w_out, slope, tile):
    sources, experts, slots, model = g.shape
    hidden = w_in.shape[2]
    rows = sources * slots
    row_spec = pl.BlockSpec((sources, 1, slots, model), lambda e, f: (0, e, 0, 0))
    return pl.pallas_call(
        expert_back_kernel,
        grid=(experts, hidden // tile),
        in_specs=[
            row_spec,
            pl.BlockSpec((1, model, tile), lambda e, f: (e, 0, f)),
            pl.BlockSpec((1, tile, model), lambda e, f: (e, f, 0)),
            pl.BlockSpec((1, rows, tile), lambda e, f: (e, 0, f)),
        ],
        out_specs=row_spec,
        out_shape=jax.ShapeDtypeStruct(g.shape, bf16),
        scratch_shapes=[pltpu.VMEM((rows, model), f32)],
        compiler_params=PARAMS,
        cost_estimate=cost(4 * experts * rows * model * hidden, g, w_in, w_out, slope),
        name="expert_backward",
    )(g, w_in, w_out, slope)


def weight_grad_kernel(pieces, place_ref, *refs):
    x_refs, g_refs = refs[:pieces], refs[pieces : 2 * pieces]
    win_ref, wout_ref = refs[2 * pieces : 2 * pieces + 2]
    earlier = refs[2 * pieces + 2 : -2]
    gin_ref, gout_ref = refs[-2:]
    gin, gout = (earlier[0][0], earlier[1][0]) if earlier else (None, None)
    for x_ref, g_ref in zip(x_refs, g_refs):
        rows = x_ref.shape[0] * x_ref.shape[2]
        x = x_ref[...].reshape(rows, x_ref.shape[-1])
        g = g_ref[...].reshape(rows, g_ref.shape[-1])
        hidden, slope = gelu_and_slope(nn(x, win_ref[0]))
        pre_grad = (nt(g, wout_ref[0]) * slope).astype(bf16)
        gin_part = tn(x, pre_grad)
        gout_part = tn(hidden.astype(bf16), g)
        gin = gin_part if gin is None else gin + gin_part
        gout = gout_part if gout is None else gout + gout_part
    gin_ref[0] = gin
    gout_ref[0] = gout


def weight_grads(place, xs, gs, w_in, w_out, ways, earlier):
    experts, model, hidden = w_in.shape
    cols = hidden // ways
    tile = GRAD_TILE if cols % GRAD_TILE == 0 else cols
    tiles = cols // tile

    def rows_of(array):
        sources, _, slots, _ = array.shape
        return pl.BlockSpec((sources, 1, slots, model), lambda e, t, q: (0, e, 0, 0))

    out_shape = [shape((experts, model, cols), f32), shape((experts, cols, model), f32)]
    out_specs = [
        pl.BlockSpec((1, model, tile), lambda e, t, q: (e, 0, t)),
        pl.BlockSpec((1, tile, model), lambda e, t, q: (e, t, 0)),
    ]
    flops = 16 * sum(math.prod(a.shape) for a in xs) * cols
    operands = [place, *xs, *gs, w_in, w_out]
    specs = [rows_of(a) for a in (*xs, *gs)] + [
        pl.BlockSpec((1, model, tile), lambda e, t, q: (e, 0, q[0] * tiles + t)),
        pl.BlockSpec((1, tile, model), lambda e, t, q: (e, q[0] * tiles + t, 0)),
    ]
    aliases = {}
    if earlier is not None:
        aliases = {len(operands): 0, len(operands) + 1: 1}
        operands += list(earlier)
        specs += out_specs
    return pl.pallas_call(
        functools.partial(weight_grad_kernel, len(xs)),
        grid_spec=pltpu.PrefetchScalarGridSpec(
            num_scalar_prefetch=1,
            grid=(experts, tiles),
            in_specs=specs,
            out_specs=out_specs,
        ),
        out_shape=out_shape,
        input_output_aliases=aliases,
        compiler_params=PARAMS,
        cost_estimate=cost(flops, *out_shape, *xs, *gs),
        name="weight_grads",
    )(*operands)


def partners(ways, step):
    return [(index, index ^ step) for index in range(ways)]


def swap(value, axis, step):
    return lax.ppermute(value, axis, partners(lax.axis_size(axis), step))


def gather_near(value):
    return swap(value, "seq", 1), swap(value, "seq", 2)


def gather_far(near, far):
    half = near.shape[0] // 2
    return swap(near[:half], "seq", 2), swap(far[half:], "seq", 1)


def sum_exchange(value, axis):
    copies = jnp.broadcast_to(value[None], (lax.axis_size(axis),) + value.shape)
    return jnp.sum(lax.all_to_all(copies, axis, 0, 0, tiled=True), axis=0)


def add_low(a, b):
    return (a.astype(f32) + b.astype(f32)).astype(bf16)


def scatter_rows(value):
    ways = lax.axis_size("shard")
    rows, cols = value.shape
    parts = lax.all_to_all(value.reshape(ways, rows // ways, cols), "shard", 0, 0, tiled=True)
    return jnp.sum(parts.astype(f32), axis=0)


def body(
    block_input,
    gain_attn,
    gain_ffn,
    w_qkv,
    w_out,
    w_router,
    rel_bias,
    w_in,
    w_exp_out,
    expert_id,
    capacity_slot,
    buckets,
    output_grad,
):
    seqs, piece, model = block_input.shape
    seq_ways = lax.axis_size("seq")
    shard_ways = lax.axis_size("shard")
    bucket_count, heads_all = rel_bias.shape
    heads = heads_all // seq_ways
    width = model // seq_ways
    length = piece * seq_ways
    experts = w_router.shape[1]
    tokens = seqs * piece
    capacity = 2 * tokens // experts
    positions = experts * capacity
    slot_shape = (shard_ways, experts // shard_ways, capacity, model)
    weight_rows = w_qkv.shape[0]
    seq_index = lax.axis_index("seq").astype(jnp.int32)
    places = jnp.stack([seq_index ^ step for step in range(seq_ways)])
    gain_one_row = gain_attn.reshape(1, model)
    gain_two_row = gain_ffn.reshape(1, model)
    bucket_row = jnp.pad(
        buckets, (0, 2 * length - buckets.shape[0]), constant_values=-1
    ).reshape(1, 2 * length)
    target = jnp.where(capacity_slot < capacity, expert_id * capacity + capacity_slot, -1)
    target_row = target.reshape(1, tokens)
    target_column = target.reshape(tokens, 1)
    by_chunks = shard_ways <= 8 and weight_rows % 16 == 0
    shard_index = lax.axis_index("shard").astype(jnp.int32)
    order = jnp.stack([shard_index ^ step for step in range(shard_ways)])
    id_column = expert_id.reshape(tokens, 1)
    upstream = output_grad.reshape(tokens, model)

    own_columns = lax.dynamic_slice_in_dim(
        w_qkv.reshape(weight_rows, 3, model), seq_index * width, width, 2
    ).reshape(weight_rows, 3 * width)
    own_columns = jnp.pad(own_columns, ((0, 0), (0, max(0, model - 3 * width))))
    head_weight = lax.all_gather(own_columns, "shard", axis=0, tiled=True)
    inputs = block_input.astype(f32)
    normed = (inputs * inverse_norm(inputs) * gain_attn).astype(bf16)
    tiles = bias_tiles(
        lax.dynamic_slice_in_dim(rel_bias, seq_index * heads, heads, 1), bucket_row
    )

    first_near = gather_near(normed[0])
    held = lax.optimization_barrier((normed[1], first_near))
    first_near = held[1]
    second_near = gather_near(held[0])
    first_far = gather_far(*first_near)
    dense_rows, head_weight, first_far, second_near, tiles = lax.optimization_barrier(
        (jnp.concatenate([w_out, w_router], axis=1), head_weight, first_far, second_near, tiles)
    )
    second_far = gather_far(*second_near)
    dense = lax.all_gather(dense_rows, "shard", axis=0, tiled=True)
    sequence_pieces = (
        (normed[0], *first_near, *first_far),
        (normed[1], *second_near, *second_far),
    )
    kept, attended_tok = [], []
    for pieces in sequence_pieces:
        rows, qkv, attended, probs = attend(places, pieces, head_weight, tiles)
        kept.append((rows, qkv, probs))
        attended_tok.append(lax.all_to_all(attended, "seq", 0, 0, tiled=True))

    middle, second, sent = project(
        block_input.reshape(tokens, model), target_row, gain_two_row, dense, attended_tok, positions
    )
    attended_flat, router_probs, sent_grad = route(
        second, upstream, id_column, target_row, dense, attended_tok, positions
    )

    def exchange(rows):
        return lax.all_to_all(rows, "shard", 0, 0, tiled=True)

    held_weight = lax.optimization_barrier((head_weight[:, : 3 * width], attended_tok[0]))[0]
    weight_groups = lax.all_gather(held_weight, "seq")
    arrived = exchange(sent.reshape(slot_shape))
    arrived, sent_grad = lax.optimization_barrier((arrived, sent_grad))
    arrived_near = gather_near(arrived)
    out_arrived = exchange(sent_grad.reshape(slot_shape))
    expert_out, slope = expert_forward(arrived, w_in, w_exp_out, FORWARD_TILE)
    expert_out, out_arrived, weight_groups, arrived_near = lax.optimization_barrier(
        (expert_out, out_arrived, weight_groups, arrived_near)
    )
    back_out = exchange(expert_out).reshape(positions, model)
    out_near = gather_near(out_arrived)

    def expert_grads(xs, gs, earlier):
        return weight_grads(places, xs, gs, w_in, w_exp_out, seq_ways, earlier)

    rows_grad = expert_backward(out_arrived, w_in, w_exp_out, slope, FORWARD_TILE)
    expert_part = expert_grads((arrived,), (out_arrived,), None)
    rows_grad, back_out, expert_part = lax.optimization_barrier((rows_grad, back_out, expert_part))
    back_grad = exchange(rows_grad).reshape(positions, model)
    block_output, logit_low, grad_router = returned(
        (back_out,), target_column, id_column, middle, upstream, router_probs, second
    )
    expert_part = expert_grads(arrived_near, out_near, expert_part)
    arrived_near, out_near = lax.optimization_barrier((arrived_near, out_near))
    out_far = gather_far(*out_near)
    arrived_far = gather_far(*arrived_near)
    back_grad, logit_low, expert_part = lax.optimization_barrier(
        (back_grad, logit_low, expert_part)
    )
    middle_grads, branches, grad_heads, gain_two = [], [], [], []
    for number in range(seqs):
        middle_grad, branch, attended_grad, gain_part = branch_back(
            back_grad, target_column, logit_low, dense, middle, gain_two_row, upstream,
            number, seqs, seq_ways,
        )
        middle_grads.append(middle_grad)
        branches.append(branch)
        gain_two.append(gain_part)
        grad_heads.append(lax.all_to_all(attended_grad, "seq", 0, 0, tiled=True))
    grad_dense = dense_grads(attended_flat, branches, grad_router)
    grad_heads[0], grad_dense, out_far, arrived_far = lax.optimization_barrier(
        (grad_heads[0], grad_dense, out_far, arrived_far)
    )
    grad_dense = lax.psum_scatter(grad_dense, "shard", scatter_dimension=0, tiled=True)

    qkv_grads, bias_parts, grad_tok = [], [], []
    for number in range(seqs):
        _, qkv, probs = kept[number]
        grad = grad_heads[number]
        qkv_grad, bias_part = attend_back(qkv, probs, grad, bucket_row, bucket_count)
        qkv_grads.append(qkv_grad)
        bias_parts.append(bias_part)
        grad_tok.append(lax.all_to_all(qkv_grad, "seq", 0, 0, tiled=True))
    input_grad, first_gain = input_back(
        grad_tok[0], weight_groups, block_input, gain_one_row, middle_grads[0], 0, None
    )
    gain_one = [first_gain]
    qkv_grads[-1], grad_dense = lax.optimization_barrier((qkv_grads[-1], grad_dense))
    rows_all = [each[0] for each in kept]
    if by_chunks:
        columns, other = column_grads(order, rows_all, qkv_grads, shard_ways)
        last = other
        columns = add_low(columns, swap(other, "shard", 1))
        step = shard_ways // 2
        if step > 1:
            half = columns.shape[0] // 2
            columns = add_low(columns[:half], swap(columns[half:], "shard", step))
            step //= 2
    else:
        (last,) = column_grads(places - places, rows_all, qkv_grads, 1)
        columns = last
    grad_tok[-1], input_grad, columns = lax.optimization_barrier(
        (grad_tok[-1], input_grad, columns)
    )
    for number in range(1, seqs):
        input_grad, gain_part = input_back(
            grad_tok[number], weight_groups, block_input, gain_one_row,
            middle_grads[number], number, input_grad,
        )
        gain_one.append(gain_part)
    out_far, grad_dense, _ = lax.optimization_barrier((out_far, grad_dense, gain_one[-1]))
    grad_dense = grad_dense.astype(f32) + swap(grad_dense, "seq", 1).astype(f32)
    grad_dense = grad_dense + swap(grad_dense, "seq", 2)
    grad_in_part, grad_exp_part = expert_grads(arrived_far, out_far, expert_part)
    bias_grad = lax.dynamic_update_slice_in_dim(
        jnp.zeros((bucket_count, heads_all), f32),
        functools.reduce(jnp.add, bias_parts)[:, :heads],
        seq_index * heads,
        1,
    )
    small = jnp.concatenate(
        [bias_grad.reshape(-1), sum(gain_two).reshape(-1), sum(gain_one).reshape(-1)]
    ).reshape(-1, LANES)
    if by_chunks:
        while step > 1:
            half = columns.shape[0] // 2
            columns = add_low(columns[:half], swap(columns[half:], "shard", step))
            step //= 2
        columns = columns[0]
    else:
        columns = scatter_rows(columns).astype(bf16)
    grad_qkv = column_order(
        places, [columns] + [swap(columns, "seq", step) for step in range(1, seq_ways)]
    )
    small = sum_exchange(sum_exchange(small, "seq"), "shard").reshape(-1)
    bias_size = bucket_count * heads_all
    return (
        block_output.reshape(block_input.shape),
        input_grad,
        small[bias_size + model :],
        small[bias_size : bias_size + model],
        grad_qkv,
        grad_dense[:, :model],
        grad_dense[:, model:],
        small[:bias_size].reshape(bucket_count, heads_all),
        grad_in_part,
        grad_exp_part,
    )


def solution(mesh):
    placed = (
        P("shard", "seq", None),
        P(),
        P(),
        P("shard", None),
        P("shard", None),
        P("shard", None),
        P(),
        P("shard", None, None),
        P("shard", None, None),
        P("shard", "seq"),
        P("shard", "seq"),
        P(),
        P("shard", "seq", None),
    )
    return jax.shard_map(
        body,
        mesh=mesh,
        in_specs=placed,
        out_specs=(
            P("shard", "seq", None),
            P("shard", "seq", None),
            P(),
            P(),
            P("shard", None),
            P("shard", None),
            P("shard", None),
            P(),
            P("shard", None, "seq"),
            P("shard", "seq", None),
        ),
        check_vma=False,
    )
```

```python
import functools
import math

import jax
import jax.numpy as jnp
from jax import lax
from jax.experimental import pallas as pl
from jax.experimental.pallas import tpu as pltpu
from jax.sharding import PartitionSpec as P

f32 = jnp.float32
bf16 = jnp.bfloat16
LANES = 128
MIB = 1024 * 1024
BLOCK_ROWS = 256
FORWARD_TILE = 1024
GRAD_TILE = 768
norm_eps = 1e-06
ROOT_HALF = 1.0 / math.sqrt(2.0)
DENSITY = 1.0 / math.sqrt(2.0 * math.pi)
PARAMS = pltpu.CompilerParams(vmem_limit_bytes=52 * MIB)
SMEM = pl.BlockSpec(memory_space=pltpu.SMEM)


def nn(a, b):
    return jnp.dot(a, b, preferred_element_type=f32)


def nt(a, b):
    return lax.dot_general(a, b, (((1,), (1,)), ((), ())), preferred_element_type=f32)


def tn(a, b):
    return lax.dot_general(a, b, (((0,), (0,)), ((), ())), preferred_element_type=f32)


def whole(array):
    zeros = (0,) * array.ndim
    return pl.BlockSpec(array.shape, lambda *_: zeros)


def cost(flops, *arrays):
    return pl.CostEstimate(
        flops=int(flops),
        bytes_accessed=int(sum(math.prod(a.shape) * a.dtype.itemsize for a in arrays)),
        transcendentals=0,
    )


def shape(dims, kind):
    return jax.ShapeDtypeStruct(dims, kind)


def pack_rows(values):
    half = values.shape[0] // 2
    return jnp.concatenate([values[:half], values[half:]], axis=1)


def unpack_rows(packed):
    width = packed.shape[1] // 2
    return jnp.concatenate([packed[:, :width], packed[:, width:]], axis=0)


def inverse_norm(values):
    return lax.rsqrt(jnp.mean(values * values, axis=-1, keepdims=True) + norm_eps)


def norm_backward(values, gain, upstream):
    inverse = inverse_norm(values)
    scaled = upstream * gain
    inner = jnp.mean(scaled * values, axis=-1, keepdims=True)
    result = inverse * scaled - values * (inverse * inverse * inverse * inner)
    return result, jnp.sum(upstream * values * inverse, axis=0, keepdims=True)


def gelu_and_slope(v):
    cumulative = 0.5 * (1.0 + lax.erf(v * ROOT_HALF))
    return v * cumulative, cumulative + v * (jnp.exp(-0.5 * v * v) * DENSITY)


def bias_kernel(rel_ref, bucket_ref, out_ref):
    span = bucket_ref.shape[1]
    bucket_row = bucket_ref[...]
    for head in range(out_ref.shape[0]):
        row = jnp.zeros((1, span), f32)
        for bucket in range(rel_ref.shape[0]):
            row = jnp.where(bucket_row == bucket, rel_ref[bucket, head], row)
        out_ref[head] = pltpu.roll(
            jnp.broadcast_to(row, (LANES, span)), span - LANES + 1, 1, stride=1, stride_axis=0
        )


def bias_tiles(rel, bucket_row):
    out_shape = shape((rel.shape[1], LANES, bucket_row.shape[1]), f32)
    return pl.pallas_call(
        bias_kernel,
        in_specs=[SMEM, whole(bucket_row)],
        out_specs=whole(out_shape),
        out_shape=out_shape,
        compiler_params=PARAMS,
        cost_estimate=cost(0, out_shape),
        name="bias_tiles",
    )(rel, bucket_row)


def attend_kernel(
    place_ref, own_ref, near_ref, far_ref, low_ref, high_ref, w_ref, toeplitz_ref,
    rows_ref, qkv_ref, att_ref, prob_ref, split, outs,
):
    head = pl.program_id(0)
    heads, length, head_dim = outs.shape
    width = heads * head_dim
    piece = own_ref.shape[0]

    @pl.when(head == 0)
    def _():
        for number, ref in enumerate((own_ref, near_ref, far_ref)):
            at = pl.multiple_of(place_ref[number] * piece, piece)
            rows_ref[pl.ds(at, piece), :] = ref[...]
        at = pl.multiple_of(place_ref[3] * piece, piece)
        half = piece // 2
        rows_ref[pl.ds(at, half), :] = low_ref[...]
        rows_ref[pl.ds(pl.multiple_of(at + half, half), half), :] = high_ref[...]
        qkv = nn(rows_ref[...], w_ref[:, : 3 * width]).astype(bf16)
        qkv_ref[...] = qkv
        for part in range(3):
            for each in range(heads):
                at = part * width + each * head_dim
                split[part, each] = qkv[:, at : at + head_dim]

    keys = split[1, head]
    turned = split[2, head].T
    for start in range(0, length, BLOCK_ROWS):
        scores = nt(split[0, head, start : start + BLOCK_ROWS], keys)
        parts = []
        for sub in range(0, BLOCK_ROWS, LANES):
            off = length - LANES - start - sub
            parts.append(scores[sub : sub + LANES] + toeplitz_ref[0, :, off : off + length])
        scores = jnp.concatenate(parts, axis=0)
        peak = jnp.max(scores, axis=-1, keepdims=True)
        grown = jnp.exp(scores - peak)
        total = jnp.sum(grown, axis=-1, keepdims=True)
        prob_ref[0, start : start + BLOCK_ROWS, :] = (grown * (1.0 / total)).astype(bf16)
    outs[head] = nt(turned, prob_ref[0]).T

    @pl.when(head == heads - 1)
    def _():
        joined = jnp.concatenate([outs[each].astype(bf16) for each in range(heads)], axis=1)
        for number in range(length // piece):
            att_ref[number] = pack_rows(joined[number * piece : (number + 1) * piece])


def attend(place, pieces, weight, tiles):
    own, near, far, low, high = pieces
    piece, model = own.shape
    heads, _, span = tiles.shape
    length = span // 2
    cols = 3 * (model // (length // piece))
    width = cols // 3
    head_dim = width // heads
    out_shape = [
        shape((length, model), bf16),
        shape((length, cols), bf16),
        shape((length // piece, piece // 2, 2 * width), bf16),
        shape((heads, length, length), bf16),
    ]
    return pl.pallas_call(
        attend_kernel,
        grid=(heads,),
        in_specs=[SMEM]
        + [whole(a) for a in (own, near, far, low, high, weight)]
        + [pl.BlockSpec((1, LANES, span), lambda h: (h, 0, 0))],
        out_specs=[whole(a) for a in out_shape[:3]]
        + [pl.BlockSpec((1, length, length), lambda h: (h, 0, 0))],
        out_shape=out_shape,
        scratch_shapes=[
            pltpu.VMEM((3, heads, length, head_dim), bf16),
            pltpu.VMEM((heads, length, head_dim), f32),
        ],
        compiler_params=PARAMS,
        cost_estimate=cost(2 * length * model * cols + 16 * heads * length * length * head_dim, *out_shape),
        name="attend",
    )(place, own, near, far, low, high, weight, tiles)


def attend_back_kernel(
    qkv_ref, prob_ref, grad_ref, bucket_ref, out_ref, bias_ref, split, outs, acc, score_grads
):
    head = pl.program_id(0)
    heads, length, head_dim = outs.shape[1:]
    width = heads * head_dim
    span = 2 * length
    pieces, half, _ = grad_ref.shape
    piece = 2 * half

    @pl.when(head == 0)
    def _():
        bias_ref[...] = jnp.zeros_like(bias_ref)
        for part in range(3):
            for each in range(heads):
                at = part * width + each * head_dim
                split[part, each] = qkv_ref[:, at : at + head_dim]
        for number in range(pieces):
            grad = unpack_rows(grad_ref[number])
            for each in range(heads):
                split[3, each, number * piece : (number + 1) * piece, :] = grad[
                    :, each * head_dim : (each + 1) * head_dim
                ]

    acc[...] = jnp.zeros_like(acc)
    values = split[2, head]
    for start in range(0, length, BLOCK_ROWS):
        prob_grad = nt(split[3, head, start : start + BLOCK_ROWS], values)
        prob = prob_ref[0, start : start + BLOCK_ROWS, :].astype(f32)
        weighted = prob * prob_grad
        inner = jnp.sum(weighted, axis=-1, keepdims=True)
        score_grad = weighted - prob * inner
        score_grads[start : start + BLOCK_ROWS, :] = score_grad.astype(bf16)
        for sub in range(0, BLOCK_ROWS, LANES):
            off = length - LANES - start - sub
            acc[:, off : off + length] += score_grad[sub : sub + LANES]
    outs[0, head] = nn(score_grads[...], split[1, head])
    outs[1, head] = tn(split[0, head], score_grads[...]).T
    outs[2, head] = tn(split[3, head], prob_ref[0]).T

    part = acc[...]
    rows = LANES
    while rows > 8:
        rows //= 2
        part = part[:rows] + pltpu.roll(part[rows:], span - rows, 1)
    offsets = part[0:1]
    for row in range(1, 8):
        offsets = offsets + pltpu.roll(part[row : row + 1], span - row, 1)
    offsets = pltpu.roll(offsets, LANES - 1, 1)
    hot = lax.broadcasted_iota(jnp.int32, (bias_ref.shape[0], span), 0) == bucket_ref[...]
    total = jnp.sum(jnp.where(hot, offsets, 0.0), axis=1, keepdims=True)
    lane = lax.broadcasted_iota(jnp.int32, bias_ref.shape, 1)
    bias_ref[...] = jnp.where(lane == head, total, bias_ref[...])

    @pl.when(head == heads - 1)
    def _():
        joined = jnp.concatenate(
            [outs[part, each].astype(bf16) for part in range(3) for each in range(heads)], axis=1
        )
        for number in range(pieces):
            out_ref[number] = pack_rows(joined[number * piece : (number + 1) * piece])


def attend_back(qkv, prob, grad, bucket_row, bucket_count):
    length, cols = qkv.shape
    heads = prob.shape[0]
    head_dim = cols // (3 * heads)
    pieces, half, _ = grad.shape
    out_shape = [shape((pieces, half, 2 * cols), bf16), shape((bucket_count, LANES), f32)]
    return pl.pallas_call(
        attend_back_kernel,
        grid=(heads,),
        in_specs=[
            whole(qkv),
            pl.BlockSpec((1, length, length), lambda h: (h, 0, 0)),
            whole(grad),
            whole(bucket_row),
        ],
        out_specs=[whole(a) for a in out_shape],
        out_shape=out_shape,
        scratch_shapes=[
            pltpu.VMEM((4, heads, length, head_dim), bf16),
            pltpu.VMEM((3, heads, length, head_dim), f32),
            pltpu.VMEM((LANES, 2 * length), f32),
            pltpu.VMEM((length, length), bf16),
        ],
        compiler_params=PARAMS,
        cost_estimate=cost(40 * heads * length * length * head_dim, qkv, prob, grad),
        name="attend_back",
    )(qkv, prob, grad, bucket_row)


def project_kernel(x_ref, target_ref, gain_ref, dense_ref, *refs):
    att_refs, (middle_ref, second_ref, sent_ref) = refs[:-3], refs[-3:]
    model = x_ref.shape[1]
    flats = []
    for ref in att_refs:
        flats.append(
            jnp.concatenate([unpack_rows(ref[g]) for g in range(ref.shape[0])], axis=1)
        )
    flat = jnp.concatenate(flats, axis=0)
    middle = x_ref[...].astype(f32) + nn(flat, dense_ref[:, :model])
    middle_ref[...] = middle
    second = (middle * inverse_norm(middle) * gain_ref[...]).astype(bf16)
    second_ref[...] = second
    positions = sent_ref.shape[0]
    hot = (
        lax.broadcasted_iota(jnp.int32, (positions, x_ref.shape[0]), 0) == target_ref[...]
    ).astype(bf16)
    sent_ref[...] = nn(hot, second).astype(bf16)


def project(x, target_row, gain, dense, attended, positions):
    tokens, model = x.shape
    out_shape = [
        shape((tokens, model), f32),
        shape((tokens, model), bf16),
        shape((positions, model), bf16),
    ]
    operands = (x, target_row, gain, dense, *attended)
    return pl.pallas_call(
        project_kernel,
        in_specs=[whole(a) for a in operands],
        out_specs=[whole(a) for a in out_shape],
        out_shape=out_shape,
        compiler_params=PARAMS,
        cost_estimate=cost(2 * tokens * model * (model + positions), *out_shape),
        name="project",
    )(*operands)


def route_kernel(
    second_ref, dy_ref, id_ref, target_ref, dense_ref, *refs
):
    att_refs, (flat_ref, prob_ref, grad_ref) = refs[:-3], refs[-3:]
    tokens, model = dy_ref.shape
    flats = []
    for ref in att_refs:
        flats.append(
            jnp.concatenate([unpack_rows(ref[g]) for g in range(ref.shape[0])], axis=1)
        )
    flat_ref[...] = jnp.concatenate(flats, axis=0)
    logits = nn(second_ref[...], dense_ref[:, model:])
    peak = jnp.max(logits, axis=-1, keepdims=True)
    grown = jnp.exp(logits - peak)
    probs = grown / jnp.sum(grown, axis=-1, keepdims=True)
    prob_ref[...] = probs
    chosen = lax.broadcasted_iota(jnp.int32, probs.shape, 1) == id_ref[...]
    gate = jnp.sum(jnp.where(chosen, probs, 0.0), axis=-1, keepdims=True)
    out_grad = (gate * dy_ref[...].astype(f32)).astype(bf16)
    hot = (
        lax.broadcasted_iota(jnp.int32, (grad_ref.shape[0], tokens), 0) == target_ref[...]
    ).astype(bf16)
    grad_ref[...] = nn(hot, out_grad).astype(bf16)


def route(second, dy, id_column, target_row, dense, attended, positions):
    tokens, model = dy.shape
    out_shape = [
        shape((tokens, model), bf16),
        shape((tokens, dense.shape[1] - model), f32),
        shape((positions, model), bf16),
    ]
    operands = (second, dy, id_column, target_row, dense, *attended)
    return pl.pallas_call(
        route_kernel,
        in_specs=[whole(a) for a in operands],
        out_specs=[whole(a) for a in out_shape],
        out_shape=out_shape,
        compiler_params=PARAMS,
        cost_estimate=cost(2 * tokens * model * positions, *out_shape),
        name="route",
    )(*operands)


def returned_kernel(target_ref, id_ref, middle_ref, dy_ref, prob_ref, second_ref, *refs):
    back_refs, (out_ref, logit_ref, router_ref) = refs[:-3], refs[-3:]
    tokens, model = middle_ref.shape
    back = jnp.concatenate([ref[...].reshape(-1, model) for ref in back_refs], axis=0)
    hot = (
        lax.broadcasted_iota(jnp.int32, (tokens, back.shape[0]), 1) == target_ref[...]
    ).astype(bf16)
    token_out = nn(hot, back)
    probs = prob_ref[...]
    chosen = lax.broadcasted_iota(jnp.int32, probs.shape, 1) == id_ref[...]
    gate = jnp.sum(jnp.where(chosen, probs, 0.0), axis=-1, keepdims=True)
    out_ref[...] = (middle_ref[...] + gate * token_out).astype(bf16)
    gate_grad = jnp.sum(dy_ref[...].astype(f32) * token_out, axis=-1, keepdims=True)
    picked = jnp.where(chosen, gate_grad, 0.0)
    logit_grad = probs * (picked - jnp.sum(probs * picked, axis=-1, keepdims=True))
    logit_low = logit_grad.astype(bf16)
    logit_ref[...] = logit_low
    router_ref[...] = tn(second_ref[...], logit_low).astype(bf16)


def returned(back, target_column, id_column, middle, dy, probs, second):
    tokens, model = middle.shape
    experts = probs.shape[1]
    out_shape = [
        shape((tokens, model), bf16),
        shape((tokens, experts), bf16),
        shape((model, experts), bf16),
    ]
    operands = (target_column, id_column, middle, dy, probs, second, *back)
    return pl.pallas_call(
        returned_kernel,
        in_specs=[whole(a) for a in operands],
        out_specs=[whole(a) for a in out_shape],
        out_shape=out_shape,
        compiler_params=PARAMS,
        cost_estimate=cost(4 * tokens * tokens * model, *out_shape, middle, *back),
        name="returned",
    )(*operands)


def branch_kernel(
    back_ref, target_ref, logit_ref, dense_ref, middle_ref, gain_ref, dy_ref,
    middle_grad_ref, branch_ref, grad_ref, gain_grad_ref,
):
    tokens, model = middle_ref.shape
    hot = (
        lax.broadcasted_iota(jnp.int32, (tokens, back_ref.shape[0]), 1) == target_ref[...]
    ).astype(bf16)
    second_grad = nn(hot, back_ref[...]) + nt(logit_ref[...], dense_ref[:, model:])
    norm_grad, gain_grad = norm_backward(middle_ref[...], gain_ref[...], second_grad)
    gain_grad_ref[...] = gain_grad
    middle_grad = dy_ref[...].astype(f32) + norm_grad
    middle_grad_ref[...] = middle_grad
    branch = middle_grad.astype(bf16)
    branch_ref[...] = branch
    grad = nt(branch, dense_ref[:, :model]).astype(bf16)
    groups = grad_ref.shape[0]
    width = model // groups
    for group in range(groups):
        grad_ref[group] = pack_rows(grad[:, group * width : (group + 1) * width])


def branch_back(back, target_column, logit, dense, middle, gain, dy, number, seqs, groups):
    tokens, model = middle.shape
    piece = tokens // seqs

    def rows_of(array):
        return pl.BlockSpec((piece, array.shape[1]), lambda _: (number, 0))

    out_shape = [
        shape((piece, model), f32),
        shape((piece, model), bf16),
        shape((groups, piece // 2, 2 * model // groups), bf16),
        shape((1, model), f32),
    ]
    return pl.pallas_call(
        branch_kernel,
        grid=(1,),
        in_specs=[
            whole(back), rows_of(target_column), rows_of(logit), whole(dense), rows_of(middle),
            whole(gain), rows_of(dy),
        ],
        out_specs=[whole(a) for a in out_shape],
        out_shape=out_shape,
        compiler_params=PARAMS,
        cost_estimate=cost(6 * piece * model * model, *out_shape, back, dense),
        name="branch_back",
    )(back, target_column, logit, dense, middle, gain, dy)


def dense_kernel(flat_ref, router_ref, *refs):
    out_ref = refs[-1]
    branch = jnp.concatenate([ref[...] for ref in refs[:-1]], axis=0)
    model = branch.shape[1]
    out_ref[:, :model] = tn(flat_ref[...], branch).astype(bf16)
    out_ref[:, model:] = router_ref[...]


def dense_grads(flat, branches, router):
    model, experts = router.shape
    out_shape = shape((model, model + experts), bf16)
    return pl.pallas_call(
        dense_kernel,
        in_specs=[whole(a) for a in (flat, router, *branches)],
        out_specs=whole(out_shape),
        out_shape=out_shape,
        compiler_params=PARAMS,
        cost_estimate=cost(2 * math.prod(flat.shape) * model, flat, router, *branches),
        name="dense_grads",
    )(flat, router, *branches)


def input_kernel(grad_ref, weight_ref, x_ref, gain_ref, middle_grad_ref, *refs):
    out_ref, gain_grad_ref = refs[-2:]
    total = None
    for group in range(weight_ref.shape[0]):
        part = nt(unpack_rows(grad_ref[group]), weight_ref[group])
        total = part if total is None else total + part
    norm_grad, gain_grad = norm_backward(x_ref[0].astype(f32), gain_ref[...], total)
    out_ref[0] = middle_grad_ref[...] + norm_grad
    gain_grad_ref[...] = gain_grad


def input_back(grad, weights, x, gain, middle_grad, number, earlier):
    seqs, piece, model = x.shape
    row_spec = pl.BlockSpec((1, piece, model), lambda _: (number, 0, 0))
    out_shape = [shape(x.shape, f32), shape((1, model), f32)]
    operands = [grad, weights, x, gain, middle_grad]
    specs = [whole(grad), whole(weights), row_spec, whole(gain), whole(middle_grad)]
    aliases = {}
    if earlier is not None:
        aliases = {len(operands): 0}
        operands.append(earlier)
        specs.append(pl.BlockSpec(memory_space=pl.ANY))
    return pl.pallas_call(
        input_kernel,
        grid=(1,),
        in_specs=specs,
        out_specs=[row_spec, whole(out_shape[1])],
        out_shape=out_shape,
        input_output_aliases=aliases,
        compiler_params=PARAMS,
        cost_estimate=cost(2 * piece * math.prod(weights.shape), grad, weights, middle_grad),
        name="input_back",
    )(*operands)


def column_kernel(seqs, place_ref, *refs):
    row_refs, grad_refs, out_refs = refs[:seqs], refs[seqs : 2 * seqs], refs[2 * seqs : -1]
    total = refs[-1]
    value = None
    for row_ref, grad_ref in zip(row_refs, grad_refs):
        grad = jnp.concatenate(
            [unpack_rows(grad_ref[piece]) for piece in range(grad_ref.shape[0])], axis=0
        )
        part = tn(row_ref[...], grad)
        value = part if value is None else value + part
    if len(out_refs) == 1:
        out_refs[0][...] = value.astype(bf16)
        return
    total[...] = value.astype(bf16)
    for number in range(2 * out_refs[0].shape[0]):
        ref = out_refs[number % 2]
        rows = ref.shape[1]
        at = pl.multiple_of(place_ref[number] * rows, rows)
        ref[number // 2] = total[pl.ds(at, rows), :]


def column_grads(places, rows, grads, chunks):
    model = rows[0].shape[1]
    cols = grads[0].shape[2] // 2
    if chunks > 1:
        out_shape = [shape((chunks // 2, model // chunks, cols), bf16)] * 2
    else:
        out_shape = [shape((model, cols), bf16)]
    return pl.pallas_call(
        functools.partial(column_kernel, len(rows)),
        in_specs=[SMEM] + [whole(a) for a in (*rows, *grads)],
        out_specs=[whole(a) for a in out_shape],
        out_shape=out_shape,
        scratch_shapes=[pltpu.VMEM((model, cols), bf16)],
        compiler_params=PARAMS,
        cost_estimate=cost(2 * sum(math.prod(r.shape) for r in rows) * cols, *rows, *grads),
        name="column_grads",
    )(places, *rows, *grads)


def column_order_kernel(place_ref, *refs):
    out_ref, held = refs[-2:]
    groups = held.shape[0]
    width = held.shape[2] // 3
    for number in range(groups):
        held[number] = refs[number][...].astype(f32)
    for part in range(3):
        joined = [
            held[place_ref[group], :, part * width : (part + 1) * width] for group in range(groups)
        ]
        out_ref[:, part * groups * width : (part + 1) * groups * width] = jnp.concatenate(
            joined, axis=1
        )


def column_order(places, pieces):
    rows, cols = pieces[0].shape
    out_shape = shape((rows, cols * len(pieces)), f32)
    return pl.pallas_call(
        column_order_kernel,
        in_specs=[SMEM] + [whole(a) for a in pieces],
        out_specs=whole(out_shape),
        out_shape=out_shape,
        scratch_shapes=[pltpu.VMEM((len(pieces), rows, cols), f32)],
        compiler_params=PARAMS,
        cost_estimate=cost(0, out_shape, *pieces),
        name="column_order",
    )(places, *pieces)


def expert_kernel(x_ref, win_ref, wout_ref, y_ref, slope_ref, acc):
    tile = pl.program_id(1)
    rows = acc.shape[0]
    x = x_ref[...].reshape(rows, x_ref.shape[-1])
    pre = jnp.dot(x, win_ref[0], preferred_element_type=f32)
    hidden, slope = gelu_and_slope(pre)
    slope_ref[0] = slope.astype(bf16)
    part = jnp.dot(hidden.astype(bf16), wout_ref[0], preferred_element_type=f32)

    @pl.when(tile == 0)
    def _():
        acc[...] = part

    @pl.when(tile > 0)
    def _():
        acc[...] += part

    @pl.when(tile == pl.num_programs(1) - 1)
    def _():
        y_ref[...] = acc[...].astype(bf16).reshape(y_ref.shape)


def expert_forward(x, w_in, w_out, tile):
    sources, experts, slots, model = x.shape
    hidden = w_in.shape[2]
    rows = sources * slots
    row_spec = pl.BlockSpec((sources, 1, slots, model), lambda e, f: (0, e, 0, 0))
    return pl.pallas_call(
        expert_kernel,
        grid=(experts, hidden // tile),
        in_specs=[
            row_spec,
            pl.BlockSpec((1, model, tile), lambda e, f: (e, 0, f)),
            pl.BlockSpec((1, tile, model), lambda e, f: (e, f, 0)),
        ],
        out_specs=[row_spec, pl.BlockSpec((1, rows, tile), lambda e, f: (e, 0, f))],
        out_shape=[
            jax.ShapeDtypeStruct(x.shape, bf16),
            jax.ShapeDtypeStruct((experts, rows, hidden), bf16),
        ],
        scratch_shapes=[pltpu.VMEM((rows, model), f32)],
        compiler_params=pltpu.CompilerParams(vmem_limit_bytes=52 * MIB),
        name="expert_forward",
    )(x, w_in, w_out)


def expert_back_kernel(g_ref, win_ref, wout_ref, slope_ref, y_ref, acc):
    tile = pl.program_id(1)
    rows = acc.shape[0]
    g = g_ref[...].reshape(rows, g_ref.shape[-1])
    pre_grad = (nt(g, wout_ref[0]) * slope_ref[0].astype(f32)).astype(bf16)
    part = nt(pre_grad, win_ref[0])

    @pl.when(tile == 0)
    def _():
        acc[...] = part

    @pl.when(tile > 0)
    def _():
        acc[...] += part

    @pl.when(tile == pl.num_programs(1) - 1)
    def _():
        y_ref[...] = acc[...].astype(bf16).reshape(y_ref.shape)


def expert_backward(g, w_in, w_out, slope, tile):
    sources, experts, slots, model = g.shape
    hidden = w_in.shape[2]
    rows = sources * slots
    row_spec = pl.BlockSpec((sources, 1, slots, model), lambda e, f: (0, e, 0, 0))
    return pl.pallas_call(
        expert_back_kernel,
        grid=(experts, hidden // tile),
        in_specs=[
            row_spec,
            pl.BlockSpec((1, model, tile), lambda e, f: (e, 0, f)),
            pl.BlockSpec((1, tile, model), lambda e, f: (e, f, 0)),
            pl.BlockSpec((1, rows, tile), lambda e, f: (e, 0, f)),
        ],
        out_specs=row_spec,
        out_shape=jax.ShapeDtypeStruct(g.shape, bf16),
        scratch_shapes=[pltpu.VMEM((rows, model), f32)],
        compiler_params=PARAMS,
        cost_estimate=cost(4 * experts * rows * model * hidden, g, w_in, w_out, slope),
        name="expert_backward",
    )(g, w_in, w_out, slope)


def weight_grad_kernel(pieces, place_ref, *refs):
    x_refs, g_refs = refs[:pieces], refs[pieces : 2 * pieces]
    win_ref, wout_ref = refs[2 * pieces : 2 * pieces + 2]
    earlier = refs[2 * pieces + 2 : -2]
    gin_ref, gout_ref = refs[-2:]
    gin, gout = (earlier[0][0], earlier[1][0]) if earlier else (None, None)
    for x_ref, g_ref in zip(x_refs, g_refs):
        rows = x_ref.shape[0] * x_ref.shape[2]
        x = x_ref[...].reshape(rows, x_ref.shape[-1])
        g = g_ref[...].reshape(rows, g_ref.shape[-1])
        hidden, slope = gelu_and_slope(nn(x, win_ref[0]))
        pre_grad = (nt(g, wout_ref[0]) * slope).astype(bf16)
        gin_part = tn(x, pre_grad)
        gout_part = tn(hidden.astype(bf16), g)
        gin = gin_part if gin is None else gin + gin_part
        gout = gout_part if gout is None else gout + gout_part
    gin_ref[0] = gin
    gout_ref[0] = gout


def weight_grads(place, xs, gs, w_in, w_out, ways, earlier):
    experts, model, hidden = w_in.shape
    cols = hidden // ways
    tile = GRAD_TILE if cols % GRAD_TILE == 0 else cols
    tiles = cols // tile

    def rows_of(array):
        sources, _, slots, _ = array.shape
        return pl.BlockSpec((sources, 1, slots, model), lambda e, t, q: (0, e, 0, 0))

    out_shape = [shape((experts, model, cols), f32), shape((experts, cols, model), f32)]
    out_specs = [
        pl.BlockSpec((1, model, tile), lambda e, t, q: (e, 0, t)),
        pl.BlockSpec((1, tile, model), lambda e, t, q: (e, t, 0)),
    ]
    flops = 16 * sum(math.prod(a.shape) for a in xs) * cols
    operands = [place, *xs, *gs, w_in, w_out]
    specs = [rows_of(a) for a in (*xs, *gs)] + [
        pl.BlockSpec((1, model, tile), lambda e, t, q: (e, 0, q[0] * tiles + t)),
        pl.BlockSpec((1, tile, model), lambda e, t, q: (e, q[0] * tiles + t, 0)),
    ]
    aliases = {}
    if earlier is not None:
        aliases = {len(operands): 0, len(operands) + 1: 1}
        operands += list(earlier)
        specs += out_specs
    return pl.pallas_call(
        functools.partial(weight_grad_kernel, len(xs)),
        grid_spec=pltpu.PrefetchScalarGridSpec(
            num_scalar_prefetch=1,
            grid=(experts, tiles),
            in_specs=specs,
            out_specs=out_specs,
        ),
        out_shape=out_shape,
        input_output_aliases=aliases,
        compiler_params=PARAMS,
        cost_estimate=cost(flops, *out_shape, *xs, *gs),
        name="weight_grads",
    )(*operands)


def partners(ways, step):
    return [(index, index ^ step) for index in range(ways)]


def swap(value, axis, step):
    return lax.ppermute(value, axis, partners(lax.axis_size(axis), step))


def gather_near(value):
    return swap(value, "seq", 1), swap(value, "seq", 2)


def gather_far(near, far):
    half = near.shape[0] // 2
    return swap(near[:half], "seq", 2), swap(far[half:], "seq", 1)


def sum_exchange(value, axis):
    copies = jnp.broadcast_to(value[None], (lax.axis_size(axis),) + value.shape)
    return jnp.sum(lax.all_to_all(copies, axis, 0, 0, tiled=True), axis=0)


def add_low(a, b):
    return (a.astype(f32) + b.astype(f32)).astype(bf16)


def scatter_rows(value):
    ways = lax.axis_size("shard")
    rows, cols = value.shape
    parts = lax.all_to_all(value.reshape(ways, rows // ways, cols), "shard", 0, 0, tiled=True)
    return jnp.sum(parts.astype(f32), axis=0)


def body(
    block_input,
    gain_attn,
    gain_ffn,
    w_qkv,
    w_out,
    w_router,
    rel_bias,
    w_in,
    w_exp_out,
    expert_id,
    capacity_slot,
    buckets,
    output_grad,
):
    seqs, piece, model = block_input.shape
    seq_ways = lax.axis_size("seq")
    shard_ways = lax.axis_size("shard")
    bucket_count, heads_all = rel_bias.shape
    heads = heads_all // seq_ways
    width = model // seq_ways
    length = piece * seq_ways
    experts = w_router.shape[1]
    tokens = seqs * piece
    capacity = 2 * tokens // experts
    positions = experts * capacity
    slot_shape = (shard_ways, experts // shard_ways, capacity, model)
    weight_rows = w_qkv.shape[0]
    seq_index = lax.axis_index("seq").astype(jnp.int32)
    places = jnp.stack([seq_index ^ step for step in range(seq_ways)])
    gain_one_row = gain_attn.reshape(1, model)
    gain_two_row = gain_ffn.reshape(1, model)
    bucket_row = jnp.pad(
        buckets, (0, 2 * length - buckets.shape[0]), constant_values=-1
    ).reshape(1, 2 * length)
    target = jnp.where(capacity_slot < capacity, expert_id * capacity + capacity_slot, -1)
    target_row = target.reshape(1, tokens)
    target_column = target.reshape(tokens, 1)
    by_chunks = shard_ways <= 8 and weight_rows % 16 == 0
    shard_index = lax.axis_index("shard").astype(jnp.int32)
    order = jnp.stack([shard_index ^ step for step in range(shard_ways)])
    id_column = expert_id.reshape(tokens, 1)
    upstream = output_grad.reshape(tokens, model)

    own_columns = lax.dynamic_slice_in_dim(
        w_qkv.reshape(weight_rows, 3, model), seq_index * width, width, 2
    ).reshape(weight_rows, 3 * width)
    own_columns = jnp.pad(own_columns, ((0, 0), (0, max(0, model - 3 * width))))
    head_weight = lax.all_gather(own_columns, "shard", axis=0, tiled=True)
    inputs = block_input.astype(f32)
    normed = (inputs * inverse_norm(inputs) * gain_attn).astype(bf16)
    tiles = bias_tiles(
        lax.dynamic_slice_in_dim(rel_bias, seq_index * heads, heads, 1), bucket_row
    )

    first_near = gather_near(normed[0])
    held = lax.optimization_barrier((normed[1], first_near))
    first_near = held[1]
    second_near = gather_near(held[0])
    first_far = gather_far(*first_near)
    dense_rows, head_weight, first_far, second_near, tiles = lax.optimization_barrier(
        (jnp.concatenate([w_out, w_router], axis=1), head_weight, first_far, second_near, tiles)
    )
    second_far = gather_far(*second_near)
    dense = lax.all_gather(dense_rows, "shard", axis=0, tiled=True)
    sequence_pieces = (
        (normed[0], *first_near, *first_far),
        (normed[1], *second_near, *second_far),
    )
    kept, attended_tok = [], []
    for pieces in sequence_pieces:
        rows, qkv, attended, probs = attend(places, pieces, head_weight, tiles)
        kept.append((rows, qkv, probs))
        attended_tok.append(lax.all_to_all(attended, "seq", 0, 0, tiled=True))

    middle, second, sent = project(
        block_input.reshape(tokens, model), target_row, gain_two_row, dense, attended_tok, positions
    )
    attended_flat, router_probs, sent_grad = route(
        second, upstream, id_column, target_row, dense, attended_tok, positions
    )

    def exchange(rows):
        return lax.all_to_all(rows, "shard", 0, 0, tiled=True)

    held_weight = lax.optimization_barrier((head_weight[:, : 3 * width], attended_tok[0]))[0]
    weight_groups = lax.all_gather(held_weight, "seq")
    arrived = exchange(sent.reshape(slot_shape))
    arrived, sent_grad, weight_groups = lax.optimization_barrier(
        (arrived, sent_grad, weight_groups)
    )
    arrived_near = gather_near(arrived)
    out_arrived = exchange(sent_grad.reshape(slot_shape))
    expert_out, slope = expert_forward(arrived, w_in, w_exp_out, FORWARD_TILE)
    expert_out, out_arrived, weight_groups, arrived_near = lax.optimization_barrier(
        (expert_out, out_arrived, weight_groups, arrived_near)
    )
    back_out = exchange(expert_out).reshape(positions, model)
    out_near = gather_near(out_arrived)

    def expert_grads(xs, gs, earlier):
        return weight_grads(places, xs, gs, w_in, w_exp_out, seq_ways, earlier)

    rows_grad = expert_backward(out_arrived, w_in, w_exp_out, slope, FORWARD_TILE)
    expert_part = expert_grads((arrived,), (out_arrived,), None)
    rows_grad, back_out, expert_part = lax.optimization_barrier((rows_grad, back_out, expert_part))
    back_grad = exchange(rows_grad).reshape(positions, model)
    block_output, logit_low, grad_router = returned(
        (back_out,), target_column, id_column, middle, upstream, router_probs, second
    )
    expert_part = expert_grads(arrived_near, out_near, expert_part)
    arrived_near, out_near = lax.optimization_barrier((arrived_near, out_near))
    out_far = gather_far(*out_near)
    arrived_far = gather_far(*arrived_near)
    back_grad, logit_low, expert_part = lax.optimization_barrier(
        (back_grad, logit_low, expert_part)
    )
    middle_grads, branches, grad_heads, gain_two = [], [], [], []
    for number in range(seqs):
        middle_grad, branch, attended_grad, gain_part = branch_back(
            back_grad, target_column, logit_low, dense, middle, gain_two_row, upstream,
            number, seqs, seq_ways,
        )
        middle_grads.append(middle_grad)
        branches.append(branch)
        gain_two.append(gain_part)
        grad_heads.append(lax.all_to_all(attended_grad, "seq", 0, 0, tiled=True))
    grad_dense = dense_grads(attended_flat, branches, grad_router)
    grad_heads[0], grad_dense, out_far, arrived_far = lax.optimization_barrier(
        (grad_heads[0], grad_dense, out_far, arrived_far)
    )
    grad_dense = lax.psum_scatter(grad_dense, "shard", scatter_dimension=0, tiled=True)

    qkv_grads, bias_parts, grad_tok = [], [], []
    for number in range(seqs):
        _, qkv, probs = kept[number]
        grad = grad_heads[number]
        qkv_grad, bias_part = attend_back(qkv, probs, grad, bucket_row, bucket_count)
        qkv_grads.append(qkv_grad)
        bias_parts.append(bias_part)
        grad_tok.append(lax.all_to_all(qkv_grad, "seq", 0, 0, tiled=True))
    input_grad, first_gain = input_back(
        grad_tok[0], weight_groups, block_input, gain_one_row, middle_grads[0], 0, None
    )
    gain_one = [first_gain]
    qkv_grads[-1], grad_dense = lax.optimization_barrier((qkv_grads[-1], grad_dense))
    rows_all = [each[0] for each in kept]
    if by_chunks:
        columns, other = column_grads(order, rows_all, qkv_grads, shard_ways)
        last = other
        columns = add_low(columns, swap(other, "shard", 1))
        out_far = lax.optimization_barrier((out_far, columns))[0]
        step = shard_ways // 2
        if step > 1:
            half = columns.shape[0] // 2
            columns = add_low(columns[:half], swap(columns[half:], "shard", step))
            step //= 2
    else:
        (last,) = column_grads(places - places, rows_all, qkv_grads, 1)
        columns = last
    expert_part = expert_grads(arrived_far, out_far, expert_part)
    grad_tok[-1], input_grad, columns, expert_part = lax.optimization_barrier(
        (grad_tok[-1], input_grad, columns, expert_part)
    )
    grad_in_part, grad_exp_part = expert_part
    for number in range(1, seqs):
        input_grad, gain_part = input_back(
            grad_tok[number], weight_groups, block_input, gain_one_row,
            middle_grads[number], number, input_grad,
        )
        gain_one.append(gain_part)
    grad_dense = lax.optimization_barrier((grad_dense, gain_one[-1]))[0]
    grad_dense = add_low(grad_dense, swap(grad_dense, "seq", 1))
    grad_dense = grad_dense.astype(f32) + swap(grad_dense, "seq", 2).astype(f32)
    bias_grad = lax.dynamic_update_slice_in_dim(
        jnp.zeros((bucket_count, heads_all), f32),
        functools.reduce(jnp.add, bias_parts)[:, :heads],
        seq_index * heads,
        1,
    )
    small = jnp.concatenate(
        [bias_grad.reshape(-1), sum(gain_two).reshape(-1), sum(gain_one).reshape(-1)]
    ).reshape(-1, LANES)
    if by_chunks:
        while step > 1:
            half = columns.shape[0] // 2
            columns = add_low(columns[:half], swap(columns[half:], "shard", step))
            step //= 2
        columns = columns[0]
    else:
        columns = scatter_rows(columns).astype(bf16)
    grad_qkv = column_order(
        places, [columns] + [swap(columns, "seq", step) for step in range(1, seq_ways)]
    )
    small = sum_exchange(sum_exchange(small, "seq"), "shard").reshape(-1)
    bias_size = bucket_count * heads_all
    return (
        block_output.reshape(block_input.shape),
        input_grad,
        small[bias_size + model :],
        small[bias_size : bias_size + model],
        grad_qkv,
        grad_dense[:, :model],
        grad_dense[:, model:],
        small[:bias_size].reshape(bucket_count, heads_all),
        grad_in_part,
        grad_exp_part,
    )


def solution(mesh):
    placed = (
        P("shard", "seq", None),
        P(),
        P(),
        P("shard", None),
        P("shard", None),
        P("shard", None),
        P(),
        P("shard", None, None),
        P("shard", None, None),
        P("shard", "seq"),
        P("shard", "seq"),
        P(),
        P("shard", "seq", None),
    )
    return jax.shard_map(
        body,
        mesh=mesh,
        in_specs=placed,
        out_specs=(
            P("shard", "seq", None),
            P("shard", "seq", None),
            P(),
            P(),
            P("shard", None),
            P("shard", None),
            P("shard", None),
            P(),
            P("shard", None, "seq"),
            P("shard", "seq", None),
        ),
        check_vma=False,
    )
```

```python
import functools
import math

import jax
import jax.numpy as jnp
from jax import lax
from jax.experimental import pallas as pl
from jax.experimental.pallas import tpu as pltpu
from jax.sharding import PartitionSpec as P

f32 = jnp.float32
bf16 = jnp.bfloat16
LANES = 128
MIB = 1024 * 1024
BLOCK_ROWS = 256
FORWARD_TILE = 1024
GRAD_TILE = 768
norm_eps = 1e-06
ROOT_HALF = 1.0 / math.sqrt(2.0)
DENSITY = 1.0 / math.sqrt(2.0 * math.pi)
PARAMS = pltpu.CompilerParams(vmem_limit_bytes=52 * MIB)
SMEM = pl.BlockSpec(memory_space=pltpu.SMEM)


def nn(a, b):
    return jnp.dot(a, b, preferred_element_type=f32)


def nt(a, b):
    return lax.dot_general(a, b, (((1,), (1,)), ((), ())), preferred_element_type=f32)


def tn(a, b):
    return lax.dot_general(a, b, (((0,), (0,)), ((), ())), preferred_element_type=f32)


def whole(array):
    zeros = (0,) * array.ndim
    return pl.BlockSpec(array.shape, lambda *_: zeros)


def cost(flops, *arrays):
    return pl.CostEstimate(
        flops=int(flops),
        bytes_accessed=int(sum(math.prod(a.shape) * a.dtype.itemsize for a in arrays)),
        transcendentals=0,
    )


def shape(dims, kind):
    return jax.ShapeDtypeStruct(dims, kind)


def pack_rows(values):
    half = values.shape[0] // 2
    return jnp.concatenate([values[:half], values[half:]], axis=1)


def unpack_rows(packed):
    width = packed.shape[1] // 2
    return jnp.concatenate([packed[:, :width], packed[:, width:]], axis=0)


def inverse_norm(values):
    return lax.rsqrt(jnp.mean(values * values, axis=-1, keepdims=True) + norm_eps)


def norm_backward(values, gain, upstream):
    inverse = inverse_norm(values)
    scaled = upstream * gain
    inner = jnp.mean(scaled * values, axis=-1, keepdims=True)
    result = inverse * scaled - values * (inverse * inverse * inverse * inner)
    return result, jnp.sum(upstream * values * inverse, axis=0, keepdims=True)


def gelu_and_slope(v):
    cumulative = 0.5 * (1.0 + lax.erf(v * ROOT_HALF))
    return v * cumulative, cumulative + v * (jnp.exp(-0.5 * v * v) * DENSITY)


def bias_kernel(rel_ref, bucket_ref, out_ref):
    span = bucket_ref.shape[1]
    bucket_row = bucket_ref[...]
    for head in range(out_ref.shape[0]):
        row = jnp.zeros((1, span), f32)
        for bucket in range(rel_ref.shape[0]):
            row = jnp.where(bucket_row == bucket, rel_ref[bucket, head], row)
        out_ref[head] = pltpu.roll(
            jnp.broadcast_to(row, (LANES, span)), span - LANES + 1, 1, stride=1, stride_axis=0
        )


def bias_tiles(rel, bucket_row):
    out_shape = shape((rel.shape[1], LANES, bucket_row.shape[1]), f32)
    return pl.pallas_call(
        bias_kernel,
        in_specs=[SMEM, whole(bucket_row)],
        out_specs=whole(out_shape),
        out_shape=out_shape,
        compiler_params=PARAMS,
        cost_estimate=cost(0, out_shape),
        name="bias_tiles",
    )(rel, bucket_row)


def attend_kernel(
    place_ref, own_ref, near_ref, far_ref, low_ref, high_ref, w_ref, toeplitz_ref,
    rows_ref, qkv_ref, att_ref, prob_ref, split, outs,
):
    head = pl.program_id(0)
    heads, length, head_dim = outs.shape
    width = heads * head_dim
    piece = own_ref.shape[0]

    @pl.when(head == 0)
    def _():
        for number, ref in enumerate((own_ref, near_ref, far_ref)):
            at = pl.multiple_of(place_ref[number] * piece, piece)
            rows_ref[pl.ds(at, piece), :] = ref[...]
        at = pl.multiple_of(place_ref[3] * piece, piece)
        half = piece // 2
        rows_ref[pl.ds(at, half), :] = low_ref[...]
        rows_ref[pl.ds(pl.multiple_of(at + half, half), half), :] = high_ref[...]
        qkv = nn(rows_ref[...], w_ref[:, : 3 * width]).astype(bf16)
        qkv_ref[...] = qkv
        for part in range(3):
            for each in range(heads):
                at = part * width + each * head_dim
                split[part, each] = qkv[:, at : at + head_dim]

    keys = split[1, head]
    turned = split[2, head].T
    for start in range(0, length, BLOCK_ROWS):
        scores = nt(split[0, head, start : start + BLOCK_ROWS], keys)
        parts = []
        for sub in range(0, BLOCK_ROWS, LANES):
            off = length - LANES - start - sub
            parts.append(scores[sub : sub + LANES] + toeplitz_ref[0, :, off : off + length])
        scores = jnp.concatenate(parts, axis=0)
        peak = jnp.max(scores, axis=-1, keepdims=True)
        grown = jnp.exp(scores - peak)
        total = jnp.sum(grown, axis=-1, keepdims=True)
        prob_ref[0, start : start + BLOCK_ROWS, :] = (grown * (1.0 / total)).astype(bf16)
    outs[head] = nt(turned, prob_ref[0]).T

    @pl.when(head == heads - 1)
    def _():
        joined = jnp.concatenate([outs[each].astype(bf16) for each in range(heads)], axis=1)
        for number in range(length // piece):
            att_ref[number] = pack_rows(joined[number * piece : (number + 1) * piece])


def attend(place, pieces, weight, tiles):
    own, near, far, low, high = pieces
    piece, model = own.shape
    heads, _, span = tiles.shape
    length = span // 2
    cols = 3 * (model // (length // piece))
    width = cols // 3
    head_dim = width // heads
    out_shape = [
        shape((length, model), bf16),
        shape((length, cols), bf16),
        shape((length // piece, piece // 2, 2 * width), bf16),
        shape((heads, length, length), bf16),
    ]
    return pl.pallas_call(
        attend_kernel,
        grid=(heads,),
        in_specs=[SMEM]
        + [whole(a) for a in (own, near, far, low, high, weight)]
        + [pl.BlockSpec((1, LANES, span), lambda h: (h, 0, 0))],
        out_specs=[whole(a) for a in out_shape[:3]]
        + [pl.BlockSpec((1, length, length), lambda h: (h, 0, 0))],
        out_shape=out_shape,
        scratch_shapes=[
            pltpu.VMEM((3, heads, length, head_dim), bf16),
            pltpu.VMEM((heads, length, head_dim), f32),
        ],
        compiler_params=PARAMS,
        cost_estimate=cost(2 * length * model * cols + 16 * heads * length * length * head_dim, *out_shape),
        name="attend",
    )(place, own, near, far, low, high, weight, tiles)


def attend_back_kernel(
    qkv_ref, prob_ref, grad_ref, bucket_ref, out_ref, bias_ref, split, outs, acc, score_grads
):
    head = pl.program_id(0)
    heads, length, head_dim = outs.shape[1:]
    width = heads * head_dim
    span = 2 * length
    pieces, half, _ = grad_ref.shape
    piece = 2 * half

    @pl.when(head == 0)
    def _():
        bias_ref[...] = jnp.zeros_like(bias_ref)
        for part in range(3):
            for each in range(heads):
                at = part * width + each * head_dim
                split[part, each] = qkv_ref[:, at : at + head_dim]
        for number in range(pieces):
            grad = unpack_rows(grad_ref[number])
            for each in range(heads):
                split[3, each, number * piece : (number + 1) * piece, :] = grad[
                    :, each * head_dim : (each + 1) * head_dim
                ]

    acc[...] = jnp.zeros_like(acc)
    values = split[2, head]
    for start in range(0, length, BLOCK_ROWS):
        prob_grad = nt(split[3, head, start : start + BLOCK_ROWS], values)
        prob = prob_ref[0, start : start + BLOCK_ROWS, :].astype(f32)
        weighted = prob * prob_grad
        inner = jnp.sum(weighted, axis=-1, keepdims=True)
        score_grad = weighted - prob * inner
        score_grads[start : start + BLOCK_ROWS, :] = score_grad.astype(bf16)
        for sub in range(0, BLOCK_ROWS, LANES):
            off = length - LANES - start - sub
            acc[:, off : off + length] += score_grad[sub : sub + LANES]
    outs[0, head] = nn(score_grads[...], split[1, head])
    outs[1, head] = tn(split[0, head], score_grads[...]).T
    outs[2, head] = tn(split[3, head], prob_ref[0]).T

    part = acc[...]
    rows = LANES
    while rows > 8:
        rows //= 2
        part = part[:rows] + pltpu.roll(part[rows:], span - rows, 1)
    offsets = part[0:1]
    for row in range(1, 8):
        offsets = offsets + pltpu.roll(part[row : row + 1], span - row, 1)
    offsets = pltpu.roll(offsets, LANES - 1, 1)
    hot = lax.broadcasted_iota(jnp.int32, (bias_ref.shape[0], span), 0) == bucket_ref[...]
    total = jnp.sum(jnp.where(hot, offsets, 0.0), axis=1, keepdims=True)
    lane = lax.broadcasted_iota(jnp.int32, bias_ref.shape, 1)
    bias_ref[...] = jnp.where(lane == head, total, bias_ref[...])

    @pl.when(head == heads - 1)
    def _():
        joined = jnp.concatenate(
            [outs[part, each].astype(bf16) for part in range(3) for each in range(heads)], axis=1
        )
        for number in range(pieces):
            out_ref[number] = pack_rows(joined[number * piece : (number + 1) * piece])


def attend_back(qkv, prob, grad, bucket_row, bucket_count):
    length, cols = qkv.shape
    heads = prob.shape[0]
    head_dim = cols // (3 * heads)
    pieces, half, _ = grad.shape
    out_shape = [shape((pieces, half, 2 * cols), bf16), shape((bucket_count, LANES), f32)]
    return pl.pallas_call(
        attend_back_kernel,
        grid=(heads,),
        in_specs=[
            whole(qkv),
            pl.BlockSpec((1, length, length), lambda h: (h, 0, 0)),
            whole(grad),
            whole(bucket_row),
        ],
        out_specs=[whole(a) for a in out_shape],
        out_shape=out_shape,
        scratch_shapes=[
            pltpu.VMEM((4, heads, length, head_dim), bf16),
            pltpu.VMEM((3, heads, length, head_dim), f32),
            pltpu.VMEM((LANES, 2 * length), f32),
            pltpu.VMEM((length, length), bf16),
        ],
        compiler_params=PARAMS,
        cost_estimate=cost(40 * heads * length * length * head_dim, qkv, prob, grad),
        name="attend_back",
    )(qkv, prob, grad, bucket_row)


def project_kernel(x_ref, target_ref, gain_ref, dense_ref, *refs):
    att_refs, (middle_ref, second_ref, sent_ref) = refs[:-3], refs[-3:]
    model = x_ref.shape[1]
    flats = []
    for ref in att_refs:
        flats.append(
            jnp.concatenate([unpack_rows(ref[g]) for g in range(ref.shape[0])], axis=1)
        )
    flat = jnp.concatenate(flats, axis=0)
    middle = x_ref[...].astype(f32) + nn(flat, dense_ref[:, :model])
    middle_ref[...] = middle
    second = (middle * inverse_norm(middle) * gain_ref[...]).astype(bf16)
    second_ref[...] = second
    positions = sent_ref.shape[0]
    hot = (
        lax.broadcasted_iota(jnp.int32, (positions, x_ref.shape[0]), 0) == target_ref[...]
    ).astype(bf16)
    sent_ref[...] = nn(hot, second).astype(bf16)


def project(x, target_row, gain, dense, attended, positions):
    tokens, model = x.shape
    out_shape = [
        shape((tokens, model), f32),
        shape((tokens, model), bf16),
        shape((positions, model), bf16),
    ]
    operands = (x, target_row, gain, dense, *attended)
    return pl.pallas_call(
        project_kernel,
        in_specs=[whole(a) for a in operands],
        out_specs=[whole(a) for a in out_shape],
        out_shape=out_shape,
        compiler_params=PARAMS,
        cost_estimate=cost(2 * tokens * model * (model + positions), *out_shape),
        name="project",
    )(*operands)


def route_kernel(
    second_ref, dy_ref, id_ref, target_ref, dense_ref, *refs
):
    att_refs, (flat_ref, prob_ref, grad_ref) = refs[:-3], refs[-3:]
    tokens, model = dy_ref.shape
    flats = []
    for ref in att_refs:
        flats.append(
            jnp.concatenate([unpack_rows(ref[g]) for g in range(ref.shape[0])], axis=1)
        )
    flat_ref[...] = jnp.concatenate(flats, axis=0)
    logits = nn(second_ref[...], dense_ref[:, model:])
    peak = jnp.max(logits, axis=-1, keepdims=True)
    grown = jnp.exp(logits - peak)
    probs = grown / jnp.sum(grown, axis=-1, keepdims=True)
    prob_ref[...] = probs
    chosen = lax.broadcasted_iota(jnp.int32, probs.shape, 1) == id_ref[...]
    gate = jnp.sum(jnp.where(chosen, probs, 0.0), axis=-1, keepdims=True)
    out_grad = (gate * dy_ref[...].astype(f32)).astype(bf16)
    hot = (
        lax.broadcasted_iota(jnp.int32, (grad_ref.shape[0], tokens), 0) == target_ref[...]
    ).astype(bf16)
    grad_ref[...] = nn(hot, out_grad).astype(bf16)


def route(second, dy, id_column, target_row, dense, attended, positions):
    tokens, model = dy.shape
    out_shape = [
        shape((tokens, model), bf16),
        shape((tokens, dense.shape[1] - model), f32),
        shape((positions, model), bf16),
    ]
    operands = (second, dy, id_column, target_row, dense, *attended)
    return pl.pallas_call(
        route_kernel,
        in_specs=[whole(a) for a in operands],
        out_specs=[whole(a) for a in out_shape],
        out_shape=out_shape,
        compiler_params=PARAMS,
        cost_estimate=cost(2 * tokens * model * positions, *out_shape),
        name="route",
    )(*operands)


def returned_kernel(target_ref, id_ref, middle_ref, dy_ref, prob_ref, second_ref, *refs):
    back_refs, (out_ref, logit_ref, router_ref) = refs[:-3], refs[-3:]
    tokens, model = middle_ref.shape
    back = jnp.concatenate([ref[...].reshape(-1, model) for ref in back_refs], axis=0)
    hot = (
        lax.broadcasted_iota(jnp.int32, (tokens, back.shape[0]), 1) == target_ref[...]
    ).astype(bf16)
    token_out = nn(hot, back)
    probs = prob_ref[...]
    chosen = lax.broadcasted_iota(jnp.int32, probs.shape, 1) == id_ref[...]
    gate = jnp.sum(jnp.where(chosen, probs, 0.0), axis=-1, keepdims=True)
    out_ref[...] = (middle_ref[...] + gate * token_out).astype(bf16)
    gate_grad = jnp.sum(dy_ref[...].astype(f32) * token_out, axis=-1, keepdims=True)
    picked = jnp.where(chosen, gate_grad, 0.0)
    logit_grad = probs * (picked - jnp.sum(probs * picked, axis=-1, keepdims=True))
    logit_low = logit_grad.astype(bf16)
    logit_ref[...] = logit_low
    router_ref[...] = tn(second_ref[...], logit_low).astype(bf16)


def returned(back, target_column, id_column, middle, dy, probs, second):
    tokens, model = middle.shape
    experts = probs.shape[1]
    out_shape = [
        shape((tokens, model), bf16),
        shape((tokens, experts), bf16),
        shape((model, experts), bf16),
    ]
    operands = (target_column, id_column, middle, dy, probs, second, *back)
    return pl.pallas_call(
        returned_kernel,
        in_specs=[whole(a) for a in operands],
        out_specs=[whole(a) for a in out_shape],
        out_shape=out_shape,
        compiler_params=PARAMS,
        cost_estimate=cost(4 * tokens * tokens * model, *out_shape, middle, *back),
        name="returned",
    )(*operands)


def branch_kernel(
    back_ref, target_ref, logit_ref, dense_ref, middle_ref, gain_ref, dy_ref,
    middle_grad_ref, branch_ref, grad_ref, gain_grad_ref,
):
    tokens, model = middle_ref.shape
    hot = (
        lax.broadcasted_iota(jnp.int32, (tokens, back_ref.shape[0]), 1) == target_ref[...]
    ).astype(bf16)
    second_grad = nn(hot, back_ref[...]) + nt(logit_ref[...], dense_ref[:, model:])
    norm_grad, gain_grad = norm_backward(middle_ref[...], gain_ref[...], second_grad)
    gain_grad_ref[...] = gain_grad
    middle_grad = dy_ref[...].astype(f32) + norm_grad
    middle_grad_ref[...] = middle_grad
    branch = middle_grad.astype(bf16)
    branch_ref[...] = branch
    grad = nt(branch, dense_ref[:, :model]).astype(bf16)
    groups = grad_ref.shape[0]
    width = model // groups
    for group in range(groups):
        grad_ref[group] = pack_rows(grad[:, group * width : (group + 1) * width])


def branch_back(back, target_column, logit, dense, middle, gain, dy, number, seqs, groups):
    tokens, model = middle.shape
    piece = tokens // seqs

    def rows_of(array):
        return pl.BlockSpec((piece, array.shape[1]), lambda _: (number, 0))

    out_shape = [
        shape((piece, model), f32),
        shape((piece, model), bf16),
        shape((groups, piece // 2, 2 * model // groups), bf16),
        shape((1, model), f32),
    ]
    return pl.pallas_call(
        branch_kernel,
        grid=(1,),
        in_specs=[
            whole(back), rows_of(target_column), rows_of(logit), whole(dense), rows_of(middle),
            whole(gain), rows_of(dy),
        ],
        out_specs=[whole(a) for a in out_shape],
        out_shape=out_shape,
        compiler_params=PARAMS,
        cost_estimate=cost(6 * piece * model * model, *out_shape, back, dense),
        name="branch_back",
    )(back, target_column, logit, dense, middle, gain, dy)


def dense_kernel(flat_ref, router_ref, *refs):
    out_ref = refs[-1]
    branch = jnp.concatenate([ref[...] for ref in refs[:-1]], axis=0)
    model = branch.shape[1]
    out_ref[:, :model] = tn(flat_ref[...], branch).astype(bf16)
    out_ref[:, model:] = router_ref[...]


def dense_grads(flat, branches, router):
    model, experts = router.shape
    out_shape = shape((model, model + experts), bf16)
    return pl.pallas_call(
        dense_kernel,
        in_specs=[whole(a) for a in (flat, router, *branches)],
        out_specs=whole(out_shape),
        out_shape=out_shape,
        compiler_params=PARAMS,
        cost_estimate=cost(2 * math.prod(flat.shape) * model, flat, router, *branches),
        name="dense_grads",
    )(flat, router, *branches)


def input_kernel(grad_ref, weight_ref, x_ref, gain_ref, middle_grad_ref, *refs):
    out_ref, gain_grad_ref = refs[-2:]
    total = None
    for group in range(weight_ref.shape[0]):
        part = nt(unpack_rows(grad_ref[group]), weight_ref[group])
        total = part if total is None else total + part
    norm_grad, gain_grad = norm_backward(x_ref[0].astype(f32), gain_ref[...], total)
    out_ref[0] = middle_grad_ref[...] + norm_grad
    gain_grad_ref[...] = gain_grad


def input_back(grad, weights, x, gain, middle_grad, number, earlier):
    seqs, piece, model = x.shape
    row_spec = pl.BlockSpec((1, piece, model), lambda _: (number, 0, 0))
    out_shape = [shape(x.shape, f32), shape((1, model), f32)]
    operands = [grad, weights, x, gain, middle_grad]
    specs = [whole(grad), whole(weights), row_spec, whole(gain), whole(middle_grad)]
    aliases = {}
    if earlier is not None:
        aliases = {len(operands): 0}
        operands.append(earlier)
        specs.append(pl.BlockSpec(memory_space=pl.ANY))
    return pl.pallas_call(
        input_kernel,
        grid=(1,),
        in_specs=specs,
        out_specs=[row_spec, whole(out_shape[1])],
        out_shape=out_shape,
        input_output_aliases=aliases,
        compiler_params=PARAMS,
        cost_estimate=cost(2 * piece * math.prod(weights.shape), grad, weights, middle_grad),
        name="input_back",
    )(*operands)


def column_kernel(seqs, place_ref, *refs):
    row_refs, grad_refs, out_refs = refs[:seqs], refs[seqs : 2 * seqs], refs[2 * seqs : -1]
    total = refs[-1]
    value = None
    for row_ref, grad_ref in zip(row_refs, grad_refs):
        grad = jnp.concatenate(
            [unpack_rows(grad_ref[piece]) for piece in range(grad_ref.shape[0])], axis=0
        )
        part = tn(row_ref[...], grad)
        value = part if value is None else value + part
    if len(out_refs) == 1:
        out_refs[0][...] = value.astype(bf16)
        return
    total[...] = value.astype(bf16)
    for number in range(2 * out_refs[0].shape[0]):
        ref = out_refs[number % 2]
        rows = ref.shape[1]
        at = pl.multiple_of(place_ref[number] * rows, rows)
        ref[number // 2] = total[pl.ds(at, rows), :]


def column_grads(places, rows, grads, chunks):
    model = rows[0].shape[1]
    cols = grads[0].shape[2] // 2
    if chunks > 1:
        out_shape = [shape((chunks // 2, model // chunks, cols), bf16)] * 2
    else:
        out_shape = [shape((model, cols), bf16)]
    return pl.pallas_call(
        functools.partial(column_kernel, len(rows)),
        in_specs=[SMEM] + [whole(a) for a in (*rows, *grads)],
        out_specs=[whole(a) for a in out_shape],
        out_shape=out_shape,
        scratch_shapes=[pltpu.VMEM((model, cols), bf16)],
        compiler_params=PARAMS,
        cost_estimate=cost(2 * sum(math.prod(r.shape) for r in rows) * cols, *rows, *grads),
        name="column_grads",
    )(places, *rows, *grads)


def column_order_kernel(place_ref, *refs):
    out_ref, held = refs[-2:]
    groups = held.shape[0]
    width = held.shape[2] // 3
    for number in range(groups):
        held[number] = refs[number][...].astype(f32)
    for part in range(3):
        joined = [
            held[place_ref[group], :, part * width : (part + 1) * width] for group in range(groups)
        ]
        out_ref[:, part * groups * width : (part + 1) * groups * width] = jnp.concatenate(
            joined, axis=1
        )


def column_order(places, pieces):
    rows, cols = pieces[0].shape
    out_shape = shape((rows, cols * len(pieces)), f32)
    return pl.pallas_call(
        column_order_kernel,
        in_specs=[SMEM] + [whole(a) for a in pieces],
        out_specs=whole(out_shape),
        out_shape=out_shape,
        scratch_shapes=[pltpu.VMEM((len(pieces), rows, cols), f32)],
        compiler_params=PARAMS,
        cost_estimate=cost(0, out_shape, *pieces),
        name="column_order",
    )(places, *pieces)


def expert_kernel(x_ref, win_ref, wout_ref, y_ref, slope_ref, acc):
    tile = pl.program_id(1)
    rows = acc.shape[0]
    x = x_ref[...].reshape(rows, x_ref.shape[-1])
    pre = jnp.dot(x, win_ref[0], preferred_element_type=f32)
    hidden, slope = gelu_and_slope(pre)
    slope_ref[0] = slope.astype(bf16)
    part = jnp.dot(hidden.astype(bf16), wout_ref[0], preferred_element_type=f32)

    @pl.when(tile == 0)
    def _():
        acc[...] = part

    @pl.when(tile > 0)
    def _():
        acc[...] += part

    @pl.when(tile == pl.num_programs(1) - 1)
    def _():
        y_ref[...] = acc[...].astype(bf16).reshape(y_ref.shape)


def expert_forward(x, w_in, w_out, tile):
    sources, experts, slots, model = x.shape
    hidden = w_in.shape[2]
    rows = sources * slots
    row_spec = pl.BlockSpec((sources, 1, slots, model), lambda e, f: (0, e, 0, 0))
    return pl.pallas_call(
        expert_kernel,
        grid=(experts, hidden // tile),
        in_specs=[
            row_spec,
            pl.BlockSpec((1, model, tile), lambda e, f: (e, 0, f)),
            pl.BlockSpec((1, tile, model), lambda e, f: (e, f, 0)),
        ],
        out_specs=[row_spec, pl.BlockSpec((1, rows, tile), lambda e, f: (e, 0, f))],
        out_shape=[
            jax.ShapeDtypeStruct(x.shape, bf16),
            jax.ShapeDtypeStruct((experts, rows, hidden), bf16),
        ],
        scratch_shapes=[pltpu.VMEM((rows, model), f32)],
        compiler_params=pltpu.CompilerParams(vmem_limit_bytes=52 * MIB),
        name="expert_forward",
    )(x, w_in, w_out)


def expert_back_kernel(g_ref, win_ref, wout_ref, slope_ref, y_ref, acc):
    tile = pl.program_id(1)
    rows = acc.shape[0]
    g = g_ref[...].reshape(rows, g_ref.shape[-1])
    pre_grad = (nt(g, wout_ref[0]) * slope_ref[0].astype(f32)).astype(bf16)
    part = nt(pre_grad, win_ref[0])

    @pl.when(tile == 0)
    def _():
        acc[...] = part

    @pl.when(tile > 0)
    def _():
        acc[...] += part

    @pl.when(tile == pl.num_programs(1) - 1)
    def _():
        y_ref[...] = acc[...].astype(bf16).reshape(y_ref.shape)


def expert_backward(g, w_in, w_out, slope, tile):
    sources, experts, slots, model = g.shape
    hidden = w_in.shape[2]
    rows = sources * slots
    row_spec = pl.BlockSpec((sources, 1, slots, model), lambda e, f: (0, e, 0, 0))
    return pl.pallas_call(
        expert_back_kernel,
        grid=(experts, hidden // tile),
        in_specs=[
            row_spec,
            pl.BlockSpec((1, model, tile), lambda e, f: (e, 0, f)),
            pl.BlockSpec((1, tile, model), lambda e, f: (e, f, 0)),
            pl.BlockSpec((1, rows, tile), lambda e, f: (e, 0, f)),
        ],
        out_specs=row_spec,
        out_shape=jax.ShapeDtypeStruct(g.shape, bf16),
        scratch_shapes=[pltpu.VMEM((rows, model), f32)],
        compiler_params=PARAMS,
        cost_estimate=cost(4 * experts * rows * model * hidden, g, w_in, w_out, slope),
        name="expert_backward",
    )(g, w_in, w_out, slope)


def weight_grad_kernel(pieces, place_ref, *refs):
    x_refs, g_refs = refs[:pieces], refs[pieces : 2 * pieces]
    win_ref, wout_ref = refs[2 * pieces : 2 * pieces + 2]
    earlier = refs[2 * pieces + 2 : -2]
    gin_ref, gout_ref = refs[-2:]
    gin, gout = (earlier[0][0], earlier[1][0]) if earlier else (None, None)
    for x_ref, g_ref in zip(x_refs, g_refs):
        rows = x_ref.shape[0] * x_ref.shape[2]
        x = x_ref[...].reshape(rows, x_ref.shape[-1])
        g = g_ref[...].reshape(rows, g_ref.shape[-1])
        hidden, slope = gelu_and_slope(nn(x, win_ref[0]))
        pre_grad = (nt(g, wout_ref[0]) * slope).astype(bf16)
        gin_part = tn(x, pre_grad)
        gout_part = tn(hidden.astype(bf16), g)
        gin = gin_part if gin is None else gin + gin_part
        gout = gout_part if gout is None else gout + gout_part
    gin_ref[0] = gin
    gout_ref[0] = gout


def weight_grads(place, xs, gs, w_in, w_out, ways, earlier):
    experts, model, hidden = w_in.shape
    cols = hidden // ways
    tile = GRAD_TILE if cols % GRAD_TILE == 0 else cols
    tiles = cols // tile

    def rows_of(array):
        sources, _, slots, _ = array.shape
        return pl.BlockSpec((sources, 1, slots, model), lambda e, t, q: (0, e, 0, 0))

    out_shape = [shape((experts, model, cols), f32), shape((experts, cols, model), f32)]
    out_specs = [
        pl.BlockSpec((1, model, tile), lambda e, t, q: (e, 0, t)),
        pl.BlockSpec((1, tile, model), lambda e, t, q: (e, t, 0)),
    ]
    flops = 16 * sum(math.prod(a.shape) for a in xs) * cols
    operands = [place, *xs, *gs, w_in, w_out]
    specs = [rows_of(a) for a in (*xs, *gs)] + [
        pl.BlockSpec((1, model, tile), lambda e, t, q: (e, 0, q[0] * tiles + t)),
        pl.BlockSpec((1, tile, model), lambda e, t, q: (e, q[0] * tiles + t, 0)),
    ]
    aliases = {}
    if earlier is not None:
        aliases = {len(operands): 0, len(operands) + 1: 1}
        operands += list(earlier)
        specs += out_specs
    return pl.pallas_call(
        functools.partial(weight_grad_kernel, len(xs)),
        grid_spec=pltpu.PrefetchScalarGridSpec(
            num_scalar_prefetch=1,
            grid=(experts, tiles),
            in_specs=specs,
            out_specs=out_specs,
        ),
        out_shape=out_shape,
        input_output_aliases=aliases,
        compiler_params=PARAMS,
        cost_estimate=cost(flops, *out_shape, *xs, *gs),
        name="weight_grads",
    )(*operands)


def partners(ways, step):
    return [(index, index ^ step) for index in range(ways)]


def swap(value, axis, step):
    return lax.ppermute(value, axis, partners(lax.axis_size(axis), step))


def gather_near(value):
    return swap(value, "seq", 1), swap(value, "seq", 2)


def gather_far(near, far):
    half = near.shape[0] // 2
    return swap(near[:half], "seq", 2), swap(far[half:], "seq", 1)


def sum_exchange(value, axis):
    copies = jnp.broadcast_to(value[None], (lax.axis_size(axis),) + value.shape)
    return jnp.sum(lax.all_to_all(copies, axis, 0, 0, tiled=True), axis=0)


def add_low(a, b):
    return (a.astype(f32) + b.astype(f32)).astype(bf16)


def scatter_rows(value):
    ways = lax.axis_size("shard")
    rows, cols = value.shape
    parts = lax.all_to_all(value.reshape(ways, rows // ways, cols), "shard", 0, 0, tiled=True)
    return jnp.sum(parts.astype(f32), axis=0)


def body(
    block_input,
    gain_attn,
    gain_ffn,
    w_qkv,
    w_out,
    w_router,
    rel_bias,
    w_in,
    w_exp_out,
    expert_id,
    capacity_slot,
    buckets,
    output_grad,
):
    seqs, piece, model = block_input.shape
    seq_ways = lax.axis_size("seq")
    shard_ways = lax.axis_size("shard")
    bucket_count, heads_all = rel_bias.shape
    heads = heads_all // seq_ways
    width = model // seq_ways
    length = piece * seq_ways
    experts = w_router.shape[1]
    tokens = seqs * piece
    capacity = 2 * tokens // experts
    positions = experts * capacity
    slot_shape = (shard_ways, experts // shard_ways, capacity, model)
    weight_rows = w_qkv.shape[0]
    seq_index = lax.axis_index("seq").astype(jnp.int32)
    places = jnp.stack([seq_index ^ step for step in range(seq_ways)])
    gain_one_row = gain_attn.reshape(1, model)
    gain_two_row = gain_ffn.reshape(1, model)
    bucket_row = jnp.pad(
        buckets, (0, 2 * length - buckets.shape[0]), constant_values=-1
    ).reshape(1, 2 * length)
    target = jnp.where(capacity_slot < capacity, expert_id * capacity + capacity_slot, -1)
    target_row = target.reshape(1, tokens)
    target_column = target.reshape(tokens, 1)
    by_chunks = shard_ways <= 8 and weight_rows % 16 == 0
    shard_index = lax.axis_index("shard").astype(jnp.int32)
    order = jnp.stack([shard_index ^ step for step in range(shard_ways)])
    id_column = expert_id.reshape(tokens, 1)
    upstream = output_grad.reshape(tokens, model)

    own_columns = lax.dynamic_slice_in_dim(
        w_qkv.reshape(weight_rows, 3, model), seq_index * width, width, 2
    ).reshape(weight_rows, 3 * width)
    own_columns = jnp.pad(own_columns, ((0, 0), (0, max(0, model - 3 * width))))
    head_weight = lax.all_gather(own_columns, "shard", axis=0, tiled=True)
    inputs = block_input.astype(f32)
    normed = (inputs * inverse_norm(inputs) * gain_attn).astype(bf16)
    tiles = bias_tiles(
        lax.dynamic_slice_in_dim(rel_bias, seq_index * heads, heads, 1), bucket_row
    )

    first_near = gather_near(normed[0])
    held = lax.optimization_barrier((normed[1], first_near))
    first_near = held[1]
    second_near = gather_near(held[0])
    first_far = gather_far(*first_near)
    dense_rows, head_weight, first_far, second_near, tiles = lax.optimization_barrier(
        (jnp.concatenate([w_out, w_router], axis=1), head_weight, first_far, second_near, tiles)
    )
    second_far = gather_far(*second_near)
    dense = lax.all_gather(dense_rows, "shard", axis=0, tiled=True)
    sequence_pieces = (
        (normed[0], *first_near, *first_far),
        (normed[1], *second_near, *second_far),
    )
    kept, attended_tok = [], []
    for pieces in sequence_pieces:
        rows, qkv, attended, probs = attend(places, pieces, head_weight, tiles)
        kept.append((rows, qkv, probs))
        attended_tok.append(lax.all_to_all(attended, "seq", 0, 0, tiled=True))

    middle, second, sent = project(
        block_input.reshape(tokens, model), target_row, gain_two_row, dense, attended_tok, positions
    )
    attended_flat, router_probs, sent_grad = route(
        second, upstream, id_column, target_row, dense, attended_tok, positions
    )

    def exchange(rows):
        return lax.all_to_all(rows, "shard", 0, 0, tiled=True)

    held_weight = lax.optimization_barrier((head_weight[:, : 3 * width], kept[0][1]))[0]
    weight_groups = lax.all_gather(held_weight, "seq")
    arrived = exchange(sent.reshape(slot_shape))
    arrived, sent_grad, weight_groups = lax.optimization_barrier(
        (arrived, sent_grad, weight_groups)
    )
    arrived_near = gather_near(arrived)
    out_arrived = exchange(sent_grad.reshape(slot_shape))
    expert_out, slope = expert_forward(arrived, w_in, w_exp_out, FORWARD_TILE)
    expert_out, out_arrived, weight_groups, arrived_near = lax.optimization_barrier(
        (expert_out, out_arrived, weight_groups, arrived_near)
    )
    back_out = exchange(expert_out).reshape(positions, model)
    out_near = gather_near(out_arrived)

    def expert_grads(xs, gs, earlier):
        return weight_grads(places, xs, gs, w_in, w_exp_out, seq_ways, earlier)

    rows_grad = expert_backward(out_arrived, w_in, w_exp_out, slope, FORWARD_TILE)
    expert_part = expert_grads((arrived,), (out_arrived,), None)
    rows_grad, back_out, expert_part = lax.optimization_barrier((rows_grad, back_out, expert_part))
    back_grad = exchange(rows_grad).reshape(positions, model)
    block_output, logit_low, grad_router = returned(
        (back_out,), target_column, id_column, middle, upstream, router_probs, second
    )
    expert_part = expert_grads(arrived_near, out_near, expert_part)
    arrived_near, out_near = lax.optimization_barrier((arrived_near, out_near))
    out_far = gather_far(*out_near)
    arrived_far = gather_far(*arrived_near)
    back_grad, logit_low, expert_part = lax.optimization_barrier(
        (back_grad, logit_low, expert_part)
    )
    middle_grads, branches, grad_heads, gain_two = [], [], [], []
    for number in range(seqs):
        middle_grad, branch, attended_grad, gain_part = branch_back(
            back_grad, target_column, logit_low, dense, middle, gain_two_row, upstream,
            number, seqs, seq_ways,
        )
        middle_grads.append(middle_grad)
        branches.append(branch)
        gain_two.append(gain_part)
        grad_heads.append(lax.all_to_all(attended_grad, "seq", 0, 0, tiled=True))
    grad_dense = dense_grads(attended_flat, branches, grad_router)
    grad_heads[0], grad_dense, out_far, arrived_far = lax.optimization_barrier(
        (grad_heads[0], grad_dense, out_far, arrived_far)
    )
    grad_dense = lax.psum_scatter(grad_dense, "shard", scatter_dimension=0, tiled=True)

    qkv_grads, bias_parts, grad_tok = [], [], []
    for number in range(seqs):
        _, qkv, probs = kept[number]
        grad = grad_heads[number]
        qkv_grad, bias_part = attend_back(qkv, probs, grad, bucket_row, bucket_count)
        qkv_grads.append(qkv_grad)
        bias_parts.append(bias_part)
        grad_tok.append(lax.all_to_all(qkv_grad, "seq", 0, 0, tiled=True))
    input_grad, first_gain = input_back(
        grad_tok[0], weight_groups, block_input, gain_one_row, middle_grads[0], 0, None
    )
    gain_one = [first_gain]
    qkv_grads[-1], grad_dense = lax.optimization_barrier((qkv_grads[-1], grad_dense))
    rows_all = [each[0] for each in kept]
    if by_chunks:
        columns, other = column_grads(order, rows_all, qkv_grads, shard_ways)
        last = other
        columns = add_low(columns, swap(other, "shard", 1))
        out_far = lax.optimization_barrier((out_far, columns))[0]
        step = shard_ways // 2
        if step > 1:
            half = columns.shape[0] // 2
            columns = add_low(columns[:half], swap(columns[half:], "shard", step))
            step //= 2
    else:
        (last,) = column_grads(places - places, rows_all, qkv_grads, 1)
        columns = last
    expert_part = expert_grads(arrived_far, out_far, expert_part)
    grad_tok[-1], input_grad, columns, expert_part = lax.optimization_barrier(
        (grad_tok[-1], input_grad, columns, expert_part)
    )
    grad_in_part, grad_exp_part = expert_part
    for number in range(1, seqs):
        input_grad, gain_part = input_back(
            grad_tok[number], weight_groups, block_input, gain_one_row,
            middle_grads[number], number, input_grad,
        )
        gain_one.append(gain_part)
    grad_dense = lax.optimization_barrier((grad_dense, gain_one[-1]))[0]
    grad_dense = add_low(grad_dense, swap(grad_dense, "seq", 1))
    grad_dense = grad_dense.astype(f32) + swap(grad_dense, "seq", 2).astype(f32)
    bias_grad = lax.dynamic_update_slice_in_dim(
        jnp.zeros((bucket_count, heads_all), f32),
        functools.reduce(jnp.add, bias_parts)[:, :heads],
        seq_index * heads,
        1,
    )
    small = jnp.concatenate(
        [bias_grad.reshape(-1), sum(gain_two).reshape(-1), sum(gain_one).reshape(-1)]
    ).reshape(-1, LANES)
    if by_chunks:
        while step > 1:
            half = columns.shape[0] // 2
            columns = add_low(columns[:half], swap(columns[half:], "shard", step))
            step //= 2
        columns = columns[0]
    else:
        columns = scatter_rows(columns).astype(bf16)
    grad_qkv = column_order(
        places, [columns] + [swap(columns, "seq", step) for step in range(1, seq_ways)]
    )
    small = sum_exchange(sum_exchange(small, "seq"), "shard").reshape(-1)
    bias_size = bucket_count * heads_all
    return (
        block_output.reshape(block_input.shape),
        input_grad,
        small[bias_size + model :],
        small[bias_size : bias_size + model],
        grad_qkv,
        grad_dense[:, :model],
        grad_dense[:, model:],
        small[:bias_size].reshape(bucket_count, heads_all),
        grad_in_part,
        grad_exp_part,
    )


def solution(mesh):
    placed = (
        P("shard", "seq", None),
        P(),
        P(),
        P("shard", None),
        P("shard", None),
        P("shard", None),
        P(),
        P("shard", None, None),
        P("shard", None, None),
        P("shard", "seq"),
        P("shard", "seq"),
        P(),
        P("shard", "seq", None),
    )
    return jax.shard_map(
        body,
        mesh=mesh,
        in_specs=placed,
        out_specs=(
            P("shard", "seq", None),
            P("shard", "seq", None),
            P(),
            P(),
            P("shard", None),
            P("shard", None),
            P("shard", None),
            P(),
            P("shard", None, "seq"),
            P("shard", "seq", None),
        ),
        check_vma=False,
    )
```
